32 devices in a mesh: batch: 4 (over y, x), rows: 8 (over z, core).
Axes of the slice: x: 2, y: 2, z: 4, core: 2. Of those that a mesh axis runs over, the one named last changes fastest.
Arguments:
- features: bfloat16 [2, 4, 32, 96, 2048], P(None, 'batch', 'rows'), may hold values from -6 to 6
- task_grads: bfloat16 [3, 2, 4, 32, 96, 2048], P(None, None, 'batch', 'rows'), may hold values from -32 to 32
- row_counts: int32 [2, 4], replicated, may hold values from 8 to 32, as said below
- col_counts: int32 [2, 4], replicated, may hold values from 48 to 96, as said below
- weight_in: float32 [2048, 512], P(('batch', 'rows')), may hold values from -0.125 to 0.125
- weight_mid: float32 [4608, 512], P(('batch', 'rows')), may hold values from -0.09375 to 0.09375
- weight_out: float32 [512, 2048], P(None, ('batch', 'rows')), may hold values from -0.25 to 0.25
- first_in: float32 [2048, 512], P(('batch', 'rows')), may hold values from -0.0007324219 to 0.0007324219
- first_mid: float32 [4608, 512], P(('batch', 'rows')), may hold values from -0.0007324219 to 0.0007324219
- first_out: float32 [512, 2048], P(None, ('batch', 'rows')), may hold values from -0.0007324219 to 0.0007324219
- second_in: float32 [2048, 512], P(('batch', 'rows')), may hold values from 2.2408501e-10 to 8.9634006e-10
- second_mid: float32 [4608, 512], P(('batch', 'rows')), may hold values from 2.2408501e-10 to 8.9634006e-10
- second_out: float32 [512, 2048], P(None, ('batch', 'rows')), may hold values from 2.2408501e-10 to 8.9634006e-10
- norm_params: float32 [2, 3072], replicated, may hold values from -1.2 to 1.95, as said below
- norm_first: float32 [2, 3072], replicated, may hold values from -0.0007324219 to 0.0007324219
- norm_second: float32 [2, 3072], replicated, may hold values from 2.2408501e-10 to 8.9634006e-10
Outputs:
- block_out: bfloat16 [2, 4, 32, 96, 2048], P(None, 'batch', 'rows')
- input_grad: bfloat16 [2, 4, 32, 96, 2048], P(None, 'batch', 'rows')
- new_weight_in: float32 [2048, 512], P(('batch', 'rows'))
- new_weight_mid: float32 [4608, 512], P(('batch', 'rows'))
- new_weight_out: float32 [512, 2048], P(None, ('batch', 'rows'))
- new_first_in: float32 [2048, 512], P(('batch', 'rows'))
- new_first_mid: float32 [4608, 512], P(('batch', 'rows'))
- new_first_out: float32 [512, 2048], P(None, ('batch', 'rows'))
- new_second_in: float32 [2048, 512], P(('batch', 'rows'))
- new_second_mid: float32 [4608, 512], P(('batch', 'rows'))
- new_second_out: float32 [512, 2048], P(None, ('batch', 'rows'))
- new_norm: float32 [2, 3072], replicated
- new_norm_first: float32 [2, 3072], replicated
- new_norm_second: float32 [2, 3072], replicated
- grad_norm: float32 [1], replicated
The draws below stay inside these ranges and needn't reach their ends.
Inputs may be any that keep to these rules, and one draw needn't show every extreme that they name: `row_counts`: in each micro-batch some crop has all 32 rows valid. `col_counts`: in each micro-batch some crop has all 96 columns valid. `norm_params`: row 0 holds positive gains.
All inputs are finite; a program needn't handle non-finite values.
Results may differ from the reference program's by a relative error of at most 0.0085.
Values may be sent and summed in bfloat16 or wider, within the bound.
No kernel may reach another device: no remote copies, remote signals or barrier semaphores. Data moves between devices by JAX's collectives and lax.ppermute only.
A program may use at most 192 MiB of HBM per device.

```python
import math
import jax
import jax.numpy as jnp
from jax import lax

C = 2048
INNER_CHANNELS = 512
W = 96
MICRO = 2
DILATION_SIZE = 4
NEWTON = 6
STEP = 10
H = 32
CROPS = 4
NPARAM = 4462592


def task_ramp(top_value):
    place = (jnp.arange(CROPS, dtype=jnp.float32)[:, None] * H + jnp.arange(H, dtype=jnp.float32)[None, :]) / (CROPS * H - 1)
    rising = 1.0 + (top_value - 1.0) * place
    falling = top_value + 1.0 - rising
    flat_part = jnp.ones_like(rising)
    ramps = jnp.stack([rising, 1.4 * falling, 0.8 * flat_part])
    return ramps.reshape(3, 1, CROPS, H, 1, 1)


def draw_task_grads(key, part):
    key = jax.random.fold_in(key, 11)
    common_key, own_key = jax.random.split(key)
    shape = (MICRO, CROPS, H, W, C)
    common = jnp.clip(jax.random.normal(common_key, shape, jnp.float32), -5.0, 5.0)
    own = jnp.clip(jax.random.normal(own_key, (3,) + shape, jnp.float32), -5.0, 5.0)
    share = 0.5
    scales = task_ramp(3.0)
    return (scales * (own + share * common[None])).astype(jnp.bfloat16)


def draw_row_counts(key, part):
    key = jax.random.fold_in(key, 21)
    count_key, pick_key = jax.random.split(key)
    counts = jax.random.randint(count_key, (MICRO, CROPS), H // 4, H + 1)
    pick = jax.random.randint(pick_key, (MICRO, 1), 0, CROPS)
    return jnp.where(jnp.arange(CROPS)[None, :] == pick, H, counts).astype(jnp.int32)


def draw_col_counts(key, part):
    key = jax.random.fold_in(key, 22)
    count_key, pick_key = jax.random.split(key)
    counts = jax.random.randint(count_key, (MICRO, CROPS), W // 2, W + 1)
    pick = jax.random.randint(pick_key, (MICRO, 1), 0, CROPS)
    return jnp.where(jnp.arange(CROPS)[None, :] == pick, W, counts).astype(jnp.int32)


def draw_norm_params(key, part):
    key = jax.random.fold_in(key, 31)
    gain_key, shift_key = jax.random.split(key)
    frac = jnp.concatenate([jnp.arange(INNER_CHANNELS) / INNER_CHANNELS, jnp.arange(INNER_CHANNELS) / INNER_CHANNELS, jnp.arange(C) / C]).astype(jnp.float32)
    gains = jax.random.uniform(gain_key, (2 * INNER_CHANNELS + C,), jnp.float32, 0.7, 1.3) * (0.5 + frac)
    shifts = 0.3 * jnp.clip(jax.random.normal(shift_key, (2 * INNER_CHANNELS + C,), jnp.float32), -4.0, 4.0)
    return jnp.stack([gains, shifts])


def block_scale(stream_key, dims, shards, smallest, largest):
    factor_of = 1.0
    for position, blocks in shards:
        steps = jax.random.uniform(jax.random.fold_in(jax.random.fold_in(stream_key, 6), position), (blocks,), jnp.float32, smallest / len(shards), largest / len(shards))
        factor_of = factor_of * jnp.repeat(jnp.exp(steps), dims[position] // blocks).reshape((-1,) + (1,) * (len(dims) - 1 - position))
    return factor_of


def bell_draw(key, dims, deviation, limit, cuts=(), held_as=jnp.bfloat16):
    drawn = deviation * jax.random.normal(key, dims, jnp.float32)
    if cuts:
        drawn = drawn * block_scale(key, dims, cuts, -0.22, 0.18)
    return jnp.clip(drawn, -limit, limit).astype(held_as)


def setup_inputs(seed: int = 0) -> dict:
    splits = jax.random.split(jax.random.key(seed), 17)
    features = bell_draw(splits[0], (MICRO, CROPS, H, W, C), 1.0, 6.0, ((1, 4), (2, 8)))
    task_grads = draw_task_grads(jax.random.fold_in(splits[16], 71), 0)
    row_counts = draw_row_counts(jax.random.fold_in(splits[16], 71), 0)
    col_counts = draw_col_counts(jax.random.fold_in(splits[16], 71), 0)
    weight_in = bell_draw(splits[4], (C, INNER_CHANNELS), C ** -0.5, 0.125, ((0, 32),), jnp.float32)
    weight_mid = bell_draw(splits[5], (9 * INNER_CHANNELS, INNER_CHANNELS), (9 * INNER_CHANNELS) ** -0.5, 0.09375, ((0, 32),), jnp.float32)
    weight_out = bell_draw(splits[6], (INNER_CHANNELS, C), INNER_CHANNELS ** -0.5, 0.25, ((1, 32),), jnp.float32)
    first_in = bell_draw(splits[7], (C, INNER_CHANNELS), (0.11 / NPARAM ** 0.5), 0.0007324219, ((0, 32),), jnp.float32)
    first_mid = bell_draw(splits[8], (9 * INNER_CHANNELS, INNER_CHANNELS), (0.11 / NPARAM ** 0.5), 0.0007324219, ((0, 32),), jnp.float32)
    first_out = bell_draw(splits[9], (INNER_CHANNELS, C), (0.11 / NPARAM ** 0.5), 0.0007324219, ((1, 32),), jnp.float32)
    second_in = jnp.clip(jnp.exp(math.log(8.963400577322034e-10) - 1.3862944 * jax.random.uniform(splits[10], (C, INNER_CHANNELS), jnp.float32) ** block_scale(splits[10], (C, INNER_CHANNELS), ((0, 32),), -0.2, 0.2)), 2.2408501443305084e-10, 8.963400577322034e-10)
    second_mid = jnp.clip(jnp.exp(math.log(8.963400577322034e-10) - 1.3862944 * jax.random.uniform(splits[11], (9 * INNER_CHANNELS, INNER_CHANNELS), jnp.float32) ** block_scale(splits[11], (9 * INNER_CHANNELS, INNER_CHANNELS), ((0, 32),), -0.2, 0.2)), 2.2408501443305084e-10, 8.963400577322034e-10)
    second_out = jnp.clip(jnp.exp(math.log(8.963400577322034e-10) - 1.3862944 * jax.random.uniform(splits[12], (INNER_CHANNELS, C), jnp.float32) ** block_scale(splits[12], (INNER_CHANNELS, C), ((1, 32),), -0.2, 0.2)), 2.2408501443305084e-10, 8.963400577322034e-10)
    norm_params = draw_norm_params(jax.random.fold_in(splits[16], 71), 0)
    norm_first = bell_draw(splits[14], (2, 2 * INNER_CHANNELS + C), (0.11 / NPARAM ** 0.5), 0.0007324219, (), jnp.float32)
    norm_second = jnp.clip(jnp.exp(jax.random.uniform(splits[15], (2, 2 * INNER_CHANNELS + C), jnp.float32, math.log(2.2408501443305084e-10), math.log(8.963400577322034e-10))), 2.2408501443305084e-10, 8.963400577322034e-10)
    return {"features": features, "task_grads": task_grads, "row_counts": row_counts, "col_counts": col_counts, "weight_in": weight_in, "weight_mid": weight_mid, "weight_out": weight_out, "first_in": first_in, "first_mid": first_mid, "first_out": first_out, "second_in": second_in, "second_mid": second_mid, "second_out": second_out, "norm_params": norm_params, "norm_first": norm_first, "norm_second": norm_second}


@jax.custom_vjp
def low(v):
    return lax.optimization_barrier(v.astype(jnp.bfloat16)).astype(jnp.float32)

@jax.custom_vjp
def low_back(v):
    return v

def low_keep(v):
    return (low(v), None)

def low_pass(kept, grad):
    return (grad,)

def back_keep(v):
    return (v, None)

def back_low(kept, grad):
    return (low(grad),)
low.defvjp(low_keep, low_pass)
low_back.defvjp(back_keep, back_low)
EPS_NORM = 1e-05
CLIP = 1.0
RATE = 0.02
RATE_NORM = 0.3
BETA_ONE = 0.9
BETA_TWO = 0.999
ADAM_EPS = 1e-08
DECAY = 0.01

def product(left_offset, right):
    return jnp.dot(left_offset, right, precision=lax.Precision.HIGHEST, preferred_element_type=jnp.float32)

def align_coeffs(gram):
    trace = gram[0, 0] + gram[1, 1] + gram[2, 2]
    ymat = gram / trace
    ident = jnp.eye(3, dtype=jnp.float32)
    zmat = ident
    for sweep in range(NEWTON):
        pmat = 1.5 * ident - 0.5 * product(zmat, ymat)
        ymat = product(ymat, pmat)
        zmat = product(pmat, zmat)
    return lax.optimization_barrier(jnp.sum(zmat, axis=1)) / jnp.sqrt(jnp.float32(3.0))

def norm_layer(value, flat_mask, count, gain, shift):
    total = lax.optimization_barrier(jnp.sum(flat_mask * value, axis=0))
    squares = lax.optimization_barrier(jnp.sum(flat_mask * value * value, axis=0))
    mean = total / count
    rstd = lax.rsqrt(squares / count - mean * mean + EPS_NORM)
    return (value - mean) * rstd * gain + shift

def shifted_taps(padded_input, image_height, image_width):
    pieces = []
    for vertical_step in (-1, 0, 1):
        for horizontal_step in (-1, 0, 1):
            top_offset = DILATION_SIZE + vertical_step * DILATION_SIZE
            left_offset = DILATION_SIZE + horizontal_step * DILATION_SIZE
            pieces.append(padded_input[:, top_offset:top_offset + image_height, left_offset:left_offset + image_width])
    return jnp.stack(pieces, axis=3)

def block(xf, w_in, w_mid, w_out, params, mask):
    crop_windows, image_height, image_width, chan = xf.shape
    pixels = crop_windows * image_height * image_width
    flat_mask = mask.reshape(pixels, 1)
    count = jnp.sum(mask)
    flat_x = xf.reshape(pixels, chan)
    z_one = norm_layer(low_back(product(flat_x, low(w_in))), flat_mask, count, params[0, :INNER_CHANNELS], params[1, :INNER_CHANNELS])
    hidden_first = low(flat_mask * jax.nn.softplus(z_one))
    padded_input = jnp.pad(hidden_first.reshape(crop_windows, image_height, image_width, INNER_CHANNELS), ((0, 0), (DILATION_SIZE, DILATION_SIZE), (DILATION_SIZE, DILATION_SIZE), (0, 0)))
    gathered = shifted_taps(padded_input, image_height, image_width).reshape(pixels, 9 * INNER_CHANNELS)
    z_two = norm_layer(low_back(product(gathered, low(w_mid))), flat_mask, count, params[0, INNER_CHANNELS:2 * INNER_CHANNELS], params[1, INNER_CHANNELS:2 * INNER_CHANNELS])
    h_two = low(flat_mask * jax.nn.softplus(z_two))
    z_three = norm_layer(low_back(product(h_two, low(w_out))), flat_mask, count, params[0, 2 * INNER_CHANNELS:], params[1, 2 * INNER_CHANNELS:])
    return flat_mask * jax.nn.softplus(z_three + flat_x)

def adamw(weight, first, second, grad, rate, decay):
    new_first = BETA_ONE * first + (1.0 - BETA_ONE) * grad
    new_second = BETA_TWO * second + (1.0 - BETA_TWO) * grad * grad
    first_hat = new_first / (1.0 - BETA_ONE ** STEP)
    second_hat = new_second / (1.0 - BETA_TWO ** STEP)
    new_weight = weight - rate * (first_hat / (jnp.sqrt(second_hat) + ADAM_EPS) + decay * weight)
    return (new_weight, new_first, new_second)

def reference(features, task_grads, row_counts, col_counts, weight_in, weight_mid, weight_out, first_in, first_mid, first_out, second_in, second_mid, second_out, norm_params, norm_first, norm_second):
    row_ids = jnp.arange(H, dtype=jnp.int32)
    col_ids = jnp.arange(W, dtype=jnp.int32)
    masks = ((row_ids[None, None, :, None] < row_counts[:, :, None, None]) & (col_ids[None, None, None, :] < col_counts[:, :, None, None])).astype(jnp.float32)
    gram = jnp.zeros((3, 3), jnp.float32)
    for micro in range(MICRO):
        flat = (task_grads[:, micro].astype(jnp.float32) * masks[micro][None, :, :, :, None]).reshape(3, -1)
        gram = gram + lax.dot_general(flat, flat, (((1,), (1,)), ((), ())), precision=lax.Precision.HIGHEST, preferred_element_type=jnp.float32)
    coeffs = align_coeffs(gram)
    grad_in = jnp.zeros_like(weight_in)
    grad_mid = jnp.zeros_like(weight_mid)
    grad_out = jnp.zeros_like(weight_out)
    grad_norm_params = jnp.zeros_like(norm_params)
    outputs = []
    input_grads = []
    for micro in range(MICRO):
        xf = features[micro].astype(jnp.float32)
        mask = masks[micro]
        value, pullback = jax.vjp(lambda xv, wa, wb, wc, pv: block(xv, wa, wb, wc, pv, mask), xf, weight_in, weight_mid, weight_out, norm_params)
        upstream = coeffs[0] * task_grads[0, micro].astype(jnp.float32)
        upstream = upstream + coeffs[1] * task_grads[1, micro].astype(jnp.float32)
        upstream = upstream + coeffs[2] * task_grads[2, micro].astype(jnp.float32)
        dx, g_in, g_mid, g_out, g_par = pullback(upstream.reshape(-1, C))
        outputs.append(value.reshape(xf.shape).astype(jnp.bfloat16))
        input_grads.append(dx.reshape(xf.shape).astype(jnp.bfloat16))
        grad_in = grad_in + g_in
        grad_mid = grad_mid + g_mid
        grad_out = grad_out + g_out
        grad_norm_params = grad_norm_params + g_par
    total = jnp.sum(grad_in * grad_in) + jnp.sum(grad_mid * grad_mid) + jnp.sum(grad_out * grad_out) + jnp.sum(grad_norm_params * grad_norm_params)
    grad_norm = jnp.sqrt(total)
    scale = CLIP / jnp.maximum(grad_norm, CLIP)
    new_in, new_first_in, new_second_in = adamw(weight_in, first_in, second_in, grad_in * scale, RATE, DECAY)
    new_mid, new_first_mid, new_second_mid = adamw(weight_mid, first_mid, second_mid, grad_mid * scale, RATE, DECAY)
    new_out, new_first_out, new_second_out = adamw(weight_out, first_out, second_out, grad_out * scale, RATE, DECAY)
    new_norm, new_norm_first, new_norm_second = adamw(norm_params, norm_first, norm_second, grad_norm_params * scale, RATE_NORM, 0.0)
    return (jnp.stack(outputs), jnp.stack(input_grads), new_in, new_mid, new_out, new_first_in, new_first_mid, new_first_out, new_second_in, new_second_mid, new_second_out, new_norm, new_norm_first, new_norm_second, grad_norm.reshape(1))
```

```python
import jax
import jax.numpy as jnp
from jax import lax
from jax.sharding import PartitionSpec as P

DILATION_SIZE = 4
NEWTON = 6
STEP = 10

EPS_NORM = 1e-05
CLIP = 1.0
RATE = 0.02
RATE_NORM = 0.3
BETA_ONE = 0.9
BETA_TWO = 0.999
ADAM_EPS = 1e-08
DECAY = 0.01

F32 = jnp.float32
BF16 = jnp.bfloat16


def swap(x, axis, mask):
    return lax.ppermute(x, axis, [(i, i ^ mask) for i in range(lax.axis_size(axis))])


def row_groups():
    groups = []
    bit, rest = 1, lax.axis_size("rows") // 2
    while rest > 1:
        size = min(4, rest)
        groups.append((bit, size))
        bit += size.bit_length() - 1
        rest //= size
    return groups


def group_sum(x, axis, shift, size):
    got = [x] + [swap(x, axis, m << shift) for m in range(1, size)]
    if size == 2:
        return got[0] + got[1]
    return (got[0] + got[1]) + (got[2] + got[3])


def all_sum(x):
    x = group_sum(x, "rows", 0, 2)
    x = group_sum(x, "batch", 0, lax.axis_size("batch"))
    for bit, size in row_groups():
        x = group_sum(x, "rows", bit, size)
    return x


def put(buf, piece, index, axis):
    return lax.dynamic_update_slice_in_dim(buf, jnp.expand_dims(piece, axis), index, axis)


def take(buf, index, axis):
    return lax.dynamic_index_in_dim(buf, index, axis, keepdims=False)


def gather_shards(shard):
    mine = lax.axis_index("rows")
    core = mine & 1
    batch = lax.axis_index("batch")
    block = shard[None]
    for bit, size in row_groups():
        place = (mine >> bit) & (size - 1)
        got = [block] + [swap(block, "rows", m << bit) for m in range(1, size)]
        buf = jnp.zeros((size,) + block.shape, block.dtype)
        for m, piece in enumerate(got):
            buf = put(buf, piece, place ^ m, 0)
        block = buf.reshape((-1,) + block.shape[1:])
    half = block.shape[0] // 2
    from_x = swap(block, "batch", 1)
    from_y = swap(block, "batch", 2)
    far_low = swap(from_x[:half], "batch", 2)
    far_high = swap(from_y[half:], "batch", 1)
    far = jnp.concatenate([far_low, far_high], axis=0)
    full = jnp.zeros((4, block.shape[0], 2) + block.shape[1:], block.dtype)
    for m, piece in enumerate((block, from_x, from_y, far)):
        other = swap(piece, "rows", 1)
        for value, where in ((piece, core), (other, 1 - core)):
            full = lax.dynamic_update_slice(
                full, value[None, :, None], (batch ^ m, 0, where, 0, 0)
            )
    return full


def scatter_sums(grad):
    mine = lax.axis_index("rows")
    core = mine & 1
    batch = lax.axis_index("batch")
    count = lax.axis_size("rows")
    grad = grad.reshape(4, count // 2, 2, -1, grad.shape[-1])
    got = swap(take(grad, 1 - core, 2).astype(BF16), "rows", 1)
    part = take(grad, core, 2) + got.astype(F32)
    half = part.shape[1] // 2
    own, to_x, to_y, far = [take(part, batch ^ m, 0) for m in range(4)]
    low = swap(far[:half].astype(BF16), "batch", 1).astype(F32)
    high = swap(far[half:].astype(BF16), "batch", 2).astype(F32)
    to_x = jnp.concatenate([to_x[:half], to_x[half:] + high], axis=0)
    to_y = jnp.concatenate([to_y[:half] + low, to_y[half:]], axis=0)
    from_x = swap(to_x.astype(BF16), "batch", 1)
    from_y = swap(to_y.astype(BF16), "batch", 2)
    own = own + from_x.astype(F32) + from_y.astype(F32)
    for bit, size in reversed(row_groups()):
        place = (mine >> bit) & (size - 1)
        own = own.reshape((size, -1) + own.shape[1:])
        total = take(own, place, 0)
        for m in range(1, size):
            total = total + swap(take(own, place ^ m, 0).astype(BF16), "rows", m << bit).astype(F32)
        own = total
    return own.reshape(own.shape[-2:])


def dot3(left, right):
    return jnp.sum(left[:, :, None] * right[None, :, :], axis=1)


def align_coeffs(gram):
    trace = gram[0, 0] + gram[1, 1] + gram[2, 2]
    ymat = gram / trace
    ident = jnp.eye(3, dtype=F32)
    zmat = ident
    for _ in range(NEWTON):
        pmat = 1.5 * ident - 0.5 * dot3(zmat, ymat)
        ymat = dot3(ymat, pmat)
        zmat = dot3(pmat, zmat)
    return jnp.sum(zmat, axis=1) / jnp.sqrt(F32(3.0))


def dot(left, right, dims):
    return lax.dot_general(left, right, ((dims[:1], dims[1:]), ((), ())), preferred_element_type=F32)


def neighbours(x):
    count = lax.axis_size("rows")
    up = lax.ppermute(x, "rows", [(i, i + 1) for i in range(count - 1)])
    down = lax.ppermute(x, "rows", [(i + 1, i) for i in range(count - 1)])
    return up, down


def shift_cols(x, step, columns):
    shaped = x.reshape(-1, columns, x.shape[-1])
    zero = jnp.zeros((shaped.shape[0], abs(step), shaped.shape[2]), x.dtype)
    if step > 0:
        moved = jnp.concatenate([zero, shaped[:, :-step]], axis=1)
    else:
        moved = jnp.concatenate([shaped[:, -step:], zero], axis=1)
    return moved.reshape(x.shape)


def adamw(weight, first, second, grad, rate, decay):
    new_first = BETA_ONE * first + (1.0 - BETA_ONE) * grad
    new_second = BETA_TWO * second + (1.0 - BETA_TWO) * grad * grad
    first_hat = new_first / (1.0 - BETA_ONE**STEP)
    second_hat = new_second / (1.0 - BETA_TWO**STEP)
    new_weight = weight - rate * (first_hat / (jnp.sqrt(second_hat) + ADAM_EPS) + decay * weight)
    return (new_weight, new_first, new_second)


def per_device(
    features, task_grads, row_counts, col_counts,
    weight_in, weight_mid, weight_out,
    first_in, first_mid, first_out,
    second_in, second_mid, second_out,
    norm_params, norm_first, norm_second,
):
    micros, _, row_span, columns, chan = features.shape
    inner = weight_in.shape[1]
    pixels = row_span * columns
    batch = lax.axis_index("batch")
    own_rows = lax.dynamic_index_in_dim(row_counts, batch, 1, keepdims=False)
    own_cols = lax.dynamic_index_in_dim(col_counts, batch, 1, keepdims=False)
    row_ids = lax.axis_index("rows") * row_span + jnp.arange(row_span, dtype=jnp.int32)
    col_ids = jnp.arange(columns, dtype=jnp.int32)
    mask = (
        (row_ids[None, :, None] < own_rows[:, None, None])
        & (col_ids[None, None, :] < own_cols[:, None, None])
    ).astype(F32).reshape(micros, pixels, 1)
    inverse = 1.0 / jnp.sum(row_counts * col_counts, axis=1).astype(F32).reshape(micros, 1, 1)

    def spread(v):
        return v.reshape(micros, pixels, v.shape[-1])

    def flat(v):
        return v.reshape(micros * pixels, v.shape[-1])

    def sums(first, second):
        return jnp.stack([jnp.sum(first, axis=1), jnp.sum(second, axis=1)])

    w_in = gather_shards(weight_in.astype(BF16)).reshape(-1, inner)
    w_mid = gather_shards(weight_mid.astype(BF16)).reshape(3, 3, inner, inner)
    w_out = gather_shards(weight_out.T.astype(BF16)).reshape(-1, inner)

    tasks = [spread(task_grads[i, :, 0]).astype(F32) for i in range(3)]
    masked_tasks = [t * mask for t in tasks]
    gram = jnp.stack(
        [jnp.sum(masked_tasks[i] * masked_tasks[j]) for i in range(3) for j in range(i, 3)]
    )

    gains = [norm_params[0, :inner], norm_params[0, inner : 2 * inner], norm_params[0, 2 * inner :]]
    shifts = [norm_params[1, :inner], norm_params[1, inner : 2 * inner], norm_params[1, 2 * inner :]]

    def stats(total):
        mean = total[0][:, None] * inverse
        rstd = lax.rsqrt(total[1][:, None] * inverse - mean * mean + EPS_NORM)
        return mean, rstd

    x_flat = features.reshape(micros * pixels, chan)
    a_one = spread(dot(x_flat, w_in, (1, 0)))
    part = sums(mask * a_one, mask * a_one * a_one)
    packed = jnp.concatenate([part.reshape(-1), gram, jnp.zeros(122, F32)]).reshape(-1, 128)
    packed = all_sum(packed).reshape(-1)
    mean_one, rstd_one = stats(packed[: part.size].reshape(part.shape))
    g6 = packed[part.size : part.size + 6]
    coeffs = align_coeffs(g6[jnp.array([0, 1, 2, 1, 3, 4, 2, 4, 5])].reshape(3, 3))
    n_one = (a_one - mean_one) * rstd_one
    z_one = n_one * gains[0] + shifts[0]
    h_one = flat((mask * jax.nn.softplus(z_one)).astype(BF16))
    h_up, h_down = neighbours(h_one)
    h_blocks = (h_up, h_one, h_down)

    def conv(blocks, sign, dims):
        total = 0.0
        for tx in (-1, 0, 1):
            part = sum(dot(blocks[1 + sign * ty], w_mid[ty + 1, tx + 1], dims) for ty in (-1, 0, 1))
            if tx:
                part = shift_cols(part, -sign * tx * DILATION_SIZE, columns)
            total = total + part
        return total

    a_two = spread(conv(h_blocks, 1, (1, 0)))
    mean_two, rstd_two = stats(all_sum(sums(mask * a_two, mask * a_two * a_two)))
    n_two = (a_two - mean_two) * rstd_two
    z_two = n_two * gains[1] + shifts[1]
    h_two = flat((mask * jax.nn.softplus(z_two)).astype(BF16))
    a_three = spread(dot(h_two, w_out, (1, 1)))
    mean_three, rstd_three = stats(all_sum(sums(mask * a_three, mask * a_three * a_three)))
    n_three = (a_three - mean_three) * rstd_three
    resid = n_three * gains[2] + shifts[2] + spread(x_flat).astype(F32)
    block_out = (mask * jax.nn.softplus(resid)).astype(BF16)
    upstream = coeffs[0] * tasks[0] + coeffs[1] * tasks[1] + coeffs[2] * tasks[2]
    d_resid = upstream * mask * jax.nn.sigmoid(resid)

    def back(upper, normed, rstd, gain):
        total = all_sum(sums(upper, upper * normed))
        shift_grad, gain_grad = total[0][:, None], total[1][:, None]
        lower = mask * (gain * rstd) * (upper - (shift_grad + normed * gain_grad) * inverse)
        return flat(lower.astype(BF16)), jnp.sum(total, axis=1)

    d_three, norm_grad_three = back(d_resid, n_three, rstd_three, gains[2])
    d_h_two = spread(dot(d_three, w_out, (1, 0)))
    grad_out = scatter_sums(dot(d_three, h_two, (0, 0)))
    d_two, norm_grad_two = back(
        d_h_two * mask * jax.nn.sigmoid(z_two), n_two, rstd_two, gains[1]
    )
    d_up, d_down = neighbours(d_two)
    d_h_one = spread(conv((d_up, d_two, d_down), -1, (1, 1)))
    grads_mid = []
    for ty in (-1, 0, 1):
        for tx in (-1, 0, 1):
            right = shift_cols(d_two, tx * DILATION_SIZE, columns) if tx else d_two
            grads_mid.append(dot(h_blocks[1 + ty], right, (0, 0)))
    grad_mid = scatter_sums(jnp.concatenate(grads_mid, axis=0))
    d_one, norm_grad_one = back(
        d_h_one * mask * jax.nn.sigmoid(z_one), n_one, rstd_one, gains[0]
    )
    grad_in = scatter_sums(dot(x_flat, d_one, (0, 0)))
    input_grad = (spread(dot(d_one, w_in, (1, 1))) + d_resid).astype(BF16)

    norm_total = jnp.concatenate([norm_grad_one, norm_grad_two, norm_grad_three], axis=1)[::-1]
    local_squares = (
        jnp.sum(grad_in * grad_in) + jnp.sum(grad_mid * grad_mid) + jnp.sum(grad_out * grad_out)
    )
    total = all_sum(local_squares.reshape(1, 1)) + jnp.sum(norm_total * norm_total)
    grad_norm = jnp.sqrt(total)
    scale = CLIP / jnp.maximum(grad_norm, CLIP)
    new_in = adamw(weight_in, first_in, second_in, grad_in * scale, RATE, DECAY)
    new_mid = adamw(weight_mid, first_mid, second_mid, grad_mid * scale, RATE, DECAY)
    new_out = adamw(weight_out, first_out, second_out, (grad_out * scale).T, RATE, DECAY)
    new_norm = adamw(norm_params, norm_first, norm_second, norm_total * scale, RATE_NORM, 0.0)
    shape = (micros, 1, row_span, columns, chan)
    return (
        block_out.reshape(shape),
        input_grad.reshape(shape),
        *[group[k] for k in range(3) for group in (new_in, new_mid, new_out)],
        *new_norm,
        grad_norm.reshape(1),
    )


def solution(mesh):
    acts = P(None, "batch", "rows", None, None)
    by_row, by_col = P(("batch", "rows"), None), P(None, ("batch", "rows"))
    weights = (by_row, by_row, by_col)
    return jax.shard_map(
        per_device,
        mesh=mesh,
        in_specs=(
            acts, P(None, None, "batch", "rows", None, None), P(), P(), *(weights * 3), P(), P(), P()
        ),
        out_specs=(acts, acts, *(weights * 3), P(), P(), P(), P()),
        check_vma=False,
    )
```

```python
import functools

import jax
import jax.numpy as jnp
from jax import lax
from jax.experimental import pallas as pl
from jax.experimental.pallas import tpu as pltpu
from jax.sharding import PartitionSpec as P

DILATION_SIZE = 4
NEWTON = 6
STEP = 10

EPS_NORM = 1e-05
CLIP = 1.0
RATE = 0.02
RATE_NORM = 0.3
BETA_ONE = 0.9
BETA_TWO = 0.999
ADAM_EPS = 1e-08
DECAY = 0.01

F32 = jnp.float32
BF16 = jnp.bfloat16


def swap(x, axis, mask):
    return lax.ppermute(x, axis, [(i, i ^ mask) for i in range(lax.axis_size(axis))])


def row_groups():
    groups = []
    bit, rest = 1, lax.axis_size("rows") // 2
    while rest > 1:
        size = min(4, rest)
        groups.append((bit, size))
        bit += size.bit_length() - 1
        rest //= size
    return groups


def group_sum(x, axis, shift, size):
    got = [x] + [swap(x, axis, m << shift) for m in range(1, size)]
    if size == 2:
        return got[0] + got[1]
    return (got[0] + got[1]) + (got[2] + got[3])


def chip_sums(x):
    return group_sum(group_sum(x, "rows", 0, 2), "batch", 0, lax.axis_size("batch"))


def all_sum(x):
    return line_sums(chip_sums(x))


def line_sums(x):
    for bit, size in row_groups():
        x = group_sum(x, "rows", bit, size)
    return x


def put(buf, piece, index, axis):
    return lax.dynamic_update_slice_in_dim(buf, jnp.expand_dims(piece, axis), index, axis)


def take(buf, index, axis):
    return lax.dynamic_index_in_dim(buf, index, axis, keepdims=False)


def gather_shards(shard):
    mine = lax.axis_index("rows")
    core = mine & 1
    batch = lax.axis_index("batch")
    block = shard[None]
    for bit, size in row_groups():
        place = (mine >> bit) & (size - 1)
        got = [block] + [swap(block, "rows", m << bit) for m in range(1, size)]
        buf = jnp.zeros((size,) + block.shape, block.dtype)
        for m, piece in enumerate(got):
            buf = put(buf, piece, place ^ m, 0)
        block = buf.reshape((-1,) + block.shape[1:])
    half = block.shape[0] // 2
    from_x = swap(block, "batch", 1)
    from_y = swap(block, "batch", 2)
    far_low = swap(from_x[:half], "batch", 2)
    far_high = swap(from_y[half:], "batch", 1)
    far = jnp.concatenate([far_low, far_high], axis=0)
    full = jnp.zeros((4, block.shape[0], 2) + block.shape[1:], block.dtype)
    for m, piece in enumerate((block, from_x, from_y, far)):
        other = swap(piece, "rows", 1)
        for value, where in ((piece, core), (other, 1 - core)):
            full = lax.dynamic_update_slice(
                full, value[None, :, None], (batch ^ m, 0, where, 0, 0)
            )
    return full


def scatter_sums(grad):
    mine = lax.axis_index("rows")
    core = mine & 1
    batch = lax.axis_index("batch")
    count = lax.axis_size("rows")
    grad = grad.reshape(4, count // 2, 2, -1, grad.shape[-1])
    got = swap(take(grad, 1 - core, 2).astype(BF16), "rows", 1)
    part = take(grad, core, 2).astype(F32) + got.astype(F32)
    half = part.shape[1] // 2
    own, to_x, to_y, far = [take(part, batch ^ m, 0) for m in range(4)]
    low = swap(far[:half].astype(BF16), "batch", 1).astype(F32)
    high = swap(far[half:].astype(BF16), "batch", 2).astype(F32)
    to_x = jnp.concatenate([to_x[:half], to_x[half:] + high], axis=0)
    to_y = jnp.concatenate([to_y[:half] + low, to_y[half:]], axis=0)
    from_x = swap(to_x.astype(BF16), "batch", 1)
    from_y = swap(to_y.astype(BF16), "batch", 2)
    own = own + from_x.astype(F32) + from_y.astype(F32)
    for bit, size in reversed(row_groups()):
        place = (mine >> bit) & (size - 1)
        own = own.reshape((size, -1) + own.shape[1:])
        total = take(own, place, 0)
        for m in range(1, size):
            total = total + swap(take(own, place ^ m, 0).astype(BF16), "rows", m << bit).astype(F32)
        own = total
    return own.reshape(own.shape[-2:])


def joined(pieces, *after):
    sizes = [piece.shape[0] for piece in pieces]

    def kernel(*refs):
        first = 0
        for ref, size in zip(refs, sizes):
            refs[-1][first : first + size] = ref[...].astype(BF16)
            first += size

    return pl.pallas_call(
        kernel,
        in_specs=[pl.BlockSpec(memory_space=pltpu.VMEM)] * len(pieces) + [pl.BlockSpec(memory_space=pl.ANY)] * len(after),
        out_specs=pl.BlockSpec(memory_space=pltpu.VMEM),
        out_shape=jax.ShapeDtypeStruct((sum(sizes),) + pieces[0].shape[1:], BF16),
    )(*pieces, *after)


def owners(batch_mask, core_mask, line):
    mine, batch = lax.axis_index("rows"), lax.axis_index("batch")
    chip = (batch ^ batch_mask) * (lax.axis_size("rows") // 2) + ((mine >> 1) ^ line)
    return chip * 2 + ((mine & 1) ^ core_mask)


def gather_pieces(shard, join):
    line = lax.axis_size("rows") // 2
    block = shard[None]
    for bit, size in row_groups():
        block = join([block] + [swap(block, "rows", m << bit) for m in range(1, size)])
    half = line // 2
    from_x = swap(block, "batch", 1)
    from_y = swap(block, "batch", 2)
    far_low = swap(from_x[:half], "batch", 2)
    far_high = swap(from_y[half:], "batch", 1)
    pieces = []
    for piece, mask, first in ((block, 0, 0), (from_x, 1, 0), (from_y, 2, 0), (far_low, 3, 0), (far_high, 3, half)):
        place = first + jnp.arange(piece.shape[0], dtype=jnp.int32)
        for array, core in ((piece, 0), (swap(piece, "rows", 1), 1)):
            pieces.append((array, owners(mask, core, place)))
    return pieces


class Assembly:
    def __init__(self, pieces, first, size):
        self.first, self.size = first, size
        owner = jnp.concatenate([owner for _, owner in pieces]).astype(jnp.int32)
        self.ins = [smem(owner * size)] + [whole(array) for array, _ in pieces]
        self.count = len(self.ins)

    def run(self, refs, held):
        starts, k = refs[0], 0
        for ref in refs[1:]:
            for j in range(ref.shape[0]):
                rows = pl.ds(pl.multiple_of(starts[k], self.size), self.size)
                held[rows, :] = ref[j, self.first : self.first + self.size, :]
                k += 1


def assemble_kernel(assembly, *refs):
    assembly.run(refs[:-1], refs[-1])


class Spread:
    def __init__(self, width, *rows):
        mine, batch = lax.axis_index("rows"), lax.axis_index("batch")
        line = lax.axis_size("rows") // 2
        self.chips = 4 * line
        self.sizes = [r // (2 * self.chips) for r in rows]
        self.direct = not any(size % 16 for size in self.sizes)
        chip = jnp.arange(self.chips, dtype=jnp.int32)
        far = (chip // line) ^ batch
        near = (chip % line) ^ (mine >> 1)
        half = line // 2
        place = ((near // half) * 4 + (far ^ (far >> 1))) * half + near % half
        self.ins = [smem(place.astype(jnp.int32)), smem((mine & 1).astype(jnp.int32).reshape(1))]
        shapes = [(r, width) for r in rows]
        if self.direct:
            shapes = [(self.chips, sum(self.sizes), width)] * 2
        self.outs = [out(shape, BF16, shape, lambda *_, n=len(shape): (0,) * n) for shape in shapes]

    def emit(self, weight, product, base, rows, place_ref, core_ref, outs):
        if not self.direct:
            outs[weight][pl.ds(base, rows), :] = product[0:rows, :].astype(BF16)
            return
        core = core_ref[0]
        size, low = self.sizes[weight], sum(self.sizes[:weight])
        pair = 2 * size
        first = base // pair
        for k in range(rows // pair):
            to = place_ref[first + k]
            for ref, c in ((outs[0], 1 - core), (outs[1], core)):
                start = pl.multiple_of(k * pair + c * size, 16)
                ref[to, low : low + size, :] = product[pl.ds(start, size), :].astype(BF16)


def in_order(*values):
    return lax.optimization_barrier(values)


class Sums:
    def __init__(self, spread, outs):
        self.direct = spread.direct
        if not self.direct:
            parts = [part.reshape(2 * spread.chips, size, -1) for part, size in zip(outs, spread.sizes)]
            self.total = scatter_sums(jnp.concatenate(parts, axis=1).reshape(-1, outs[0].shape[-1]))
            return
        shape = (2, 4, lax.axis_size("rows") // 4) + outs[0].shape[1:]
        self.keep = outs[1].reshape(shape)
        self.got = swap(outs[0], "rows", 1).reshape(shape)

    def part(self, half, index):
        return self.keep[half, index].astype(F32) + self.got[half, index].astype(F32)

    def send_far(self):
        return self.part(0, slice(1, 3)).astype(BF16), self.part(1, slice(2, 4)).astype(BF16)

    def take_far(self, sends):
        self.far = swap(sends[0], "batch", 1), swap(sends[1], "batch", 2)

    def send_near(self):
        from_x, from_y = self.far
        return (
            (self.part(1, 1) + from_y[0].astype(F32)).astype(BF16),
            (self.part(0, 3) + from_x[1].astype(F32)).astype(BF16),
        )

    def take_near(self, sends):
        self.near = swap(sends[0], "batch", 1), swap(sends[1], "batch", 2)

    def send_line(self):
        low = self.part(0, 0) + self.far[0][0].astype(F32) + self.near[1].astype(F32)
        high = self.part(1, 0) + self.far[1][1].astype(F32) + self.near[0].astype(F32)
        return jnp.concatenate([low, high], axis=0)

    def take_line(self, own):
        for bit, size in reversed(row_groups()):
            own = own.reshape((size, -1) + own.shape[1:])
            total = own[0]
            for m in range(1, size):
                total = total + swap(own[m].astype(BF16), "rows", m << bit).astype(F32)
            own = total
        self.total = own.reshape(own.shape[-2:])


CHUNK = 16
PAD = 8
NN, NT, TN = (1, 0), (1, 1), (0, 0)


def dot(left, right, dims):
    return lax.dot_general(left, right, ((dims[:1], dims[1:]), ((), ())), preferred_element_type=F32)


def softplus(z):
    e = jnp.exp(-jnp.abs(z))
    return jnp.maximum(z, 0.0) + jnp.where(e < 1e-3, e * (1.0 - 0.5 * e), jnp.log(1.0 + e))


def sigmoid(z):
    return 0.5 * jnp.tanh(0.5 * z) + 0.5


def wide(mask, width):
    return jnp.concatenate([mask] * (width // mask.shape[-1]), axis=-1)


def fold(v):
    return v[:8] + v[8:]


def down(v):
    return jnp.sum(v, axis=0, keepdims=True)


def loop(rows, body, init, unroll=2):
    def step(i, carry):
        return body(pl.ds(pl.multiple_of(i * CHUNK, CHUNK), CHUNK), carry)

    return lax.fori_loop(0, rows // CHUNK, step, init, unroll=unroll)


def zeros8(width, count=2):
    return tuple(jnp.zeros((8, width), F32) for _ in range(count))


def norm_stats(sums_ref, inv, gain):
    mean = sums_ref[0, 0:1, :] * inv
    rstd = lax.rsqrt(sums_ref[0, 1:2, :] * inv - mean * mean + EPS_NORM)
    return mean, rstd, gain * rstd


def call(kernel, grid, ins, outs, scratch=(), flops=0, nbytes=0, vmem=48):
    got = pl.pallas_call(
        kernel,
        grid=grid,
        in_specs=[spec for _, spec in ins],
        out_specs=[spec for _, spec in outs],
        out_shape=[shape for shape, _ in outs],
        scratch_shapes=list(scratch),
        compiler_params=pltpu.CompilerParams(
            dimension_semantics=("arbitrary",) * len(grid), vmem_limit_bytes=vmem * 1024 * 1024
        ),
        cost_estimate=pl.CostEstimate(flops=flops, bytes_accessed=nbytes, transcendentals=0),
    )(*[array for array, _ in ins])
    return got[0] if len(outs) == 1 else got


def block(shape, index, **kw):
    return pl.BlockSpec(shape, index, **kw)


def listed(got):
    return list(got) if isinstance(got, (list, tuple)) else [got]


def whole(array):
    zeros = (0,) * len(array.shape)
    return (array, pl.BlockSpec(array.shape, lambda *_: zeros, pipeline_mode=pl.Buffered(1)))


def smem(array):
    return (array, pl.BlockSpec(memory_space=pltpu.SMEM))


def anywhere(array):
    return (array, pl.BlockSpec(memory_space=pl.ANY))


def out(shape, dtype, spec_shape, index):
    return (jax.ShapeDtypeStruct(shape, dtype), pl.BlockSpec(spec_shape, index))


def gram_kernel(task_ref, mask_ref, out_ref):
    lanes = mask_ref.shape[-1]
    chan = task_ref.shape[-1]

    @pl.when(pl.program_id(0) == 0)
    def _():
        out_ref[...] = jnp.zeros_like(out_ref)

    def step(rows, carry):
        sums = [jnp.zeros((CHUNK, lanes), F32)] * 6
        for col in range(chan // lanes):
            cols = pl.ds(col * lanes, lanes)
            t = [task_ref[k, 0, 0, 0, rows, cols].astype(F32) for k in range(3)]
            pairs = [t[i] * t[j] for i in range(3) for j in range(i, 3)]
            sums = [s + p for s, p in zip(sums, pairs)]
        mask = mask_ref[0, 0, rows, :]
        return tuple(c + fold(s * mask) for c, s in zip(carry, sums))

    got = loop(task_ref.shape[4], step, zeros8(lanes, 6), unroll=1)
    for k in range(6):
        out_ref[k : k + 1, :] += down(got[k])


def first_kernel(assembly, x_ref, mask_ref, gram_ref, *refs):
    pieces, (wide_ref, low_ref, sums_ref, w_ref) = refs[: assembly.count], refs[assembly.count :]
    width = w_ref.shape[1]

    @pl.when(pl.program_id(0) == 0)
    def _():
        assembly.run(pieces, w_ref)

    wide_ref[0] = dot(x_ref[0], w_ref[...], NN)

    def step(rows, carry):
        v = wide_ref[0, rows, :]
        low_ref[0, rows, :] = v.astype(BF16)
        kept = v * wide(mask_ref[0, 0, rows, :], width)
        return carry[0] + fold(kept), carry[1] + fold(kept * v)

    got = loop(x_ref.shape[1], step, zeros8(width))
    sums_ref[0] = jnp.zeros_like(sums_ref[0])
    sums_ref[0, 0:1, :] = down(got[0])
    sums_ref[0, 1:2, :] = down(got[1])
    for k in range(6):
        lane = (k % 4) * 128
        sums_ref[0, 2 + k // 4 : 3 + k // 4, lane : lane + 128] = gram_ref[0, k : k + 1, :]


def upstream_kernel(sums_ref, task_ref, mask_ref, *refs):
    out_ref, coeff_ref = refs[-2:]
    lanes = mask_ref.shape[-1]

    @pl.when((pl.program_id(0) == 0) & (pl.program_id(1) == 0))
    def _():
        def entry(k):
            lane, row = (k % 4) * 128, 2 + k // 4
            both = sums_ref[0, row : row + 1, lane : lane + 128] + sums_ref[1, row : row + 1, lane : lane + 128]
            return jnp.sum(both, axis=1, keepdims=True)

        place = {}
        k = 0
        for i in range(3):
            for j in range(i, 3):
                place[i, j] = place[j, i] = entry(k)
                k += 1
        trace = place[0, 0] + place[1, 1] + place[2, 2]
        ymat = [[place[i, j] / trace for j in range(3)] for i in range(3)]
        zmat = [[jnp.full((1, 1), 1.0 if i == j else 0.0, F32) for j in range(3)] for i in range(3)]

        def mul(a, b):
            return [
                [a[i][0] * b[0][j] + a[i][1] * b[1][j] + a[i][2] * b[2][j] for j in range(3)]
                for i in range(3)
            ]

        for _ in range(NEWTON):
            zy = mul(zmat, ymat)
            pmat = [[(1.5 if i == j else 0.0) - 0.5 * zy[i][j] for j in range(3)] for i in range(3)]
            ymat = mul(ymat, pmat)
            zmat = mul(pmat, zmat)
        for i in range(3):
            value = (zmat[i][0] + zmat[i][1] + zmat[i][2]) / jnp.sqrt(F32(3.0))
            coeff_ref[i] = jnp.broadcast_to(value, (8, lanes))

    def step(rows, carry):
        mask = mask_ref[0, 0, rows, :]
        c = [jnp.concatenate([coeff_ref[i]] * (CHUNK // 8), axis=0) * mask for i in range(3)]
        for col in range(task_ref.shape[-1] // lanes):
            cols = pl.ds(col * lanes, lanes)
            t = [task_ref[k, 0, 0, 0, rows, cols].astype(F32) for k in range(3)]
            out_ref[0, rows, cols] = c[0] * t[0] + c[1] * t[1] + c[2] * t[2]
        return carry

    loop(task_ref.shape[4], step, 0, unroll=1)


def shifted_sum(parts, row, start, rows, sign):
    at = PAD + start
    low, high = at + sign * DILATION_SIZE, at - sign * DILATION_SIZE
    return (
        parts[1, row, at : at + rows, :]
        + parts[0, row, low : low + rows, :]
        + parts[2, row, high : high + rows, :]
    )


def clear_pads(ref):
    edge = ref.shape[-2]
    zero = jnp.zeros(ref.shape[:-2] + (PAD, ref.shape[-1]), ref.dtype)
    ref[..., 0:PAD, :] = zero
    ref[..., edge - PAD : edge, :] = zero


def second_kernel(
    inv_ref, sums_ref, param_ref, own_ref, up_ref, down_ref, mask_ref, w_ref, *refs
):
    h_ref, wide_ref, low_ref, out_ref, cat_ref, part_ref = refs[-6:]
    micro = pl.program_id(0)
    width = own_ref.shape[-1]
    pixels = own_ref.shape[1]
    columns = part_ref.shape[2] - 2 * PAD

    @pl.when(micro == 0)
    def _():
        clear_pads(part_ref)

    mean, rstd, scale = norm_stats(sums_ref, inv_ref[micro], param_ref[0:1, :])
    offset = param_ref[1:2, :] - mean * scale
    for k, ref in enumerate((up_ref, own_ref, down_ref)):
        def step(rows, carry):
            z = ref[0, rows, :].astype(F32) * scale + offset
            h = (softplus(z) * wide(mask_ref[k, 0, rows, :], width)).astype(BF16)
            h_ref[k, 0, rows, :] = h
            cat_ref[rows, k * width : (k + 1) * width] = h
            return carry

        loop(pixels, step, 0)

    for tx in range(3):
        taps = [w_ref[(3 * ty + tx) * width : (3 * ty + tx + 1) * width, :] for ty in range(3)]
        product = dot(cat_ref[...], jnp.concatenate(taps, axis=0), NN)
        part_ref[tx, :, PAD : PAD + columns, :] = product.reshape(-1, columns, width)

    def row_step(row, carry):
        for start in range(0, columns, CHUNK):
            rows = pl.ds(pl.multiple_of(row * columns + start, CHUNK), CHUNK)
            v = shifted_sum(part_ref, row, start, CHUNK, -1)
            wide_ref[0, rows, :] = v
            low_ref[0, rows, :] = v.astype(BF16)
            kept = v * wide(mask_ref[1, 0, rows, :], width)
            carry = carry[0] + fold(kept), carry[1] + fold(kept * v)
        return carry

    got = lax.fori_loop(0, pixels // columns, row_step, zeros8(width))
    out_ref[0, 0:1, :] = down(got[0])
    out_ref[0, 1:2, :] = down(got[1])


def third_kernel(inv_ref, sums_ref, param_ref, a_ref, mask_ref, w_ref, h_ref, wide_ref, out_ref):
    micro = pl.program_id(0)
    width = a_ref.shape[-1]
    tile = 512
    mean, rstd, scale = norm_stats(sums_ref, inv_ref[micro], param_ref[0:1, :])
    offset = param_ref[1:2, :] - mean * scale

    def step(rows, carry):
        z = a_ref[0, rows, :] * scale + offset
        h_ref[0, rows, :] = (softplus(z) * wide(mask_ref[0, 0, rows, :], width)).astype(BF16)
        return carry

    loop(a_ref.shape[1], step, 0)
    for col in range(0, w_ref.shape[0], tile):
        cols = pl.ds(col, tile)
        wide_ref[0, :, cols] = dot(h_ref[0], w_ref[cols, :], NT)

        def sum_step(rows, carry):
            v = wide_ref[0, rows, cols]
            kept = v * wide(mask_ref[0, 0, rows, :], tile)
            return carry[0] + fold(kept), carry[1] + fold(kept * v)

        got = loop(a_ref.shape[1], sum_step, zeros8(tile))
        out_ref[0, 0:1, cols] = down(got[0])
        out_ref[0, 1:2, cols] = down(got[1])


def peak_kernel(
    inv_ref, sums_ref, param_ref, a_ref, x_ref, up_ref, mask_ref, after_ref, late_ref, block_ref, du_ref, out_ref
):
    width = a_ref.shape[-1]
    mean, rstd, scale = norm_stats(sums_ref, inv_ref[pl.program_id(0)], param_ref[0:1, :])
    shift = param_ref[1:2, :]

    def step(rows, carry):
        centred = a_ref[0, rows, :] - mean
        u = centred * scale + (shift + x_ref[0, rows, :].astype(F32))
        mask = wide(mask_ref[0, 0, rows, :], width)
        block_ref[0, rows, :] = (softplus(u) * mask).astype(BF16)
        du = up_ref[0, rows, :] * sigmoid(u)
        du_ref[0, rows, :] = du
        return carry[0] + fold(du), carry[1] + fold(du * centred)

    got = loop(a_ref.shape[1], step, zeros8(width))
    out_ref[0, 0:1, :] = down(got[0])
    out_ref[0, 1:2, :] = down(got[1]) * rstd


def lower_consts(stats_ref, grads_ref, inv, gain):
    mean, rstd, scale = norm_stats(stats_ref, inv, gain)
    return mean, scale, grads_ref[0, 0:1, :] * inv, grads_ref[0, 1:2, :] * inv * rstd


def back_third_kernel(
    inv_ref, stats3_ref, grads3_ref, stats2_ref, param3_ref, param2_ref,
    a3_ref, du_ref, a2_ref, mask_ref, w_ref,
    d_ref, wide_ref, low_ref, out_ref,
):
    inv = inv_ref[pl.program_id(0)]
    tile = 512
    for col in range(0, a3_ref.shape[2], tile):
        cols = pl.ds(col, tile)
        mean = stats3_ref[0, 0:1, cols] * inv
        rstd = lax.rsqrt(stats3_ref[0, 1:2, cols] * inv - mean * mean + EPS_NORM)
        scale = param3_ref[0:1, cols] * rstd
        base = grads3_ref[0, 0:1, cols] * inv
        slope = grads3_ref[0, 1:2, cols] * inv * rstd

        def step(rows, carry):
            d = du_ref[0, rows, cols] - (base + (a3_ref[0, rows, cols] - mean) * slope)
            d_ref[0, rows, cols] = (d * scale * wide(mask_ref[0, 0, rows, :], tile)).astype(BF16)
            return carry

        loop(a3_ref.shape[1], step, 0)
    wide_ref[0] = dot(d_ref[0], w_ref[...], NN)
    width = w_ref.shape[1]
    mean, rstd, scale = norm_stats(stats2_ref, inv, param2_ref[0:1, :])
    shift = param2_ref[1:2, :]

    def last(rows, carry):
        centred = a2_ref[0, rows, :] - mean
        gate = sigmoid(centred * scale + shift) * wide(mask_ref[0, 0, rows, :], width)
        dz = wide_ref[0, rows, :] * gate
        wide_ref[0, rows, :] = dz
        low_ref[0, rows, :] = dz.astype(BF16)
        return carry[0] + fold(dz), carry[1] + fold(dz * centred)

    got = loop(a2_ref.shape[1], last, zeros8(width))
    out_ref[0, 0:1, :] = down(got[0])
    out_ref[0, 1:2, :] = down(got[1]) * rstd


def lower_second_kernel(
    inv_ref, stats2_ref, grads2_ref, param2_ref,
    a2_ref, a2_up_ref, a2_down_ref, dz_ref, dz_up_ref, dz_down_ref, mask_ref, cat_ref, shift_ref, pad_ref,
):
    inv = inv_ref[pl.program_id(0)]
    pixels, width = a2_ref.shape[1:]
    columns = pad_ref.shape[1] - 2 * PAD

    @pl.when(pl.program_id(0) == 0)
    def _():
        clear_pads(pad_ref)

    mean, scale, base, slope = lower_consts(stats2_ref, grads2_ref, inv, param2_ref[0:1, :])

    def lowered(k, a, dz, rows):
        d = dz.astype(F32) - (base + (a.astype(F32) - mean) * slope)
        return d * scale * wide(mask_ref[k, 0, rows, :], width)

    for k, a_ref, d_ref, place in ((0, a2_up_ref, dz_up_ref, 2), (2, a2_down_ref, dz_down_ref, 0)):
        def step(rows, carry):
            d = lowered(k, a_ref[0, rows, :], d_ref[0, rows, :], rows)
            cat_ref[0, rows, place * width : (place + 1) * width] = d.astype(BF16)
            return carry

        loop(pixels, step, 0)

    def own_step(row, carry):
        for start in range(0, columns, CHUNK):
            rows = pl.ds(pl.multiple_of(row * columns + start, CHUNK), CHUNK)
            d = lowered(1, a2_ref[0, rows, :], dz_ref[0, rows, :], rows)
            low = d.astype(BF16)
            cat_ref[0, rows, width : 2 * width] = low
            shift_ref[0, rows, width : 2 * width] = low
            pad_ref[row, PAD + start : PAD + start + CHUNK, :] = d
        for start in range(0, columns, CHUNK):
            rows = pl.ds(pl.multiple_of(row * columns + start, CHUNK), CHUNK)
            for tx in (-1, 1):
                at = PAD + start - tx * DILATION_SIZE
                moved = pad_ref[row, at : at + CHUNK, :].astype(BF16)
                shift_ref[0, rows, (tx + 1) * width : (tx + 2) * width] = moved
        return carry

    lax.fori_loop(0, pixels // columns, own_step, 0)


def back_second_kernel(
    inv_ref, stats1_ref, param1_ref, cat_ref, a1_ref, mask_ref, w_ref, after_ref, wide_ref, out_ref, part_ref
):
    inv = inv_ref[pl.program_id(0)]
    pixels, width = a1_ref.shape[1:]
    columns = part_ref.shape[2] - 2 * PAD

    @pl.when(pl.program_id(0) == 0)
    def _():
        clear_pads(part_ref)

    for tx in range(3):
        taps = [w_ref[(3 * ty + tx) * width : (3 * ty + tx + 1) * width, :] for ty in range(3)]
        product = dot(cat_ref[0], jnp.concatenate(taps, axis=1), NT)
        part_ref[tx, :, PAD : PAD + columns, :] = product.reshape(-1, columns, width)

    mean1, rstd1, scale1 = norm_stats(stats1_ref, inv, param1_ref[0:1, :])
    shift1 = param1_ref[1:2, :]

    def row_step(row, carry):
        for start in range(0, columns, CHUNK):
            rows = pl.ds(pl.multiple_of(row * columns + start, CHUNK), CHUNK)
            centred = a1_ref[0, rows, :] - mean1
            gate = sigmoid(centred * scale1 + shift1) * wide(mask_ref[0, 0, rows, :], width)
            dz = shifted_sum(part_ref, row, start, CHUNK, 1) * gate
            wide_ref[0, rows, :] = dz
            carry = carry[0] + fold(dz), carry[1] + fold(dz * centred)
        return carry

    got = lax.fori_loop(0, pixels // columns, row_step, zeros8(width))
    out_ref[0, 0:1, :] = down(got[0])
    out_ref[0, 1:2, :] = down(got[1]) * rstd1


def grads_kernel(spread, h_ref, d_ref, d3_ref, h2_ref, place_ref, core_ref, *refs):
    outs, product = refs[:-1], refs[-1]
    width = h_ref.shape[-1]
    step = pl.program_id(0)

    @pl.when(step < 3)
    def _():
        for tx in range(3):
            rows = pl.ds(pl.multiple_of((3 * step + tx) * width, width), width)
            product[rows, :] = dot(h_ref[0], d_ref[:, tx * width : (tx + 1) * width], TN)

    @pl.when(step == 2)
    def _():
        spread.emit(0, product, 0, product.shape[0], place_ref, core_ref, outs)

    @pl.when(step >= 3)
    def _():
        rows = d3_ref.shape[1]
        product[0:rows, :] = dot(d3_ref[...], h2_ref[...], TN)
        spread.emit(1, product, pl.multiple_of((step - 3) * rows, rows), rows, place_ref, core_ref, outs)


def first_back_kernel(
    spread, inv_ref, stats_ref, grads_ref, param_ref, dz_ref, a_ref, mask_ref, x_ref, place_ref, core_ref, *refs
):
    d_ref, outs, product = refs[0], refs[1:-1], refs[-1]
    pixels, width = dz_ref.shape[1:]

    @pl.when(pl.program_id(0) == 0)
    def _():
        for micro in range(dz_ref.shape[0]):
            inv = inv_ref[micro]
            mean, scale, base, slope = lower_consts(
                stats_ref.at[micro : micro + 1], grads_ref.at[micro : micro + 1], inv, param_ref[0:1, :]
            )

            def step(rows, carry):
                d = dz_ref[micro, rows, :] - (base + (a_ref[micro, rows, :] - mean) * slope)
                d = d * scale * wide(mask_ref[0, micro, rows, :], width)
                d_ref[micro, rows, :] = d.astype(BF16)
                return carry

            loop(pixels, step, 0)

    product[...] = dot(x_ref[...], d_ref[...].reshape(-1, width), TN)
    rows = product.shape[0]
    spread.emit(0, product, pl.multiple_of(pl.program_id(0) * rows, rows), rows, place_ref, core_ref, outs)


def input_grad_kernel(d_ref, w_ref, du_ref, out_ref):
    out_ref[...] = (dot(d_ref[...], w_ref[...], NT) + du_ref[...]).astype(BF16)


def adamw(weight, first, second, grad, rate, decay):
    new_first = BETA_ONE * first + (1.0 - BETA_ONE) * grad
    new_second = BETA_TWO * second + (1.0 - BETA_TWO) * grad * grad
    first_hat = new_first / (1.0 - BETA_ONE**STEP)
    second_hat = new_second / (1.0 - BETA_TWO**STEP)
    new_weight = weight - rate * (first_hat / (jnp.sqrt(second_hat) + ADAM_EPS) + decay * weight)
    return (new_weight, new_first, new_second)


def neighbours(x):
    count = lax.axis_size("rows")
    above = lax.ppermute(x, "rows", [(i, i + 1) for i in range(count - 1)])
    below = lax.ppermute(x, "rows", [(i + 1, i) for i in range(count - 1)])
    return above, below


def per_device(
    features, task_grads, row_counts, col_counts,
    weight_in, weight_mid, weight_out,
    first_in, first_mid, first_out,
    second_in, second_mid, second_out,
    norm_params, norm_first, norm_second,
):
    micros, _, row_span, columns, chan = features.shape
    inner = weight_in.shape[1]
    pixels = row_span * columns
    total_pixels = micros * pixels
    batch = lax.axis_index("batch")
    own_rows = lax.dynamic_index_in_dim(row_counts, batch, 1, keepdims=False)
    own_cols = lax.dynamic_index_in_dim(col_counts, batch, 1, keepdims=False)
    base = lax.axis_index("rows") * row_span + jnp.arange(-1, 2, dtype=jnp.int32) * row_span
    row_ids = base[:, None] + jnp.arange(row_span, dtype=jnp.int32)
    col_ids = jnp.arange(columns, dtype=jnp.int32)
    in_rows = (row_ids[:, None] >= 0) & (row_ids[:, None] < own_rows[None, :, None])
    in_cols = col_ids < own_cols[:, None]
    masks = (in_rows[:, :, :, None] & in_cols[None, :, None, :]).astype(F32)
    masks = jnp.broadcast_to(masks.reshape(3, micros, pixels, 1), (3, micros, pixels, 128))
    inverse = 1.0 / jnp.sum(row_counts * col_counts, axis=1).astype(F32)

    w_mid = lax.all_gather(weight_mid.astype(BF16), ("batch", "rows"), axis=0, tiled=True)
    grams = []
    for micro in range(micros):
        grams.append(call(
            gram_kernel, (row_span,),
            [
                (task_grads, block((3, 1, 1, 1, columns, chan), functools.partial(lambda m, r: (0, m, 0, r, 0, 0), micro))),
                (masks, block((1, 1, columns, 128), functools.partial(lambda m, r: (1, m, r, 0), micro))),
            ],
            [out((8, 128), F32, (8, 128), lambda r: (0, 0))],
            flops=6 * total_pixels * chan, nbytes=3 * total_pixels * chan,
        ))
    x = features.reshape(micros, pixels, chan)
    params = [norm_params[:, :inner], norm_params[:, inner : 2 * inner], norm_params[:, 2 * inner :]]

    def per_micro(array):
        return (array, block((1,) + array.shape[1:], lambda m, *_: (m,) + (0,) * (len(array.shape) - 1)))

    def out_micro(width, dtype, rows=pixels):
        return out((micros, rows, width), dtype, (1, rows, width), lambda m: (m, 0, 0))

    own_mask = (masks, block((1, 1, pixels, 128), lambda m, *_: (1, m, 0, 0)))
    all_masks = (masks, block((3, 1, pixels, 128), lambda m: (0, m, 0, 0)))
    row_mask = (masks, block((1, 1, columns, 128), lambda m, r: (1, m, r, 0)))
    task_rows = (
        task_grads, block((3, 1, 1, 1, columns, chan), lambda m, r: (0, m, 0, r, 0, 0))
    )
    big = total_pixels * chan
    small = total_pixels * inner
    part_rows = weight_in.shape[0]
    both = jnp.concatenate([weight_in.astype(BF16), weight_out.T.astype(BF16)], axis=0)
    if part_rows % 16:
        full = gather_shards(both).reshape(-1, 2, part_rows, inner)
        zero = jnp.zeros(1, jnp.int32)
        ins_in, ins_out = [Assembly([(full[:, k].reshape(1, -1, inner), zero)], 0, chan) for k in range(2)]
    else:
        pieces = gather_pieces(both, lambda got: joined(got, grams[0]))
        ins_in, ins_out = [Assembly(pieces, k * part_rows, part_rows) for k in range(2)]
    whole_weight = out((chan, inner), BF16, (chan, inner), lambda *_: (0, 0))
    a_one, a_one_low, part, w_in = call(
        functools.partial(first_kernel, ins_in), (micros,),
        [per_micro(x), own_mask, per_micro(jnp.stack(grams)), *ins_in.ins],
        [out_micro(inner, F32), out_micro(inner, BF16), out_micro(inner, F32, 4), whole_weight],
        flops=2 * big * inner, nbytes=2 * big + 8 * small,
    )
    a_one_up, a_one_down = neighbours(a_one_low)
    stats_one = all_sum(part)
    w_out = call(
        functools.partial(assemble_kernel, ins_out), (1,), ins_out.ins, [whole_weight], nbytes=8 * chan * inner
    )
    upstream = call(
        upstream_kernel, (micros, row_span),
        [whole(stats_one), task_rows, row_mask],
        [out((micros, pixels, chan), F32, (1, columns, chan), lambda m, r: (m, r, 0))],
        [pltpu.VMEM((3, 8, 128), F32)],
        flops=8 * big, nbytes=10 * big,
    )
    padded = (3, row_span, columns + 2 * PAD, inner)
    taps = [pltpu.VMEM((pixels, 3 * inner), BF16), pltpu.VMEM(padded, F32)]
    h_one, a_two, a_two_low, part = call(
        second_kernel, (micros,),
        [
            smem(inverse), per_micro(stats_one), whole(params[0]), per_micro(a_one),
            per_micro(a_one_up), per_micro(a_one_down), all_masks,
            whole(w_mid), anywhere(upstream),
        ],
        [
            out((3, micros, pixels, inner), BF16, (3, 1, pixels, inner), lambda m: (0, m, 0, 0)),
            out_micro(inner, F32), out_micro(inner, BF16), out_micro(inner, F32, 2),
        ],
        taps,
        flops=18 * small * inner, nbytes=20 * small + 18 * inner * inner,
    )
    a_two_up, a_two_down = neighbours(a_two_low)
    stats_two = all_sum(part)
    h_two, a_three, part = call(
        third_kernel, (micros,),
        [
            smem(inverse), per_micro(stats_two), whole(params[1]), per_micro(a_two), own_mask,
            whole(w_out),
        ],
        [out_micro(inner, BF16), out_micro(chan, F32), out_micro(chan, F32, 2)],
        flops=2 * big * inner, nbytes=4 * big + 8 * small,
    )
    stats_three = all_sum(part)
    tile = 512

    def tiled(array):
        return (array, block((1, array.shape[1], tile), lambda m, c: (m, 0, c)))

    def out_tiled(dtype, rows=pixels):
        return out((micros, rows, chan), dtype, (1, rows, tile), lambda m, c: (m, 0, c))

    block_out, d_resid, part = call(
        peak_kernel, (micros, chan // tile),
        [
            smem(inverse), tiled(stats_three), (params[2], block((2, tile), lambda m, c: (0, c))),
            tiled(a_three), tiled(x), tiled(upstream), own_mask, anywhere(a_two_up), anywhere(a_two_down),
        ],
        [out_tiled(BF16), out_tiled(F32), out_tiled(F32, 2)],
        flops=40 * big, nbytes=16 * big,
    )
    grads_three = all_sum(part)
    d_three, dz_two, dz_two_low, part = call(
        back_third_kernel, (micros,),
        [
            smem(inverse), per_micro(stats_three), per_micro(grads_three), per_micro(stats_two),
            whole(params[2]), whole(params[1]), per_micro(a_three), per_micro(d_resid),
            per_micro(a_two), own_mask, whole(w_out),
        ],
        [out_micro(chan, BF16), out_micro(inner, F32), out_micro(inner, BF16), out_micro(inner, F32, 2)],
        flops=2 * big * inner, nbytes=10 * big,
    )
    dz_two_up, dz_two_down = neighbours(dz_two_low)
    grads_two = all_sum(part)
    d_two_cat, d_two = call(
        lower_second_kernel, (micros,),
        [
            smem(inverse), per_micro(stats_two), per_micro(grads_two), whole(params[1]),
            per_micro(a_two), per_micro(a_two_up), per_micro(a_two_down),
            per_micro(dz_two), per_micro(dz_two_up), per_micro(dz_two_down), all_masks,
        ],
        [out_micro(3 * inner, BF16), out_micro(3 * inner, BF16)],
        [pltpu.VMEM(padded[1:], F32)],
        flops=60 * small, nbytes=28 * small,
    )
    spread = Spread(inner, 9 * inner, chan)
    grads = call(
        functools.partial(grads_kernel, spread), (3 + chan // tile,),
        [
            (
                h_one.reshape(3, total_pixels, inner),
                block((1, total_pixels, inner), lambda t: (jnp.minimum(t, 2), 0, 0)),
            ),
            whole(d_two.reshape(total_pixels, 3 * inner)),
            (
                d_three.reshape(total_pixels, chan),
                block((total_pixels, tile), lambda t: (0, jnp.maximum(t - 3, 0))),
            ),
            whole(h_two.reshape(total_pixels, inner)), *spread.ins,
        ],
        spread.outs, [pltpu.VMEM((9 * inner, inner), F32)],
        flops=18 * small * inner + 2 * big * inner, nbytes=12 * small + 18 * inner * inner,
    )
    sums = Sums(spread, grads)
    dz_one, part = call(
        back_second_kernel, (micros,),
        [
            smem(inverse), per_micro(stats_one), whole(params[0]), per_micro(d_two_cat),
            per_micro(a_one), own_mask, whole(w_mid), anywhere(grads[0]),
        ],
        [out_micro(inner, F32), out_micro(inner, F32, 2)],
        [pltpu.VMEM(padded, F32)],
        flops=18 * small * inner, nbytes=30 * small + 18 * inner * inner,
    )
    chip_one = chip_sums(part)
    if sums.direct:
        chip_one, *sends = in_order(chip_one, *sums.send_far())
        sums.take_far(sends)
    grads_one = line_sums(chip_one)
    spread_in = Spread(inner, chan)
    d_one, *grad_in = call(
        functools.partial(first_back_kernel, spread_in), (chan // tile,),
        [
            smem(inverse), whole(stats_one), whole(grads_one), whole(params[0]), whole(dz_one), whole(a_one),
            (masks, block((1, micros, pixels, 128), lambda c: (1, 0, 0, 0))),
            (x.reshape(total_pixels, chan), block((total_pixels, tile), lambda c: (0, c))),
            *spread_in.ins,
        ],
        [out((micros, pixels, inner), BF16, (micros, pixels, inner), lambda c: (0, 0, 0)), *spread_in.outs],
        [pltpu.VMEM((tile, inner), F32)],
        flops=2 * big * inner, nbytes=4 * big,
    )
    if sums.direct:
        d_one, *rest = in_order(d_one, *grad_in, *sums.far)
        grad_in, sums.far = rest[:2], rest[2:]
    sums_in = Sums(spread_in, grad_in)
    if sums.direct:
        d_one, *sends = in_order(d_one, *sums.send_near())
        sums.take_near(sends)
    strip = total_pixels // 4
    input_grad = call(
        input_grad_kernel, (4,),
        [
            (d_one.reshape(total_pixels, inner), block((strip, inner), lambda s: (s, 0))),
            whole(w_in),
            (d_resid.reshape(total_pixels, chan), block((strip, chan), lambda s: (s, 0))),
        ],
        [out((total_pixels, chan), BF16, (strip, chan), lambda s: (s, 0))],
        flops=2 * big * inner, nbytes=8 * big,
    )
    if sums.direct:
        input_grad, *rest = in_order(input_grad, *sums.near, *sums_in.send_far())
        sums.near = rest[:2]
        sums_in.take_far(rest[2:])
        sums.take_line(sums.send_line())
        sums_in.take_near(sums_in.send_near())
        sums_in.take_line(sums_in.send_line())
    grad_in, grad_both = sums_in.total, sums.total
    grad_mid, grad_out = grad_both[: weight_mid.shape[0]], grad_both[weight_mid.shape[0] :]

    norm_total = jnp.concatenate([grads_one[:, :2], grads_two, grads_three], axis=2)
    norm_total = jnp.sum(norm_total, axis=0)[::-1]
    local_squares = (
        jnp.sum(grad_in * grad_in) + jnp.sum(grad_both * grad_both)
    )
    total = all_sum(local_squares.reshape(1, 1)) + jnp.sum(norm_total * norm_total)
    grad_norm = jnp.sqrt(total)
    scale = CLIP / jnp.maximum(grad_norm, CLIP)
    new_in = adamw(weight_in, first_in, second_in, grad_in * scale, RATE, DECAY)
    new_mid = adamw(weight_mid, first_mid, second_mid, grad_mid * scale, RATE, DECAY)
    new_out = adamw(weight_out, first_out, second_out, (grad_out * scale).T, RATE, DECAY)
    new_norm = adamw(norm_params, norm_first, norm_second, norm_total * scale, RATE_NORM, 0.0)
    shape = (micros, 1, row_span, columns, chan)
    return (
        block_out.reshape(shape),
        input_grad.reshape(shape),
        *[group[k] for k in range(3) for group in (new_in, new_mid, new_out)],
        *new_norm,
        grad_norm.reshape(1),
    )


def solution(mesh):
    acts = P(None, "batch", "rows", None, None)
    by_row, by_col = P(("batch", "rows"), None), P(None, ("batch", "rows"))
    weights = (by_row, by_row, by_col)
    return jax.shard_map(
        per_device,
        mesh=mesh,
        in_specs=(
            acts, P(None, None, "batch", "rows", None, None), P(), P(), *(weights * 3), P(), P(), P()
        ),
        out_specs=(acts, acts, *(weights * 3), P(), P(), P(), P()),
        check_vma=False,
    )
```

```python
import functools

import jax
import jax.numpy as jnp
from jax import lax
from jax.experimental import pallas as pl
from jax.experimental.pallas import tpu as pltpu
from jax.sharding import PartitionSpec as P

DILATION_SIZE = 4
NEWTON = 6
STEP = 10

EPS_NORM = 1e-05
CLIP = 1.0
RATE = 0.02
RATE_NORM = 0.3
BETA_ONE = 0.9
BETA_TWO = 0.999
ADAM_EPS = 1e-08
DECAY = 0.01

F32 = jnp.float32
BF16 = jnp.bfloat16


def swap(x, axis, mask):
    return lax.ppermute(x, axis, [(i, i ^ mask) for i in range(lax.axis_size(axis))])


def row_groups():
    groups = []
    bit, rest = 1, lax.axis_size("rows") // 2
    while rest > 1:
        size = min(4, rest)
        groups.append((bit, size))
        bit += size.bit_length() - 1
        rest //= size
    return groups


def group_sum(x, axis, shift, size):
    got = [x] + [swap(x, axis, m << shift) for m in range(1, size)]
    if size == 2:
        return got[0] + got[1]
    return (got[0] + got[1]) + (got[2] + got[3])


def chip_sums(x):
    return group_sum(group_sum(x, "rows", 0, 2), "batch", 0, lax.axis_size("batch"))


def all_sum(x):
    return line_sums(chip_sums(x))


def line_sums(x):
    for bit, size in row_groups():
        x = group_sum(x, "rows", bit, size)
    return x


def put(buf, piece, index, axis):
    return lax.dynamic_update_slice_in_dim(buf, jnp.expand_dims(piece, axis), index, axis)


def take(buf, index, axis):
    return lax.dynamic_index_in_dim(buf, index, axis, keepdims=False)


def gather_shards(shard):
    mine = lax.axis_index("rows")
    core = mine & 1
    batch = lax.axis_index("batch")
    block = shard[None]
    for bit, size in row_groups():
        place = (mine >> bit) & (size - 1)
        got = [block] + [swap(block, "rows", m << bit) for m in range(1, size)]
        buf = jnp.zeros((size,) + block.shape, block.dtype)
        for m, piece in enumerate(got):
            buf = put(buf, piece, place ^ m, 0)
        block = buf.reshape((-1,) + block.shape[1:])
    half = block.shape[0] // 2
    from_x = swap(block, "batch", 1)
    from_y = swap(block, "batch", 2)
    far_low = swap(from_x[:half], "batch", 2)
    far_high = swap(from_y[half:], "batch", 1)
    far = jnp.concatenate([far_low, far_high], axis=0)
    full = jnp.zeros((4, block.shape[0], 2) + block.shape[1:], block.dtype)
    for m, piece in enumerate((block, from_x, from_y, far)):
        other = swap(piece, "rows", 1)
        for value, where in ((piece, core), (other, 1 - core)):
            full = lax.dynamic_update_slice(
                full, value[None, :, None], (batch ^ m, 0, where, 0, 0)
            )
    return full


def scatter_sums(grad):
    mine = lax.axis_index("rows")
    core = mine & 1
    batch = lax.axis_index("batch")
    count = lax.axis_size("rows")
    grad = grad.reshape(4, count // 2, 2, -1, grad.shape[-1])
    got = swap(take(grad, 1 - core, 2).astype(BF16), "rows", 1)
    part = take(grad, core, 2).astype(F32) + got.astype(F32)
    half = part.shape[1] // 2
    own, to_x, to_y, far = [take(part, batch ^ m, 0) for m in range(4)]
    low = swap(far[:half].astype(BF16), "batch", 1).astype(F32)
    high = swap(far[half:].astype(BF16), "batch", 2).astype(F32)
    to_x = jnp.concatenate([to_x[:half], to_x[half:] + high], axis=0)
    to_y = jnp.concatenate([to_y[:half] + low, to_y[half:]], axis=0)
    from_x = swap(to_x.astype(BF16), "batch", 1)
    from_y = swap(to_y.astype(BF16), "batch", 2)
    own = own + from_x.astype(F32) + from_y.astype(F32)
    for bit, size in reversed(row_groups()):
        place = (mine >> bit) & (size - 1)
        own = own.reshape((size, -1) + own.shape[1:])
        total = take(own, place, 0)
        for m in range(1, size):
            total = total + swap(take(own, place ^ m, 0).astype(BF16), "rows", m << bit).astype(F32)
        own = total
    return own.reshape(own.shape[-2:])


def joined(pieces, *after):
    sizes = [piece.shape[0] for piece in pieces]

    def kernel(*refs):
        first = 0
        for ref, size in zip(refs, sizes):
            refs[-1][first : first + size] = ref[...].astype(BF16)
            first += size

    return pl.pallas_call(
        kernel,
        in_specs=[pl.BlockSpec(memory_space=pltpu.VMEM)] * len(pieces) + [pl.BlockSpec(memory_space=pl.ANY)] * len(after),
        out_specs=pl.BlockSpec(memory_space=pltpu.VMEM),
        out_shape=jax.ShapeDtypeStruct((sum(sizes),) + pieces[0].shape[1:], BF16),
    )(*pieces, *after)


def owners(batch_mask, core_mask, line):
    mine, batch = lax.axis_index("rows"), lax.axis_index("batch")
    chip = (batch ^ batch_mask) * (lax.axis_size("rows") // 2) + ((mine >> 1) ^ line)
    return chip * 2 + ((mine & 1) ^ core_mask)


class Gather:
    def along_line(self, shard):
        blocks = [shard[None]]
        for bit, size in row_groups():
            block = jnp.concatenate(blocks, axis=0)
            blocks = [block] + [swap(block, "rows", m << bit) for m in range(1, size)]
        return blocks

    def near(self, block):
        self.block = block
        return swap(block, "batch", 1), swap(block, "batch", 2)

    def far(self, from_x, from_y):
        self.from_x, self.from_y = from_x, from_y
        half = from_x.shape[0] // 2
        return swap(from_x[:half], "batch", 2), swap(from_y[half:], "batch", 1)

    def pieces(self, far_low, far_high):
        got = []
        half = far_low.shape[0]
        parts = ((self.block, 0, 0), (self.from_x, 1, 0), (self.from_y, 2, 0), (far_low, 3, 0), (far_high, 3, half))
        for piece, mask, first in parts:
            place = first + jnp.arange(piece.shape[0], dtype=jnp.int32)
            for array, core in ((piece, 0), (swap(piece, "rows", 1), 1)):
                got.append((array, owners(mask, core, place)))
        return got


def in_order(*values):
    return lax.optimization_barrier(values)


class Assembly:
    def __init__(self, pieces, first, size):
        self.first, self.size = first, size
        owner = jnp.concatenate([owner for _, owner in pieces]).astype(jnp.int32)
        self.ins = [smem(owner * size)] + [whole(array) for array, _ in pieces]
        self.count = len(self.ins)

    def run(self, refs, held):
        starts, k = refs[0], 0
        for ref in refs[1:]:
            for j in range(ref.shape[0]):
                rows = pl.ds(pl.multiple_of(starts[k], self.size), self.size)
                held[rows, :] = ref[j, self.first : self.first + self.size, :]
                k += 1


def assemble_kernel(assembly, *refs):
    assembly.run(refs[:-1], refs[-1])


class Spread:
    def __init__(self, width, *rows):
        mine, batch = lax.axis_index("rows"), lax.axis_index("batch")
        line = lax.axis_size("rows") // 2
        self.chips = 4 * line
        self.sizes = [r // (2 * self.chips) for r in rows]
        self.direct = not any(size % 16 for size in self.sizes)
        chip = jnp.arange(self.chips, dtype=jnp.int32)
        far = (chip // line) ^ batch
        near = (chip % line) ^ (mine >> 1)
        half = line // 2
        place = ((near // half) * 4 + (far ^ (far >> 1))) * half + near % half
        self.ins = [smem(place.astype(jnp.int32)), smem((mine & 1).astype(jnp.int32).reshape(1))]
        shapes = [(r, width) for r in rows]
        if self.direct:
            shapes = [(self.chips, sum(self.sizes), width)] * 2
        self.outs = [constant(shape, BF16) for shape in shapes]

    def emit(self, weight, product, base, rows, place_ref, core_ref, outs):
        if not self.direct:
            outs[weight][pl.ds(base, rows), :] = product[0:rows, :].astype(BF16)
            return
        core = core_ref[0]
        size, low = self.sizes[weight], sum(self.sizes[:weight])
        pair = 2 * size
        first = base // pair
        for k in range(rows // pair):
            to = place_ref[first + k]
            for ref, c in ((outs[0], 1 - core), (outs[1], core)):
                start = pl.multiple_of(k * pair + c * size, 16)
                ref[to, low : low + size, :] = product[pl.ds(start, size), :].astype(BF16)


class Sums:
    def __init__(self, spread, outs):
        self.direct = spread.direct
        if not self.direct:
            parts = [part.reshape(2 * spread.chips, size, -1) for part, size in zip(outs, spread.sizes)]
            self.total = scatter_sums(jnp.concatenate(parts, axis=1).reshape(-1, outs[0].shape[-1]))
            return
        shape = (2, 4, lax.axis_size("rows") // 4) + outs[0].shape[1:]
        self.keep = outs[1].reshape(shape)
        self.got = swap(outs[0], "rows", 1).reshape(shape)

    def part(self, half, index):
        return self.keep[half, index].astype(F32) + self.got[half, index].astype(F32)

    def send_far(self):
        return self.part(0, slice(1, 3)).astype(BF16), self.part(1, slice(2, 4)).astype(BF16)

    def take_far(self, sends):
        self.far = swap(sends[0], "batch", 1), swap(sends[1], "batch", 2)

    def send_near(self):
        from_x, from_y = self.far
        return (
            (self.part(1, 1) + from_y[0].astype(F32)).astype(BF16),
            (self.part(0, 3) + from_x[1].astype(F32)).astype(BF16),
        )

    def take_near(self, sends):
        self.near = swap(sends[0], "batch", 1), swap(sends[1], "batch", 2)

    def send_line(self):
        low = self.part(0, 0) + self.far[0][0].astype(F32) + self.near[1].astype(F32)
        high = self.part(1, 0) + self.far[1][1].astype(F32) + self.near[0].astype(F32)
        return jnp.concatenate([low, high], axis=0)

    def take_line(self, own):
        self.parts = []
        for bit, size in reversed(row_groups()):
            if self.parts:
                own = sum(part.astype(F32) for part in self.parts)
            own = own.reshape((size, -1) + own.shape[1:])
            self.parts = [own[0]] + [swap(own[m].astype(BF16), "rows", m << bit) for m in range(1, size)]

    def finish(self):
        if self.direct:
            own = sum(part.astype(F32) for part in self.parts)
            self.total = own.reshape(own.shape[-2:])
        return self.total


CHUNK = 16
PAD = 8
NN, NT, TN = (1, 0), (1, 1), (0, 0)


def dot(left, right, dims):
    return lax.dot_general(left, right, ((dims[:1], dims[1:]), ((), ())), preferred_element_type=F32)


def softplus(z):
    e = jnp.exp(-jnp.abs(z))
    return jnp.maximum(z, 0.0) + jnp.where(e < 1e-3, e * (1.0 - 0.5 * e), jnp.log(1.0 + e))


def sigmoid(z):
    return 0.5 * jnp.tanh(0.5 * z) + 0.5


def wide(mask, width):
    return jnp.concatenate([mask] * (width // mask.shape[-1]), axis=-1)


def fold(v):
    return v[:8] + v[8:]


def down(v):
    return jnp.sum(v, axis=0, keepdims=True)


def loop(rows, body, init, unroll=2):
    def step(i, carry):
        return body(pl.ds(pl.multiple_of(i * CHUNK, CHUNK), CHUNK), carry)

    return lax.fori_loop(0, rows // CHUNK, step, init, unroll=unroll)


def zeros8(width, count=2):
    return tuple(jnp.zeros((8, width), F32) for _ in range(count))


def norm_stats(sums_ref, inv, gain):
    mean = sums_ref[0, 0:1, :] * inv
    rstd = lax.rsqrt(sums_ref[0, 1:2, :] * inv - mean * mean + EPS_NORM)
    return mean, rstd, gain * rstd


def call(kernel, grid, ins, outs, scratch=(), flops=0, nbytes=0, vmem=48):
    got = pl.pallas_call(
        kernel,
        grid=grid,
        in_specs=[spec for _, spec in ins],
        out_specs=[spec for _, spec in outs],
        out_shape=[shape for shape, _ in outs],
        scratch_shapes=list(scratch),
        compiler_params=pltpu.CompilerParams(
            dimension_semantics=("arbitrary",) * len(grid), vmem_limit_bytes=vmem * 1024 * 1024
        ),
        cost_estimate=pl.CostEstimate(flops=flops, bytes_accessed=nbytes, transcendentals=0),
    )(*[array for array, _ in ins])
    return got[0] if len(outs) == 1 else got


def block(shape, index, **kw):
    return pl.BlockSpec(shape, index, **kw)


def listed(got):
    return list(got) if isinstance(got, (list, tuple)) else [got]


def whole(array):
    zeros = (0,) * len(array.shape)
    return (array, pl.BlockSpec(array.shape, lambda *_: zeros, pipeline_mode=pl.Buffered(1)))


def smem(array):
    return (array, pl.BlockSpec(memory_space=pltpu.SMEM))


def anywhere(array):
    return (array, pl.BlockSpec(memory_space=pl.ANY))


def constant(shape, dtype):
    spec = pl.BlockSpec(shape, lambda *_: (0,) * len(shape), pipeline_mode=pl.Buffered(1))
    return (jax.ShapeDtypeStruct(shape, dtype), spec)


def out(shape, dtype, spec_shape, index):
    return (jax.ShapeDtypeStruct(shape, dtype), pl.BlockSpec(spec_shape, index))


def gram_kernel(task_ref, mask_ref, out_ref):
    lanes = mask_ref.shape[-1]
    chan = task_ref.shape[-1]

    @pl.when(pl.program_id(0) == 0)
    def _():
        out_ref[...] = jnp.zeros_like(out_ref)

    def step(rows, carry):
        sums = [jnp.zeros((CHUNK, lanes), F32)] * 6
        for col in range(chan // lanes):
            cols = pl.ds(col * lanes, lanes)
            t = [task_ref[k, 0, 0, 0, rows, cols].astype(F32) for k in range(3)]
            pairs = [t[i] * t[j] for i in range(3) for j in range(i, 3)]
            sums = [s + p for s, p in zip(sums, pairs)]
        mask = mask_ref[0, 0, rows, :]
        return tuple(c + fold(s * mask) for c, s in zip(carry, sums))

    got = loop(task_ref.shape[4], step, zeros8(lanes, 6), unroll=1)
    for k in range(6):
        out_ref[k : k + 1, :] += down(got[k])


def first_kernel(assembly, x_ref, mask_ref, gram_ref, *refs):
    pieces, (wide_ref, low_ref, sums_ref, w_ref) = refs[: assembly.count], refs[assembly.count :]
    width = w_ref.shape[1]

    @pl.when(pl.program_id(0) == 0)
    def _():
        assembly.run(pieces, w_ref)

    wide_ref[0] = dot(x_ref[0], w_ref[...], NN)

    def step(rows, carry):
        v = wide_ref[0, rows, :]
        low_ref[0, rows, :] = v.astype(BF16)
        kept = v * wide(mask_ref[0, 0, rows, :], width)
        return carry[0] + fold(kept), carry[1] + fold(kept * v)

    got = loop(x_ref.shape[1], step, zeros8(width))
    sums_ref[0] = jnp.zeros_like(sums_ref[0])
    sums_ref[0, 0:1, :] = down(got[0])
    sums_ref[0, 1:2, :] = down(got[1])
    for k in range(6):
        lane = (k % 4) * 128
        sums_ref[0, 2 + k // 4 : 3 + k // 4, lane : lane + 128] = gram_ref[0, k : k + 1, :]


def upstream_kernel(sums_ref, task_ref, mask_ref, *refs):
    out_ref, coeff_ref = refs[-2:]
    lanes = mask_ref.shape[-1]

    @pl.when((pl.program_id(0) == 0) & (pl.program_id(1) == 0))
    def _():
        def entry(k):
            lane, row = (k % 4) * 128, 2 + k // 4
            both = sums_ref[0, row : row + 1, lane : lane + 128] + sums_ref[1, row : row + 1, lane : lane + 128]
            return jnp.sum(both, axis=1, keepdims=True)

        place = {}
        k = 0
        for i in range(3):
            for j in range(i, 3):
                place[i, j] = place[j, i] = entry(k)
                k += 1
        trace = place[0, 0] + place[1, 1] + place[2, 2]
        ymat = [[place[i, j] / trace for j in range(3)] for i in range(3)]
        zmat = [[jnp.full((1, 1), 1.0 if i == j else 0.0, F32) for j in range(3)] for i in range(3)]

        def mul(a, b):
            return [
                [a[i][0] * b[0][j] + a[i][1] * b[1][j] + a[i][2] * b[2][j] for j in range(3)]
                for i in range(3)
            ]

        for _ in range(NEWTON):
            zy = mul(zmat, ymat)
            pmat = [[(1.5 if i == j else 0.0) - 0.5 * zy[i][j] for j in range(3)] for i in range(3)]
            ymat = mul(ymat, pmat)
            zmat = mul(pmat, zmat)
        for i in range(3):
            value = (zmat[i][0] + zmat[i][1] + zmat[i][2]) / jnp.sqrt(F32(3.0))
            coeff_ref[i] = jnp.broadcast_to(value, (8, lanes))

    def step(rows, carry):
        mask = mask_ref[0, 0, rows, :]
        c = [jnp.concatenate([coeff_ref[i]] * (CHUNK // 8), axis=0) * mask for i in range(3)]
        for col in range(task_ref.shape[-1] // lanes):
            cols = pl.ds(col * lanes, lanes)
            t = [task_ref[k, 0, 0, 0, rows, cols].astype(F32) for k in range(3)]
            out_ref[0, rows, cols] = c[0] * t[0] + c[1] * t[1] + c[2] * t[2]
        return carry

    loop(task_ref.shape[4], step, 0, unroll=1)


def shifted_sum(parts, row, start, rows, sign):
    at = PAD + start
    low, high = at + sign * DILATION_SIZE, at - sign * DILATION_SIZE
    return (
        parts[1, row, at : at + rows, :]
        + parts[0, row, low : low + rows, :]
        + parts[2, row, high : high + rows, :]
    )


def clear_pads(ref):
    edge = ref.shape[-2]
    zero = jnp.zeros(ref.shape[:-2] + (PAD, ref.shape[-1]), ref.dtype)
    ref[..., 0:PAD, :] = zero
    ref[..., edge - PAD : edge, :] = zero


def second_kernel(
    assembly, inv_ref, sums_ref, param_ref, own_ref, up_ref, down_ref, mask_ref, *refs
):
    h_ref, wide_ref, low_ref, out_ref, cat_ref, part_ref, w_ref = refs[-7:]
    micro = pl.program_id(0)
    width = own_ref.shape[-1]
    pixels = own_ref.shape[1]
    columns = part_ref.shape[2] - 2 * PAD

    @pl.when(micro == 0)
    def _():
        assembly.run(refs[: assembly.count], w_ref)
        clear_pads(part_ref)

    mean, rstd, scale = norm_stats(sums_ref, inv_ref[micro], param_ref[0:1, :])
    offset = param_ref[1:2, :] - mean * scale
    for k, ref in enumerate((up_ref, own_ref, down_ref)):
        def step(rows, carry):
            z = ref[0, rows, :].astype(F32) * scale + offset
            h = (softplus(z) * wide(mask_ref[k, 0, rows, :], width)).astype(BF16)
            h_ref[k, 0, rows, :] = h
            cat_ref[rows, k * width : (k + 1) * width] = h
            return carry

        loop(pixels, step, 0)

    for tx in range(3):
        taps = [w_ref[(3 * ty + tx) * width : (3 * ty + tx + 1) * width, :] for ty in range(3)]
        product = dot(cat_ref[...], jnp.concatenate(taps, axis=0), NN)
        part_ref[tx, :, PAD : PAD + columns, :] = product.reshape(-1, columns, width)

    def row_step(row, carry):
        for start in range(0, columns, CHUNK):
            rows = pl.ds(pl.multiple_of(row * columns + start, CHUNK), CHUNK)
            v = shifted_sum(part_ref, row, start, CHUNK, -1)
            wide_ref[0, rows, :] = v
            low_ref[0, rows, :] = v.astype(BF16)
            kept = v * wide(mask_ref[1, 0, rows, :], width)
            carry = carry[0] + fold(kept), carry[1] + fold(kept * v)
        return carry

    got = lax.fori_loop(0, pixels // columns, row_step, zeros8(width))
    out_ref[0, 0:1, :] = down(got[0])
    out_ref[0, 1:2, :] = down(got[1])


def third_kernel(inv_ref, sums_ref, param_ref, a_ref, mask_ref, w_ref, h_ref, wide_ref, out_ref):
    micro = pl.program_id(0)
    width = a_ref.shape[-1]
    tile = 512
    mean, rstd, scale = norm_stats(sums_ref, inv_ref[micro], param_ref[0:1, :])
    offset = param_ref[1:2, :] - mean * scale

    def step(rows, carry):
        z = a_ref[0, rows, :] * scale + offset
        h_ref[0, rows, :] = (softplus(z) * wide(mask_ref[0, 0, rows, :], width)).astype(BF16)
        return carry

    loop(a_ref.shape[1], step, 0)
    for col in range(0, w_ref.shape[0], tile):
        cols = pl.ds(col, tile)
        wide_ref[0, :, cols] = dot(h_ref[0], w_ref[cols, :], NT)

        def sum_step(rows, carry):
            v = wide_ref[0, rows, cols]
            kept = v * wide(mask_ref[0, 0, rows, :], tile)
            return carry[0] + fold(kept), carry[1] + fold(kept * v)

        got = loop(a_ref.shape[1], sum_step, zeros8(tile))
        out_ref[0, 0:1, cols] = down(got[0])
        out_ref[0, 1:2, cols] = down(got[1])


def peak_kernel(
    inv_ref, sums_ref, param_ref, a_ref, x_ref, up_ref, mask_ref, block_ref, du_ref, out_ref
):
    width = a_ref.shape[-1]
    mean, rstd, scale = norm_stats(sums_ref, inv_ref[pl.program_id(0)], param_ref[0:1, :])
    shift = param_ref[1:2, :]

    def step(rows, carry):
        centred = a_ref[0, rows, :] - mean
        u = centred * scale + (shift + x_ref[0, rows, :].astype(F32))
        mask = wide(mask_ref[0, 0, rows, :], width)
        block_ref[0, rows, :] = (softplus(u) * mask).astype(BF16)
        du = up_ref[0, rows, :] * sigmoid(u)
        du_ref[0, rows, :] = du
        return carry[0] + fold(du), carry[1] + fold(du * centred)

    got = loop(a_ref.shape[1], step, zeros8(width))
    out_ref[0, 0:1, :] = down(got[0])
    out_ref[0, 1:2, :] = down(got[1]) * rstd


def lower_consts(stats_ref, grads_ref, inv, gain):
    mean, rstd, scale = norm_stats(stats_ref, inv, gain)
    return mean, scale, grads_ref[0, 0:1, :] * inv, grads_ref[0, 1:2, :] * inv * rstd


def back_third_kernel(
    inv_ref, stats3_ref, grads3_ref, stats2_ref, param3_ref, param2_ref,
    a3_ref, du_ref, a2_ref, mask_ref, w_ref,
    d_ref, wide_ref, low_ref, out_ref,
):
    inv = inv_ref[pl.program_id(0)]
    tile = 512
    for col in range(0, a3_ref.shape[2], tile):
        cols = pl.ds(col, tile)
        mean = stats3_ref[0, 0:1, cols] * inv
        rstd = lax.rsqrt(stats3_ref[0, 1:2, cols] * inv - mean * mean + EPS_NORM)
        scale = param3_ref[0:1, cols] * rstd
        base = grads3_ref[0, 0:1, cols] * inv
        slope = grads3_ref[0, 1:2, cols] * inv * rstd

        def step(rows, carry):
            d = du_ref[0, rows, cols] - (base + (a3_ref[0, rows, cols] - mean) * slope)
            d_ref[0, rows, cols] = (d * scale * wide(mask_ref[0, 0, rows, :], tile)).astype(BF16)
            return carry

        loop(a3_ref.shape[1], step, 0)
    wide_ref[0] = dot(d_ref[0], w_ref[...], NN)
    width = w_ref.shape[1]
    mean, rstd, scale = norm_stats(stats2_ref, inv, param2_ref[0:1, :])
    shift = param2_ref[1:2, :]

    def last(rows, carry):
        centred = a2_ref[0, rows, :] - mean
        gate = sigmoid(centred * scale + shift) * wide(mask_ref[0, 0, rows, :], width)
        dz = wide_ref[0, rows, :] * gate
        wide_ref[0, rows, :] = dz
        low_ref[0, rows, :] = dz.astype(BF16)
        return carry[0] + fold(dz), carry[1] + fold(dz * centred)

    got = loop(a2_ref.shape[1], last, zeros8(width))
    out_ref[0, 0:1, :] = down(got[0])
    out_ref[0, 1:2, :] = down(got[1]) * rstd


def lower_second_kernel(
    inv_ref, stats2_ref, grads2_ref, param2_ref,
    a2_ref, a2_up_ref, a2_down_ref, dz_ref, dz_up_ref, dz_down_ref, mask_ref, cat_ref, shift_ref, pad_ref,
):
    inv = inv_ref[pl.program_id(0)]
    pixels, width = a2_ref.shape[1:]
    columns = pad_ref.shape[1] - 2 * PAD

    @pl.when(pl.program_id(0) == 0)
    def _():
        clear_pads(pad_ref)

    mean, scale, base, slope = lower_consts(stats2_ref, grads2_ref, inv, param2_ref[0:1, :])

    def lowered(k, a, dz, rows):
        d = dz.astype(F32) - (base + (a.astype(F32) - mean) * slope)
        return d * scale * wide(mask_ref[k, 0, rows, :], width)

    for k, a_ref, d_ref, place in ((0, a2_up_ref, dz_up_ref, 2), (2, a2_down_ref, dz_down_ref, 0)):
        def step(rows, carry):
            d = lowered(k, a_ref[0, rows, :], d_ref[0, rows, :], rows)
            cat_ref[0, rows, place * width : (place + 1) * width] = d.astype(BF16)
            return carry

        loop(pixels, step, 0)

    def own_step(row, carry):
        for start in range(0, columns, CHUNK):
            rows = pl.ds(pl.multiple_of(row * columns + start, CHUNK), CHUNK)
            d = lowered(1, a2_ref[0, rows, :], dz_ref[0, rows, :], rows)
            low = d.astype(BF16)
            cat_ref[0, rows, width : 2 * width] = low
            shift_ref[0, rows, width : 2 * width] = low
            pad_ref[row, PAD + start : PAD + start + CHUNK, :] = d
        for start in range(0, columns, CHUNK):
            rows = pl.ds(pl.multiple_of(row * columns + start, CHUNK), CHUNK)
            for tx in (-1, 1):
                at = PAD + start - tx * DILATION_SIZE
                moved = pad_ref[row, at : at + CHUNK, :].astype(BF16)
                shift_ref[0, rows, (tx + 1) * width : (tx + 2) * width] = moved
        return carry

    lax.fori_loop(0, pixels // columns, own_step, 0)


def back_second_kernel(
    assembly, inv_ref, stats1_ref, param1_ref, cat_ref, a1_ref, mask_ref, *refs
):
    wide_ref, out_ref, part_ref, w_ref = refs[-4:]
    inv = inv_ref[pl.program_id(0)]
    pixels, width = a1_ref.shape[1:]
    columns = part_ref.shape[2] - 2 * PAD

    @pl.when(pl.program_id(0) == 0)
    def _():
        assembly.run(refs[: assembly.count], w_ref)
        clear_pads(part_ref)

    for tx in range(3):
        taps = [w_ref[(3 * ty + tx) * width : (3 * ty + tx + 1) * width, :] for ty in range(3)]
        product = dot(cat_ref[0], jnp.concatenate(taps, axis=1), NT)
        part_ref[tx, :, PAD : PAD + columns, :] = product.reshape(-1, columns, width)

    mean1, rstd1, scale1 = norm_stats(stats1_ref, inv, param1_ref[0:1, :])
    shift1 = param1_ref[1:2, :]

    def row_step(row, carry):
        for start in range(0, columns, CHUNK):
            rows = pl.ds(pl.multiple_of(row * columns + start, CHUNK), CHUNK)
            centred = a1_ref[0, rows, :] - mean1
            gate = sigmoid(centred * scale1 + shift1) * wide(mask_ref[0, 0, rows, :], width)
            dz = shifted_sum(part_ref, row, start, CHUNK, 1) * gate
            wide_ref[0, rows, :] = dz
            carry = carry[0] + fold(dz), carry[1] + fold(dz * centred)
        return carry

    got = lax.fori_loop(0, pixels // columns, row_step, zeros8(width))
    out_ref[0, 0:1, :] = down(got[0])
    out_ref[0, 1:2, :] = down(got[1]) * rstd1


def grads_kernel(spread, h_ref, d_ref, d3_ref, h2_ref, place_ref, core_ref, *refs):
    outs, product = refs[:-1], refs[-1]
    width = h_ref.shape[-1]
    step = pl.program_id(0)

    @pl.when(step < 3)
    def _():
        for tx in range(3):
            rows = pl.ds(pl.multiple_of((3 * step + tx) * width, width), width)
            product[rows, :] = dot(h_ref[0], d_ref[:, tx * width : (tx + 1) * width], TN).astype(BF16)

    @pl.when(step == 2)
    def _():
        spread.emit(0, product, 0, product.shape[0], place_ref, core_ref, outs)

    @pl.when(step >= 3)
    def _():
        rows = d3_ref.shape[1]
        product[0:rows, :] = dot(d3_ref[...], h2_ref[...], TN).astype(BF16)
        spread.emit(1, product, pl.multiple_of((step - 3) * rows, rows), rows, place_ref, core_ref, outs)


def first_back_kernel(
    spread, inv_ref, stats_ref, grads_ref, param_ref, dz_ref, a_ref, mask_ref, x_ref, place_ref, core_ref, *refs
):
    d_ref, outs, product = refs[0], refs[1:-1], refs[-1]
    pixels, width = dz_ref.shape[1:]

    @pl.when(pl.program_id(0) == 0)
    def _():
        for micro in range(dz_ref.shape[0]):
            inv = inv_ref[micro]
            mean, scale, base, slope = lower_consts(
                stats_ref.at[micro : micro + 1], grads_ref.at[micro : micro + 1], inv, param_ref[0:1, :]
            )

            def step(rows, carry):
                d = dz_ref[micro, rows, :] - (base + (a_ref[micro, rows, :] - mean) * slope)
                d = d * scale * wide(mask_ref[0, micro, rows, :], width)
                d_ref[micro, rows, :] = d.astype(BF16)
                return carry

            loop(pixels, step, 0)

    product[...] = dot(x_ref[...], d_ref[...].reshape(-1, width), TN)
    rows = product.shape[0]
    spread.emit(0, product, pl.multiple_of(pl.program_id(0) * rows, rows), rows, place_ref, core_ref, outs)


def input_grad_kernel(d_ref, w_ref, du_ref, out_ref):
    out_ref[...] = (dot(d_ref[...], w_ref[...], NT) + du_ref[...]).astype(BF16)


def adamw(weight, first, second, grad, rate, decay):
    new_first = BETA_ONE * first + (1.0 - BETA_ONE) * grad
    new_second = BETA_TWO * second + (1.0 - BETA_TWO) * grad * grad
    first_hat = new_first / (1.0 - BETA_ONE**STEP)
    second_hat = new_second / (1.0 - BETA_TWO**STEP)
    new_weight = weight - rate * (first_hat / (jnp.sqrt(second_hat) + ADAM_EPS) + decay * weight)
    return (new_weight, new_first, new_second)


def neighbours(x):
    count = lax.axis_size("rows")
    above = lax.ppermute(x, "rows", [(i, i + 1) for i in range(count - 1)])
    below = lax.ppermute(x, "rows", [(i + 1, i) for i in range(count - 1)])
    return above, below


def per_device(
    features, task_grads, row_counts, col_counts,
    weight_in, weight_mid, weight_out,
    first_in, first_mid, first_out,
    second_in, second_mid, second_out,
    norm_params, norm_first, norm_second,
):
    micros, _, row_span, columns, chan = features.shape
    inner = weight_in.shape[1]
    pixels = row_span * columns
    total_pixels = micros * pixels
    batch = lax.axis_index("batch")
    own_rows = lax.dynamic_index_in_dim(row_counts, batch, 1, keepdims=False)
    own_cols = lax.dynamic_index_in_dim(col_counts, batch, 1, keepdims=False)
    base = lax.axis_index("rows") * row_span + jnp.arange(-1, 2, dtype=jnp.int32) * row_span
    row_ids = base[:, None] + jnp.arange(row_span, dtype=jnp.int32)
    col_ids = jnp.arange(columns, dtype=jnp.int32)
    in_rows = (row_ids[:, None] >= 0) & (row_ids[:, None] < own_rows[None, :, None])
    in_cols = col_ids < own_cols[:, None]
    masks = (in_rows[:, :, :, None] & in_cols[None, :, None, :]).astype(F32)
    masks = jnp.broadcast_to(masks.reshape(3, micros, pixels, 1), (3, micros, pixels, 128))
    inverse = 1.0 / jnp.sum(row_counts * col_counts, axis=1).astype(F32)

    grams = []
    for micro in range(micros):
        grams.append(call(
            gram_kernel, (row_span,),
            [
                (task_grads, block((3, 1, 1, 1, columns, chan), functools.partial(lambda m, r: (0, m, 0, r, 0, 0), micro))),
                (masks, block((1, 1, columns, 128), functools.partial(lambda m, r: (1, m, r, 0), micro))),
            ],
            [out((8, 128), F32, (8, 128), lambda r: (0, 0))],
            flops=6 * total_pixels * chan, nbytes=3 * total_pixels * chan, vmem=10,
        ))
    x = features.reshape(micros, pixels, chan)
    params = [norm_params[:, :inner], norm_params[:, inner : 2 * inner], norm_params[:, 2 * inner :]]

    def per_micro(array):
        return (array, block((1,) + array.shape[1:], lambda m, *_: (m,) + (0,) * (len(array.shape) - 1)))

    def out_micro(width, dtype, rows=pixels):
        return out((micros, rows, width), dtype, (1, rows, width), lambda m: (m, 0, 0))

    own_mask = (masks, block((1, 1, pixels, 128), lambda m, *_: (1, m, 0, 0)))
    all_masks = (masks, block((3, 1, pixels, 128), lambda m: (0, m, 0, 0)))
    row_mask = (masks, block((1, 1, columns, 128), lambda m, r: (1, m, r, 0)))
    task_rows = (
        task_grads, block((3, 1, 1, 1, columns, chan), lambda m, r: (0, m, 0, r, 0, 0))
    )
    big = total_pixels * chan
    small = total_pixels * inner
    part_rows = weight_in.shape[0]
    mid_rows = weight_mid.shape[0]
    low_mid = weight_mid.astype(BF16)
    both = jnp.concatenate([weight_in.astype(BF16), weight_out.T.astype(BF16)], axis=0)
    direct = part_rows % 16 == 0 and mid_rows % 16 == 0
    zero = jnp.zeros(1, jnp.int32)
    if direct:
        gather_both, gather_mid = Gather(), Gather()
        line_both = gather_both.along_line(both)
        near_both, low_mid = in_order(joined(line_both, *grams), low_mid)
        from_both = gather_both.near(near_both)
        line_mid = gather_mid.along_line(low_mid)
        far_both = gather_both.far(*from_both)
        pieces = gather_both.pieces(*far_both)
        line_mid = in_order(*line_mid, *far_both)[: len(line_mid)]
        near_mid, *arrays = in_order(joined(line_mid), *[array for array, _ in pieces])
        from_mid = gather_mid.near(near_mid)
        pieces = [(array, owner) for array, (_, owner) in zip(arrays, pieces)]
        ins_in, ins_out = [Assembly(pieces, k * part_rows, part_rows) for k in range(2)]
    else:
        full = gather_shards(both).reshape(-1, 2, part_rows, inner)
        ins_in, ins_out = [Assembly([(full[:, k].reshape(1, -1, inner), zero)], 0, chan) for k in range(2)]
        ins_mid = Assembly([(gather_shards(low_mid).reshape(1, -1, inner), zero)], 0, 9 * inner)
    whole_weight = constant((chan, inner), BF16)
    a_one, a_one_low, part, w_in = call(
        functools.partial(first_kernel, ins_in), (micros,),
        [per_micro(x), own_mask, per_micro(jnp.stack(grams)), *ins_in.ins],
        [out_micro(inner, F32), out_micro(inner, BF16), out_micro(inner, F32, 4), whole_weight],
        flops=2 * big * inner, nbytes=2 * big + 8 * small, vmem=18,
    )
    a_one_up, a_one_down = neighbours(a_one_low)
    core_one = group_sum(part, "rows", 0, 2)
    if direct:
        core_one, *from_mid = in_order(core_one, *from_mid)
    chip_one = group_sum(core_one, "batch", 0, lax.axis_size("batch"))
    chip_one, a_one_up, a_one_down = in_order(chip_one, a_one_up, a_one_down)
    if direct:
        chip_one, *from_mid = in_order(chip_one, *from_mid)
        far_mid = gather_mid.far(*from_mid)
    stats_one = line_sums(chip_one)
    upstream = call(
        upstream_kernel, (micros, row_span),
        [whole(stats_one), task_rows, row_mask],
        [out((micros, pixels, chan), F32, (1, columns, chan), lambda m, r: (m, r, 0))],
        [pltpu.VMEM((3, 8, 128), F32)],
        flops=8 * big, nbytes=10 * big, vmem=10,
    )
    if direct:
        upstream, *far_mid = in_order(upstream, *far_mid)
        ins_mid = Assembly(gather_mid.pieces(*far_mid), 0, mid_rows)
    padded = (3, row_span, columns + 2 * PAD, inner)
    held = pltpu.VMEM((9 * inner, inner), BF16)
    taps = [pltpu.VMEM((pixels, 3 * inner), BF16), pltpu.VMEM(padded, F32), held]
    h_one, a_two, a_two_low, part = call(
        functools.partial(second_kernel, ins_mid), (micros,),
        [
            smem(inverse), per_micro(stats_one), whole(params[0]), per_micro(a_one),
            per_micro(a_one_up), per_micro(a_one_down), all_masks,
            *ins_mid.ins, anywhere(upstream),
        ],
        [
            out((3, micros, pixels, inner), BF16, (3, 1, pixels, inner), lambda m: (0, m, 0, 0)),
            out_micro(inner, F32), out_micro(inner, BF16), out_micro(inner, F32, 2),
        ],
        taps,
        flops=18 * small * inner, nbytes=20 * small + 18 * inner * inner, vmem=32,
    )
    w_out = call(
        functools.partial(assemble_kernel, ins_out), (1,), ins_out.ins, [whole_weight], nbytes=8 * chan * inner, vmem=16
    )
    stats_two = all_sum(part)
    h_two, a_three, part = call(
        third_kernel, (micros,),
        [
            smem(inverse), per_micro(stats_two), whole(params[1]), per_micro(a_two), own_mask,
            whole(w_out),
        ],
        [out_micro(inner, BF16), out_micro(chan, F32), out_micro(chan, F32, 2)],
        flops=2 * big * inner, nbytes=4 * big + 8 * small, vmem=20,
    )
    stats_three = all_sum(part)
    stats_three, a_two_low = in_order(stats_three, a_two_low)
    a_two_up, a_two_down = neighbours(a_two_low)
    tile = 512

    def tiled(array):
        return (array, block((1, array.shape[1], tile), lambda m, c: (m, 0, c)))

    def out_tiled(dtype, rows=pixels):
        return out((micros, rows, chan), dtype, (1, rows, tile), lambda m, c: (m, 0, c))

    block_out, d_resid, part = call(
        peak_kernel, (micros, chan // tile),
        [
            smem(inverse), tiled(stats_three), (params[2], block((2, tile), lambda m, c: (0, c))),
            tiled(a_three), tiled(x), tiled(upstream), own_mask,
        ],
        [out_tiled(BF16), out_tiled(F32), out_tiled(F32, 2)],
        flops=40 * big, nbytes=16 * big, vmem=14,
    )
    part, a_two_up, a_two_down = in_order(part, a_two_up, a_two_down)
    grads_three = all_sum(part)
    d_three, dz_two, dz_two_low, part = call(
        back_third_kernel, (micros,),
        [
            smem(inverse), per_micro(stats_three), per_micro(grads_three), per_micro(stats_two),
            whole(params[2]), whole(params[1]), per_micro(a_three), per_micro(d_resid),
            per_micro(a_two), own_mask, whole(w_out),
        ],
        [out_micro(chan, BF16), out_micro(inner, F32), out_micro(inner, BF16), out_micro(inner, F32, 2)],
        flops=2 * big * inner, nbytes=10 * big, vmem=26,
    )
    dz_two_up, dz_two_down = neighbours(dz_two_low)
    grads_two = all_sum(part)
    d_two_cat, d_two = call(
        lower_second_kernel, (micros,),
        [
            smem(inverse), per_micro(stats_two), per_micro(grads_two), whole(params[1]),
            per_micro(a_two), per_micro(a_two_up), per_micro(a_two_down),
            per_micro(dz_two), per_micro(dz_two_up), per_micro(dz_two_down), all_masks,
        ],
        [out_micro(3 * inner, BF16), out_micro(3 * inner, BF16)],
        [pltpu.VMEM(padded[1:], F32)],
        flops=60 * small, nbytes=28 * small, vmem=20,
    )
    spread = Spread(inner, 9 * inner, chan)
    grads = call(
        functools.partial(grads_kernel, spread), (3 + chan // tile,),
        [
            (
                h_one.reshape(3, total_pixels, inner),
                block((1, total_pixels, inner), lambda t: (jnp.minimum(t, 2), 0, 0)),
            ),
            whole(d_two.reshape(total_pixels, 3 * inner)),
            (
                d_three.reshape(total_pixels, chan),
                block((total_pixels, tile), lambda t: (0, jnp.maximum(t - 3, 0))),
            ),
            whole(h_two.reshape(total_pixels, inner)), *spread.ins,
        ],
        spread.outs, [pltpu.VMEM((9 * inner, inner), BF16)],
        flops=18 * small * inner + 2 * big * inner, nbytes=12 * small + 18 * inner * inner, vmem=30,
    )
    sums = Sums(spread, grads)
    dz_one, part = call(
        functools.partial(back_second_kernel, ins_mid), (micros,),
        [
            smem(inverse), per_micro(stats_one), whole(params[0]), per_micro(d_two_cat),
            per_micro(a_one), own_mask, *ins_mid.ins, anywhere(grads[0]),
        ],
        [out_micro(inner, F32), out_micro(inner, F32, 2)],
        [pltpu.VMEM(padded, F32), held],
        flops=18 * small * inner, nbytes=30 * small + 18 * inner * inner, vmem=26,
    )
    chip_one = chip_sums(part)
    if sums.direct:
        chip_one, *sends = in_order(chip_one, *sums.send_far())
        sums.take_far(sends)
    grads_one = line_sums(chip_one)
    spread_in = Spread(inner, chan)
    d_one, *grad_in = call(
        functools.partial(first_back_kernel, spread_in), (chan // tile,),
        [
            smem(inverse), whole(stats_one), whole(grads_one), whole(params[0]), whole(dz_one), whole(a_one),
            (masks, block((1, micros, pixels, 128), lambda c: (1, 0, 0, 0))),
            (x.reshape(total_pixels, chan), block((total_pixels, tile), lambda c: (0, c))),
            *spread_in.ins,
        ],
        [out((micros, pixels, inner), BF16, (micros, pixels, inner), lambda c: (0, 0, 0)), *spread_in.outs],
        [pltpu.VMEM((tile, inner), F32)],
        flops=2 * big * inner, nbytes=4 * big, vmem=20,
    )
    if sums.direct:
        d_one, *rest = in_order(d_one, *grad_in, *sums.far)
        grad_in, sums.far = rest[:2], rest[2:]
    sums_in = Sums(spread_in, grad_in)
    if sums.direct:
        d_one, *sends = in_order(d_one, *sums.send_near())
        sums.take_near(sends)
    strip = total_pixels // 4
    input_grad = call(
        input_grad_kernel, (4,),
        [
            (d_one.reshape(total_pixels, inner), block((strip, inner), lambda s: (s, 0))),
            whole(w_in),
            (d_resid.reshape(total_pixels, chan), block((strip, chan), lambda s: (s, 0))),
        ],
        [out((total_pixels, chan), BF16, (strip, chan), lambda s: (s, 0))],
        flops=2 * big * inner, nbytes=8 * big, vmem=16,
    )
    if sums.direct:
        input_grad, *sums.near = in_order(input_grad, *sums.near)
        line, *sends = in_order(sums.send_line(), *sums_in.send_far())
        sums.take_line(line)
        sums_in.take_far(sends)
        sums.parts[1], *sums_in.far = in_order(sums.parts[1], *sums_in.far)
        sums_in.take_near(sums_in.send_near())
        sums_in.take_line(sums_in.send_line())
    grad_in, grad_both = sums_in.finish(), sums.finish()
    grad_mid, grad_out = grad_both[: weight_mid.shape[0]], grad_both[weight_mid.shape[0] :]

    norm_total = jnp.concatenate([grads_one[:, :2], grads_two, grads_three], axis=2)
    norm_total = jnp.sum(norm_total, axis=0)[::-1]
    squares = jnp.sum(grad_in * grad_in, axis=0) + jnp.sum(grad_both * grad_both, axis=0)
    squares = all_sum(squares.reshape(-1, 128))
    total = jnp.sum(squares).reshape(1, 1) + jnp.sum(norm_total * norm_total)
    grad_norm = jnp.sqrt(total)
    scale = CLIP / jnp.maximum(grad_norm, CLIP)
    new_in = adamw(weight_in, first_in, second_in, grad_in * scale, RATE, DECAY)
    new_mid = adamw(weight_mid, first_mid, second_mid, grad_mid * scale, RATE, DECAY)
    new_out = adamw(weight_out, first_out, second_out, (grad_out * scale).T, RATE, DECAY)
    new_norm = adamw(norm_params, norm_first, norm_second, norm_total * scale, RATE_NORM, 0.0)
    shape = (micros, 1, row_span, columns, chan)
    return (
        block_out.reshape(shape),
        input_grad.reshape(shape),
        *[group[k] for k in range(3) for group in (new_in, new_mid, new_out)],
        *new_norm,
        grad_norm.reshape(1),
    )


def solution(mesh):
    acts = P(None, "batch", "rows", None, None)
    by_row, by_col = P(("batch", "rows"), None), P(None, ("batch", "rows"))
    weights = (by_row, by_row, by_col)
    return jax.shard_map(
        per_device,
        mesh=mesh,
        in_specs=(
            acts, P(None, None, "batch", "rows", None, None), P(), P(), *(weights * 3), P(), P(), P()
        ),
        out_specs=(acts, acts, *(weights * 3), P(), P(), P(), P()),
        check_vma=False,
    )
```

```python
import functools

import jax
import jax.numpy as jnp
import numpy as np
from jax import lax
from jax.experimental import pallas as pl
from jax.experimental.pallas import tpu as pltpu
from jax.sharding import PartitionSpec as P

DILATION_SIZE = 4
NEWTON = 6
STEP = 10

EPS_NORM = 1e-05
CLIP = 1.0
RATE = 0.02
RATE_NORM = 0.3
BETA_ONE = 0.9
BETA_TWO = 0.999
ADAM_EPS = 1e-08
DECAY = 0.01

F32 = jnp.float32
BF16 = jnp.bfloat16


def swap(x, axis, mask):
    return lax.ppermute(x, axis, [(i, i ^ mask) for i in range(lax.axis_size(axis))])


def row_groups():
    groups = []
    bit, rest = 1, lax.axis_size("rows") // 2
    while rest > 1:
        size = min(4, rest)
        groups.append((bit, size))
        bit += size.bit_length() - 1
        rest //= size
    return groups


def group_sum(x, axis, shift, size):
    got = [x] + [swap(x, axis, m << shift) for m in range(1, size)]
    if size == 2:
        return got[0] + got[1]
    return (got[0] + got[1]) + (got[2] + got[3])


def chip_sums(x):
    return group_sum(group_sum(x, "rows", 0, 2), "batch", 0, lax.axis_size("batch"))


def all_sum(x):
    return line_sums(chip_sums(x))


def line_sums(x):
    for bit, size in row_groups():
        x = group_sum(x, "rows", bit, size)
    return x


def put(buf, piece, index, axis):
    return lax.dynamic_update_slice_in_dim(buf, jnp.expand_dims(piece, axis), index, axis)


def take(buf, index, axis):
    return lax.dynamic_index_in_dim(buf, index, axis, keepdims=False)


def gather_shards(shard):
    mine = lax.axis_index("rows")
    core = mine & 1
    batch = lax.axis_index("batch")
    block = shard[None]
    for bit, size in row_groups():
        place = (mine >> bit) & (size - 1)
        got = [block] + [swap(block, "rows", m << bit) for m in range(1, size)]
        buf = jnp.zeros((size,) + block.shape, block.dtype)
        for m, piece in enumerate(got):
            buf = put(buf, piece, place ^ m, 0)
        block = buf.reshape((-1,) + block.shape[1:])
    half = block.shape[0] // 2
    from_x = swap(block, "batch", 1)
    from_y = swap(block, "batch", 2)
    far_low = swap(from_x[:half], "batch", 2)
    far_high = swap(from_y[half:], "batch", 1)
    far = jnp.concatenate([far_low, far_high], axis=0)
    full = jnp.zeros((4, block.shape[0], 2) + block.shape[1:], block.dtype)
    for m, piece in enumerate((block, from_x, from_y, far)):
        other = swap(piece, "rows", 1)
        for value, where in ((piece, core), (other, 1 - core)):
            full = lax.dynamic_update_slice(
                full, value[None, :, None], (batch ^ m, 0, where, 0, 0)
            )
    return full


def scatter_sums(grad):
    mine = lax.axis_index("rows")
    core = mine & 1
    batch = lax.axis_index("batch")
    count = lax.axis_size("rows")
    grad = grad.reshape(4, count // 2, 2, -1, grad.shape[-1])
    got = swap(take(grad, 1 - core, 2).astype(BF16), "rows", 1)
    part = take(grad, core, 2).astype(F32) + got.astype(F32)
    half = part.shape[1] // 2
    own, to_x, to_y, far = [take(part, batch ^ m, 0) for m in range(4)]
    low = swap(far[:half].astype(BF16), "batch", 1).astype(F32)
    high = swap(far[half:].astype(BF16), "batch", 2).astype(F32)
    to_x = jnp.concatenate([to_x[:half], to_x[half:] + high], axis=0)
    to_y = jnp.concatenate([to_y[:half] + low, to_y[half:]], axis=0)
    from_x = swap(to_x.astype(BF16), "batch", 1)
    from_y = swap(to_y.astype(BF16), "batch", 2)
    own = own + from_x.astype(F32) + from_y.astype(F32)
    for bit, size in reversed(row_groups()):
        place = (mine >> bit) & (size - 1)
        own = own.reshape((size, -1) + own.shape[1:])
        total = take(own, place, 0)
        for m in range(1, size):
            total = total + swap(take(own, place ^ m, 0).astype(BF16), "rows", m << bit).astype(F32)
        own = total
    return own.reshape(own.shape[-2:])


def joined(pieces, *after):
    sizes = [piece.shape[0] for piece in pieces]

    def kernel(*refs):
        first = 0
        for ref, size in zip(refs, sizes):
            refs[-1][first : first + size] = ref[...].astype(BF16)
            first += size

    return pl.pallas_call(
        kernel,
        in_specs=[pl.BlockSpec(memory_space=pltpu.VMEM)] * len(pieces) + [pl.BlockSpec(memory_space=pl.ANY)] * len(after),
        out_specs=pl.BlockSpec(memory_space=pltpu.VMEM),
        out_shape=jax.ShapeDtypeStruct((sum(sizes),) + pieces[0].shape[1:], BF16),
    )(*pieces, *after)


def owners(table):
    mine, batch = lax.axis_index("rows"), lax.axis_index("batch")
    far, near, core = np.array(table, np.int32).T
    return ((batch ^ far) * (lax.axis_size("rows") // 2) + ((mine >> 1) ^ near)) * 2 + ((mine & 1) ^ core)


class Gather:
    def along_line(self, shard):
        blocks = [shard[None]]
        for bit, size in row_groups():
            block = jnp.concatenate(blocks, axis=0)
            blocks = [block] + [swap(block, "rows", m << bit) for m in range(1, size)]
        return blocks

    def near(self, block):
        self.block = block
        return swap(block, "batch", 1), swap(block, "batch", 2)

    def far(self, from_x, from_y):
        self.from_x, self.from_y = from_x, from_y
        half = from_x.shape[0] // 2
        return swap(from_x[:half], "batch", 2), swap(from_y[half:], "batch", 1)

    def pieces(self, far_low, far_high):
        got, table = [], []
        half = far_low.shape[0]
        parts = ((self.block, 0, 0), (self.from_x, 1, 0), (self.from_y, 2, 0), (far_low, 3, 0), (far_high, 3, half))
        for piece, mask, first in parts:
            for array, core in ((piece, 0), (swap(piece, "rows", 1), 1)):
                got.append(array)
                table += [(mask, first + j, core) for j in range(piece.shape[0])]
        return got, table


def in_order(*values):
    return lax.optimization_barrier(values)


class Assembly:
    def __init__(self, arrays, table, first, size):
        self.first, self.size = first, size
        starts = owners(table) * size if table else jnp.zeros(1, jnp.int32)
        self.ins = [smem(starts)] + [whole(array) for array in arrays]
        self.count = len(self.ins)

    def run(self, refs, held):
        starts, k = refs[0], 0
        for ref in refs[1:]:
            for j in range(ref.shape[0]):
                rows = pl.ds(pl.multiple_of(starts[k], self.size), self.size)
                held[rows, :] = ref[j, self.first : self.first + self.size, :]
                k += 1


def assemble_kernel(assembly, *refs):
    assembly.run(refs[:-1], refs[-1])


class Spread:
    def __init__(self, width, *rows):
        mine, batch = lax.axis_index("rows"), lax.axis_index("batch")
        line = lax.axis_size("rows") // 2
        self.chips = 4 * line
        self.sizes = [r // (2 * self.chips) for r in rows]
        self.direct = not any(size % 16 for size in self.sizes)
        chip = jnp.arange(self.chips, dtype=jnp.int32)
        far = (chip // line) ^ batch
        near = (chip % line) ^ (mine >> 1)
        half = line // 2
        place = ((near // half) * 4 + (far ^ (far >> 1))) * half + near % half
        self.ins = [smem(place.astype(jnp.int32)), smem((mine & 1).astype(jnp.int32).reshape(1))]
        shapes = [(r, width) for r in rows]
        if self.direct:
            shapes = [(self.chips, sum(self.sizes), width)] * 2
        self.outs = [constant(shape, BF16) for shape in shapes]

    def emit(self, weight, product, base, rows, place_ref, core_ref, outs):
        if not self.direct:
            outs[weight][pl.ds(base, rows), :] = product[0:rows, :].astype(BF16)
            return
        core = core_ref[0]
        size, low = self.sizes[weight], sum(self.sizes[:weight])
        pair = 2 * size
        first = base // pair
        for k in range(rows // pair):
            to = place_ref[first + k]
            for ref, c in ((outs[0], 1 - core), (outs[1], core)):
                start = pl.multiple_of(k * pair + c * size, 16)
                ref[to, low : low + size, :] = product[pl.ds(start, size), :].astype(BF16)


class Sums:
    def __init__(self, spread, outs):
        self.direct = spread.direct
        if not self.direct:
            parts = [part.reshape(2 * spread.chips, size, -1) for part, size in zip(outs, spread.sizes)]
            self.total = scatter_sums(jnp.concatenate(parts, axis=1).reshape(-1, outs[0].shape[-1]))
            return
        shape = (2, 4, lax.axis_size("rows") // 4) + outs[0].shape[1:]
        self.keep = outs[1].reshape(shape)
        self.got = swap(outs[0], "rows", 1).reshape(shape)

    def part(self, half, index):
        return self.keep[half, index].astype(F32) + self.got[half, index].astype(F32)

    def send_far(self):
        return self.part(0, slice(1, 3)).astype(BF16), self.part(1, slice(2, 4)).astype(BF16)

    def take_far(self, sends):
        self.far = swap(sends[0], "batch", 1), swap(sends[1], "batch", 2)

    def send_near(self):
        from_x, from_y = self.far
        return (
            (self.part(1, 1) + from_y[0].astype(F32)).astype(BF16),
            (self.part(0, 3) + from_x[1].astype(F32)).astype(BF16),
        )

    def take_near(self, sends):
        self.near = swap(sends[0], "batch", 1), swap(sends[1], "batch", 2)

    def send_line(self):
        low = self.part(0, 0) + self.far[0][0].astype(F32) + self.near[1].astype(F32)
        high = self.part(1, 0) + self.far[1][1].astype(F32) + self.near[0].astype(F32)
        return jnp.concatenate([low, high], axis=0)

    def take_line(self, own):
        self.parts = []
        for bit, size in reversed(row_groups()):
            if self.parts:
                own = sum(part.astype(F32) for part in self.parts)
            own = own.reshape((size, -1) + own.shape[1:])
            self.parts = [own[0]] + [swap(own[m].astype(BF16), "rows", m << bit) for m in range(1, size)]

    def finish(self):
        if self.direct:
            own = sum(part.astype(F32) for part in self.parts)
            self.total = own.reshape(own.shape[-2:])
        return self.total


CHUNK = 16
PAD = 8
NN, NT, TN = (1, 0), (1, 1), (0, 0)


def dot(left, right, dims):
    return lax.dot_general(left, right, ((dims[:1], dims[1:]), ((), ())), preferred_element_type=F32)


def softplus(z):
    e = jnp.exp(-jnp.abs(z))
    return jnp.maximum(z, 0.0) + jnp.where(e < 1e-3, e * (1.0 - 0.5 * e), jnp.log(1.0 + e))


def sigmoid(z):
    return 0.5 * jnp.tanh(0.5 * z) + 0.5


def wide(mask, width):
    return jnp.concatenate([mask] * (width // mask.shape[-1]), axis=-1)


def fold(v):
    return v[:8] + v[8:]


def down(v):
    return jnp.sum(v, axis=0, keepdims=True)


def loop(rows, body, init, unroll=2):
    def step(i, carry):
        return body(pl.ds(pl.multiple_of(i * CHUNK, CHUNK), CHUNK), carry)

    return lax.fori_loop(0, rows // CHUNK, step, init, unroll=unroll)


def zeros8(width, count=2):
    return tuple(jnp.zeros((8, width), F32) for _ in range(count))


def norm_stats(sums_ref, inv, gain):
    mean = sums_ref[0, 0:1, :] * inv
    rstd = lax.rsqrt(sums_ref[0, 1:2, :] * inv - mean * mean + EPS_NORM)
    return mean, rstd, gain * rstd


def call(kernel, grid, ins, outs, scratch=(), flops=0, nbytes=0, vmem=48):
    got = pl.pallas_call(
        kernel,
        grid=grid,
        in_specs=[spec for _, spec in ins],
        out_specs=[spec for _, spec in outs],
        out_shape=[shape for shape, _ in outs],
        scratch_shapes=list(scratch),
        compiler_params=pltpu.CompilerParams(
            dimension_semantics=("arbitrary",) * len(grid), vmem_limit_bytes=vmem * 1024 * 1024
        ),
        cost_estimate=pl.CostEstimate(flops=flops, bytes_accessed=nbytes, transcendentals=0),
    )(*[array for array, _ in ins])
    return got[0] if len(outs) == 1 else got


def block(shape, index, **kw):
    return pl.BlockSpec(shape, index, **kw)


def listed(got):
    return list(got) if isinstance(got, (list, tuple)) else [got]


def whole(array):
    zeros = (0,) * len(array.shape)
    return (array, pl.BlockSpec(array.shape, lambda *_: zeros, pipeline_mode=pl.Buffered(1)))


def smem(array):
    return (array, pl.BlockSpec(memory_space=pltpu.SMEM))


def anywhere(array):
    return (array, pl.BlockSpec(memory_space=pl.ANY))


def constant(shape, dtype):
    spec = pl.BlockSpec(shape, lambda *_: (0,) * len(shape), pipeline_mode=pl.Buffered(1))
    return (jax.ShapeDtypeStruct(shape, dtype), spec)


def out(shape, dtype, spec_shape, index):
    return (jax.ShapeDtypeStruct(shape, dtype), pl.BlockSpec(spec_shape, index))


def gram_kernel(task_ref, mask_ref, out_ref):
    lanes = mask_ref.shape[-1]
    chan = task_ref.shape[-1]

    @pl.when(pl.program_id(0) == 0)
    def _():
        out_ref[...] = jnp.zeros_like(out_ref)

    def step(rows, carry):
        sums = [jnp.zeros((CHUNK, lanes), F32)] * 6
        for col in range(chan // lanes):
            cols = pl.ds(col * lanes, lanes)
            t = [task_ref[k, 0, 0, 0, rows, cols].astype(F32) for k in range(3)]
            pairs = [t[i] * t[j] for i in range(3) for j in range(i, 3)]
            sums = [s + p for s, p in zip(sums, pairs)]
        mask = mask_ref[0, 0, rows, :]
        return tuple(c + fold(s * mask) for c, s in zip(carry, sums))

    got = loop(task_ref.shape[4], step, zeros8(lanes, 6), unroll=1)
    for k in range(6):
        out_ref[k : k + 1, :] += down(got[k])


def first_kernel(assembly, x_ref, mask_ref, gram_ref, *refs):
    pieces, (wide_ref, low_ref, sums_ref, w_ref) = refs[: assembly.count], refs[assembly.count :]
    width = w_ref.shape[1]

    @pl.when(pl.program_id(0) == 0)
    def _():
        assembly.run(pieces, w_ref)

    wide_ref[0] = dot(x_ref[0], w_ref[...], NN)

    def step(rows, carry):
        v = wide_ref[0, rows, :]
        low_ref[0, rows, :] = v.astype(BF16)
        kept = v * wide(mask_ref[0, 0, rows, :], width)
        return carry[0] + fold(kept), carry[1] + fold(kept * v)

    got = loop(x_ref.shape[1], step, zeros8(width))
    sums_ref[0] = jnp.zeros_like(sums_ref[0])
    sums_ref[0, 0:1, :] = down(got[0])
    sums_ref[0, 1:2, :] = down(got[1])
    for k in range(6):
        lane = (k % 4) * 128
        sums_ref[0, 2 + k // 4 : 3 + k // 4, lane : lane + 128] = gram_ref[0, k : k + 1, :]


def upstream_kernel(sums_ref, task_ref, mask_ref, *refs):
    out_ref, coeff_ref = refs[-2:]
    lanes = mask_ref.shape[-1]

    @pl.when((pl.program_id(0) == 0) & (pl.program_id(1) == 0))
    def _():
        def entry(k):
            lane, row = (k % 4) * 128, 2 + k // 4
            both = sums_ref[0, row : row + 1, lane : lane + 128] + sums_ref[1, row : row + 1, lane : lane + 128]
            return jnp.sum(both, axis=1, keepdims=True)

        place = {}
        k = 0
        for i in range(3):
            for j in range(i, 3):
                place[i, j] = place[j, i] = entry(k)
                k += 1
        trace = place[0, 0] + place[1, 1] + place[2, 2]
        ymat = [[place[i, j] / trace for j in range(3)] for i in range(3)]
        zmat = [[jnp.full((1, 1), 1.0 if i == j else 0.0, F32) for j in range(3)] for i in range(3)]

        def mul(a, b):
            return [
                [a[i][0] * b[0][j] + a[i][1] * b[1][j] + a[i][2] * b[2][j] for j in range(3)]
                for i in range(3)
            ]

        for _ in range(NEWTON):
            zy = mul(zmat, ymat)
            pmat = [[(1.5 if i == j else 0.0) - 0.5 * zy[i][j] for j in range(3)] for i in range(3)]
            ymat = mul(ymat, pmat)
            zmat = mul(pmat, zmat)
        for i in range(3):
            value = (zmat[i][0] + zmat[i][1] + zmat[i][2]) / jnp.sqrt(F32(3.0))
            coeff_ref[i] = jnp.broadcast_to(value, (8, lanes))

    def step(rows, carry):
        mask = mask_ref[0, 0, rows, :]
        c = [jnp.concatenate([coeff_ref[i]] * (CHUNK // 8), axis=0) * mask for i in range(3)]
        for col in range(task_ref.shape[-1] // lanes):
            cols = pl.ds(col * lanes, lanes)
            t = [task_ref[k, 0, 0, 0, rows, cols].astype(F32) for k in range(3)]
            out_ref[0, rows, cols] = (c[0] * t[0] + c[1] * t[1] + c[2] * t[2]).astype(BF16)
        return carry

    loop(task_ref.shape[4], step, 0, unroll=1)


def shifted_sum(parts, row, start, rows, sign):
    at = PAD + start
    low, high = at + sign * DILATION_SIZE, at - sign * DILATION_SIZE
    return (
        parts[1, row, at : at + rows, :]
        + parts[0, row, low : low + rows, :]
        + parts[2, row, high : high + rows, :]
    )


def clear_pads(ref):
    edge = ref.shape[-2]
    zero = jnp.zeros(ref.shape[:-2] + (PAD, ref.shape[-1]), ref.dtype)
    ref[..., 0:PAD, :] = zero
    ref[..., edge - PAD : edge, :] = zero


def second_kernel(
    assembly, inv_ref, sums_ref, param_ref, own_ref, up_ref, down_ref, mask_ref, *refs
):
    h_ref, wide_ref, low_ref, out_ref, cat_ref, part_ref, w_ref = refs[-7:]
    micro = pl.program_id(0)
    width = own_ref.shape[-1]
    pixels = own_ref.shape[1]
    columns = part_ref.shape[2] - 2 * PAD

    @pl.when(micro == 0)
    def _():
        assembly.run(refs[: assembly.count], w_ref)
        clear_pads(part_ref)

    mean, rstd, scale = norm_stats(sums_ref, inv_ref[micro], param_ref[0:1, :])
    offset = param_ref[1:2, :] - mean * scale
    for k, ref in enumerate((up_ref, own_ref, down_ref)):
        def step(rows, carry):
            z = ref[0, rows, :].astype(F32) * scale + offset
            h = (softplus(z) * wide(mask_ref[k, 0, rows, :], width)).astype(BF16)
            h_ref[k, 0, rows, :] = h
            cat_ref[rows, k * width : (k + 1) * width] = h
            return carry

        loop(pixels, step, 0)

    for tx in range(3):
        taps = [w_ref[(3 * ty + tx) * width : (3 * ty + tx + 1) * width, :] for ty in range(3)]
        product = dot(cat_ref[...], jnp.concatenate(taps, axis=0), NN)
        part_ref[tx, :, PAD : PAD + columns, :] = product.reshape(-1, columns, width)

    def row_step(row, carry):
        for start in range(0, columns, CHUNK):
            rows = pl.ds(pl.multiple_of(row * columns + start, CHUNK), CHUNK)
            v = shifted_sum(part_ref, row, start, CHUNK, -1)
            wide_ref[0, rows, :] = v
            low_ref[0, rows, :] = v.astype(BF16)
            kept = v * wide(mask_ref[1, 0, rows, :], width)
            carry = carry[0] + fold(kept), carry[1] + fold(kept * v)
        return carry

    got = lax.fori_loop(0, pixels // columns, row_step, zeros8(width))
    out_ref[0, 0:1, :] = down(got[0])
    out_ref[0, 1:2, :] = down(got[1])


def third_kernel(inv_ref, sums_ref, param_ref, a_ref, mask_ref, w_ref, h_ref, wide_ref, out_ref):
    micro = pl.program_id(0)
    width = a_ref.shape[-1]
    tile = 512
    mean, rstd, scale = norm_stats(sums_ref, inv_ref[micro], param_ref[0:1, :])
    offset = param_ref[1:2, :] - mean * scale

    def step(rows, carry):
        z = a_ref[0, rows, :] * scale + offset
        h_ref[0, rows, :] = (softplus(z) * wide(mask_ref[0, 0, rows, :], width)).astype(BF16)
        return carry

    loop(a_ref.shape[1], step, 0)
    for col in range(0, w_ref.shape[0], tile):
        cols = pl.ds(col, tile)
        wide_ref[0, :, cols] = dot(h_ref[0], w_ref[cols, :], NT)

        def sum_step(rows, carry):
            v = wide_ref[0, rows, cols]
            kept = v * wide(mask_ref[0, 0, rows, :], tile)
            return carry[0] + fold(kept), carry[1] + fold(kept * v)

        got = loop(a_ref.shape[1], sum_step, zeros8(tile))
        out_ref[0, 0:1, cols] = down(got[0])
        out_ref[0, 1:2, cols] = down(got[1])


def peak_kernel(
    inv_ref, sums_ref, param_ref, a_ref, x_ref, up_ref, mask_ref, block_ref, du_ref, out_ref
):
    width = a_ref.shape[-1]
    mean, rstd, scale = norm_stats(sums_ref, inv_ref[pl.program_id(0)], param_ref[0:1, :])
    shift = param_ref[1:2, :]

    def step(rows, carry):
        centred = a_ref[0, rows, :] - mean
        u = centred * scale + (shift + x_ref[0, rows, :].astype(F32))
        mask = wide(mask_ref[0, 0, rows, :], width)
        block_ref[0, rows, :] = (softplus(u) * mask).astype(BF16)
        du = up_ref[0, rows, :].astype(F32) * sigmoid(u)
        du_ref[0, rows, :] = du.astype(BF16)
        return carry[0] + fold(du), carry[1] + fold(du * centred)

    got = loop(a_ref.shape[1], step, zeros8(width))
    out_ref[0, 0:1, :] = down(got[0])
    out_ref[0, 1:2, :] = down(got[1]) * rstd


def lower_consts(stats_ref, grads_ref, inv, gain):
    mean, rstd, scale = norm_stats(stats_ref, inv, gain)
    return mean, scale, grads_ref[0, 0:1, :] * inv, grads_ref[0, 1:2, :] * inv * rstd


def back_third_kernel(
    inv_ref, stats3_ref, grads3_ref, stats2_ref, param3_ref, param2_ref,
    a3_ref, du_ref, a2_ref, mask_ref, w_ref,
    d_ref, wide_ref, low_ref, out_ref,
):
    inv = inv_ref[pl.program_id(0)]
    tile = 512
    for col in range(0, a3_ref.shape[2], tile):
        cols = pl.ds(col, tile)
        mean = stats3_ref[0, 0:1, cols] * inv
        rstd = lax.rsqrt(stats3_ref[0, 1:2, cols] * inv - mean * mean + EPS_NORM)
        scale = param3_ref[0:1, cols] * rstd
        base = grads3_ref[0, 0:1, cols] * inv
        slope = grads3_ref[0, 1:2, cols] * inv * rstd

        def step(rows, carry):
            d = du_ref[0, rows, cols].astype(F32) - (base + (a3_ref[0, rows, cols] - mean) * slope)
            d_ref[0, rows, cols] = (d * scale * wide(mask_ref[0, 0, rows, :], tile)).astype(BF16)
            return carry

        loop(a3_ref.shape[1], step, 0)
    wide_ref[0] = dot(d_ref[0], w_ref[...], NN)
    width = w_ref.shape[1]
    mean, rstd, scale = norm_stats(stats2_ref, inv, param2_ref[0:1, :])
    shift = param2_ref[1:2, :]

    def last(rows, carry):
        centred = a2_ref[0, rows, :] - mean
        gate = sigmoid(centred * scale + shift) * wide(mask_ref[0, 0, rows, :], width)
        dz = wide_ref[0, rows, :] * gate
        wide_ref[0, rows, :] = dz
        low_ref[0, rows, :] = dz.astype(BF16)
        return carry[0] + fold(dz), carry[1] + fold(dz * centred)

    got = loop(a2_ref.shape[1], last, zeros8(width))
    out_ref[0, 0:1, :] = down(got[0])
    out_ref[0, 1:2, :] = down(got[1]) * rstd


def lower_second_kernel(
    inv_ref, stats2_ref, grads2_ref, param2_ref,
    a2_ref, a2_up_ref, a2_down_ref, dz_ref, dz_up_ref, dz_down_ref, mask_ref, cat_ref, shift_ref, pad_ref,
):
    inv = inv_ref[pl.program_id(0)]
    pixels, width = a2_ref.shape[1:]
    columns = pad_ref.shape[1] - 2 * PAD

    @pl.when(pl.program_id(0) == 0)
    def _():
        clear_pads(pad_ref)

    mean, scale, base, slope = lower_consts(stats2_ref, grads2_ref, inv, param2_ref[0:1, :])

    def lowered(k, a, dz, rows):
        d = dz.astype(F32) - (base + (a.astype(F32) - mean) * slope)
        return d * scale * wide(mask_ref[k, 0, rows, :], width)

    for k, a_ref, d_ref, place in ((0, a2_up_ref, dz_up_ref, 2), (2, a2_down_ref, dz_down_ref, 0)):
        def step(rows, carry):
            d = lowered(k, a_ref[0, rows, :], d_ref[0, rows, :], rows)
            cat_ref[0, rows, place * width : (place + 1) * width] = d.astype(BF16)
            return carry

        loop(pixels, step, 0)

    def own_step(row, carry):
        for start in range(0, columns, CHUNK):
            rows = pl.ds(pl.multiple_of(row * columns + start, CHUNK), CHUNK)
            d = lowered(1, a2_ref[0, rows, :], dz_ref[0, rows, :], rows)
            low = d.astype(BF16)
            cat_ref[0, rows, width : 2 * width] = low
            shift_ref[0, rows, width : 2 * width] = low
            pad_ref[row, PAD + start : PAD + start + CHUNK, :] = d
        for start in range(0, columns, CHUNK):
            rows = pl.ds(pl.multiple_of(row * columns + start, CHUNK), CHUNK)
            for tx in (-1, 1):
                at = PAD + start - tx * DILATION_SIZE
                moved = pad_ref[row, at : at + CHUNK, :].astype(BF16)
                shift_ref[0, rows, (tx + 1) * width : (tx + 2) * width] = moved
        return carry

    lax.fori_loop(0, pixels // columns, own_step, 0)


def back_second_kernel(
    assembly, inv_ref, stats1_ref, param1_ref, cat_ref, a1_ref, mask_ref, *refs
):
    wide_ref, out_ref, part_ref, w_ref = refs[-4:]
    inv = inv_ref[pl.program_id(0)]
    pixels, width = a1_ref.shape[1:]
    columns = part_ref.shape[2] - 2 * PAD

    @pl.when(pl.program_id(0) == 0)
    def _():
        assembly.run(refs[: assembly.count], w_ref)
        clear_pads(part_ref)

    for tx in range(3):
        taps = [w_ref[(3 * ty + tx) * width : (3 * ty + tx + 1) * width, :] for ty in range(3)]
        product = dot(cat_ref[0], jnp.concatenate(taps, axis=1), NT)
        part_ref[tx, :, PAD : PAD + columns, :] = product.reshape(-1, columns, width)

    mean1, rstd1, scale1 = norm_stats(stats1_ref, inv, param1_ref[0:1, :])
    shift1 = param1_ref[1:2, :]

    def row_step(row, carry):
        for start in range(0, columns, CHUNK):
            rows = pl.ds(pl.multiple_of(row * columns + start, CHUNK), CHUNK)
            centred = a1_ref[0, rows, :] - mean1
            gate = sigmoid(centred * scale1 + shift1) * wide(mask_ref[0, 0, rows, :], width)
            dz = shifted_sum(part_ref, row, start, CHUNK, 1) * gate
            wide_ref[0, rows, :] = dz
            carry = carry[0] + fold(dz), carry[1] + fold(dz * centred)
        return carry

    got = lax.fori_loop(0, pixels // columns, row_step, zeros8(width))
    out_ref[0, 0:1, :] = down(got[0])
    out_ref[0, 1:2, :] = down(got[1]) * rstd1


def grads_kernel(spread, h_ref, d_ref, d3_ref, h2_ref, place_ref, core_ref, *refs):
    outs, product = refs[:-1], refs[-1]
    width = h_ref.shape[-1]
    step = pl.program_id(0)

    @pl.when(step < 3)
    def _():
        for tx in range(3):
            rows = pl.ds(pl.multiple_of((3 * step + tx) * width, width), width)
            product[rows, :] = dot(h_ref[0], d_ref[:, tx * width : (tx + 1) * width], TN).astype(BF16)

    @pl.when(step == 2)
    def _():
        spread.emit(0, product, 0, product.shape[0], place_ref, core_ref, outs)

    @pl.when(step >= 3)
    def _():
        rows = d3_ref.shape[1]
        product[0:rows, :] = dot(d3_ref[...], h2_ref[...], TN).astype(BF16)
        spread.emit(1, product, pl.multiple_of((step - 3) * rows, rows), rows, place_ref, core_ref, outs)


def first_back_kernel(
    spread, inv_ref, stats_ref, grads_ref, param_ref, dz_ref, a_ref, mask_ref, x_ref, place_ref, core_ref, *refs
):
    d_ref, outs, product = refs[0], refs[1:-1], refs[-1]
    pixels, width = dz_ref.shape[1:]

    @pl.when(pl.program_id(0) == 0)
    def _():
        for micro in range(dz_ref.shape[0]):
            inv = inv_ref[micro]
            mean, scale, base, slope = lower_consts(
                stats_ref.at[micro : micro + 1], grads_ref.at[micro : micro + 1], inv, param_ref[0:1, :]
            )

            def step(rows, carry):
                d = dz_ref[micro, rows, :] - (base + (a_ref[micro, rows, :] - mean) * slope)
                d = d * scale * wide(mask_ref[0, micro, rows, :], width)
                d_ref[micro, rows, :] = d.astype(BF16)
                return carry

            loop(pixels, step, 0)

    product[...] = dot(x_ref[...], d_ref[...].reshape(-1, width), TN)
    rows = product.shape[0]
    spread.emit(0, product, pl.multiple_of(pl.program_id(0) * rows, rows), rows, place_ref, core_ref, outs)


def input_grad_kernel(d_ref, w_ref, du_ref, out_ref):
    out_ref[...] = (dot(d_ref[...], w_ref[...], NT) + du_ref[...].astype(F32)).astype(BF16)


def adamw(weight, first, second, grad, rate, decay):
    new_first = BETA_ONE * first + (1.0 - BETA_ONE) * grad
    new_second = BETA_TWO * second + (1.0 - BETA_TWO) * grad * grad
    first_hat = new_first / (1.0 - BETA_ONE**STEP)
    second_hat = new_second / (1.0 - BETA_TWO**STEP)
    new_weight = weight - rate * (first_hat / (jnp.sqrt(second_hat) + ADAM_EPS) + decay * weight)
    return (new_weight, new_first, new_second)


def neighbours(x):
    count = lax.axis_size("rows")
    above = lax.ppermute(x, "rows", [(i, i + 1) for i in range(count - 1)])
    below = lax.ppermute(x, "rows", [(i + 1, i) for i in range(count - 1)])
    return above, below


def per_device(
    features, task_grads, row_counts, col_counts,
    weight_in, weight_mid, weight_out,
    first_in, first_mid, first_out,
    second_in, second_mid, second_out,
    norm_params, norm_first, norm_second,
):
    micros, _, row_span, columns, chan = features.shape
    inner = weight_in.shape[1]
    pixels = row_span * columns
    total_pixels = micros * pixels
    batch = lax.axis_index("batch")
    own_rows = lax.dynamic_index_in_dim(row_counts, batch, 1, keepdims=False)
    own_cols = lax.dynamic_index_in_dim(col_counts, batch, 1, keepdims=False)
    base = lax.axis_index("rows") * row_span + jnp.arange(-1, 2, dtype=jnp.int32) * row_span
    row_ids = base[:, None] + jnp.arange(row_span, dtype=jnp.int32)
    col_ids = jnp.arange(columns, dtype=jnp.int32)
    in_rows = (row_ids[:, None] >= 0) & (row_ids[:, None] < own_rows[None, :, None])
    in_cols = col_ids < own_cols[:, None]
    masks = (in_rows[:, :, :, None] & in_cols[None, :, None, :]).astype(F32)
    masks = jnp.broadcast_to(masks.reshape(3, micros, pixels, 1), (3, micros, pixels, 128))
    inverse = 1.0 / jnp.sum(row_counts * col_counts, axis=1).astype(F32)

    grams = []
    for micro in range(micros):
        grams.append(call(
            gram_kernel, (row_span,),
            [
                (task_grads, block((3, 1, 1, 1, columns, chan), functools.partial(lambda m, r: (0, m, 0, r, 0, 0), micro))),
                (masks, block((1, 1, columns, 128), functools.partial(lambda m, r: (1, m, r, 0), micro))),
            ],
            [out((8, 128), F32, (8, 128), lambda r: (0, 0))],
            flops=6 * total_pixels * chan, nbytes=3 * total_pixels * chan, vmem=4,
        ))
    x = features.reshape(micros, pixels, chan)
    params = [norm_params[:, :inner], norm_params[:, inner : 2 * inner], norm_params[:, 2 * inner :]]

    def per_micro(array):
        return (array, block((1,) + array.shape[1:], lambda m, *_: (m,) + (0,) * (len(array.shape) - 1)))

    def out_micro(width, dtype, rows=pixels):
        return out((micros, rows, width), dtype, (1, rows, width), lambda m: (m, 0, 0))

    own_mask = (masks, block((1, 1, pixels, 128), lambda m, *_: (1, m, 0, 0)))
    all_masks = (masks, block((3, 1, pixels, 128), lambda m: (0, m, 0, 0)))
    row_mask = (masks, block((1, 1, columns, 128), lambda m, r: (1, m, r, 0)))
    task_rows = (
        task_grads, block((3, 1, 1, 1, columns, chan), lambda m, r: (0, m, 0, r, 0, 0))
    )
    big = total_pixels * chan
    small = total_pixels * inner
    part_rows = weight_in.shape[0]
    mid_rows = weight_mid.shape[0]
    low_mid = weight_mid.astype(BF16)
    both = jnp.concatenate([weight_in.astype(BF16), weight_out.T.astype(BF16)], axis=0)
    direct = part_rows % 16 == 0 and mid_rows % 16 == 0
    if direct:
        gather_both, gather_mid = Gather(), Gather()
        line_both = gather_both.along_line(both)
        near_both, low_mid = in_order(joined(line_both, *grams), low_mid)
        from_both = gather_both.near(near_both)
        line_mid = gather_mid.along_line(low_mid)
        far_both = gather_both.far(*from_both)
        arrays, table = gather_both.pieces(*far_both)
        line_mid = in_order(*line_mid, *far_both)[: len(line_mid)]
        near_mid, *arrays = in_order(joined(line_mid), *arrays)
        from_mid = gather_mid.near(near_mid)
        ins_in, ins_out = [Assembly(arrays, table, k * part_rows, part_rows) for k in range(2)]
    else:
        full = gather_shards(both).reshape(-1, 2, part_rows, inner)
        ins_in, ins_out = [Assembly([full[:, k].reshape(1, -1, inner)], (), 0, chan) for k in range(2)]
        ins_mid = Assembly([gather_shards(low_mid).reshape(1, -1, inner)], (), 0, 9 * inner)
    whole_weight = constant((chan, inner), BF16)
    a_one, a_one_low, part, w_in = call(
        functools.partial(first_kernel, ins_in), (micros,),
        [per_micro(x), own_mask, per_micro(jnp.stack(grams)), *ins_in.ins],
        [out_micro(inner, F32), out_micro(inner, BF16), out_micro(inner, F32, 4), whole_weight],
        flops=2 * big * inner, nbytes=2 * big + 8 * small, vmem=12,
    )
    a_one_up, a_one_down = neighbours(a_one_low)
    core_one = group_sum(part, "rows", 0, 2)
    if direct:
        core_one, *from_mid = in_order(core_one, *from_mid)
    chip_one = group_sum(core_one, "batch", 0, lax.axis_size("batch"))
    chip_one, a_one_up, a_one_down = in_order(chip_one, a_one_up, a_one_down)
    if direct:
        chip_one, *from_mid = in_order(chip_one, *from_mid)
        far_mid = gather_mid.far(*from_mid)
    stats_one = line_sums(chip_one)
    upstream = call(
        upstream_kernel, (micros, row_span),
        [whole(stats_one), task_rows, row_mask],
        [out((micros, pixels, chan), BF16, (1, columns, chan), lambda m, r: (m, r, 0))],
        [pltpu.VMEM((3, 8, 128), F32)],
        flops=8 * big, nbytes=10 * big, vmem=6,
    )
    if direct:
        upstream, *far_mid = in_order(upstream, *far_mid)
        ins_mid = Assembly(*gather_mid.pieces(*far_mid), 0, mid_rows)
    padded = (3, row_span, columns + 2 * PAD, inner)
    held = pltpu.VMEM((9 * inner, inner), BF16)
    taps = [pltpu.VMEM((pixels, 3 * inner), BF16), pltpu.VMEM(padded, F32), held]
    h_one, a_two, a_two_low, part = call(
        functools.partial(second_kernel, ins_mid), (micros,),
        [
            smem(inverse), per_micro(stats_one), whole(params[0]), per_micro(a_one),
            per_micro(a_one_up), per_micro(a_one_down), all_masks,
            *ins_mid.ins, anywhere(upstream),
        ],
        [
            out((3, micros, pixels, inner), BF16, (3, 1, pixels, inner), lambda m: (0, m, 0, 0)),
            out_micro(inner, F32), out_micro(inner, BF16), out_micro(inner, F32, 2),
        ],
        taps,
        flops=18 * small * inner, nbytes=20 * small + 18 * inner * inner, vmem=27,
    )
    w_out = call(
        functools.partial(assemble_kernel, ins_out), (1,), ins_out.ins, [whole_weight], nbytes=8 * chan * inner, vmem=9
    )
    stats_two = all_sum(part)
    h_two, a_three, part = call(
        third_kernel, (micros,),
        [
            smem(inverse), per_micro(stats_two), whole(params[1]), per_micro(a_two), own_mask,
            whole(w_out),
        ],
        [out_micro(inner, BF16), out_micro(chan, F32), out_micro(chan, F32, 2)],
        flops=2 * big * inner, nbytes=4 * big + 8 * small, vmem=13,
    )
    stats_three = all_sum(part)
    stats_three, a_two_low = in_order(stats_three, a_two_low)
    a_two_up, a_two_down = neighbours(a_two_low)
    tile = 512

    def tiled(array):
        return (array, block((1, array.shape[1], tile), lambda m, c: (m, 0, c)))

    def out_tiled(dtype, rows=pixels):
        return out((micros, rows, chan), dtype, (1, rows, tile), lambda m, c: (m, 0, c))

    block_out, d_resid, part = call(
        peak_kernel, (micros, chan // tile),
        [
            smem(inverse), tiled(stats_three), (params[2], block((2, tile), lambda m, c: (0, c))),
            tiled(a_three), tiled(x), tiled(upstream), own_mask,
        ],
        [out_tiled(BF16), out_tiled(BF16), out_tiled(F32, 2)],
        flops=40 * big, nbytes=16 * big, vmem=9,
    )
    part, a_two_up, a_two_down = in_order(part, a_two_up, a_two_down)
    grads_three = all_sum(part)
    d_three, dz_two, dz_two_low, part = call(
        back_third_kernel, (micros,),
        [
            smem(inverse), per_micro(stats_three), per_micro(grads_three), per_micro(stats_two),
            whole(params[2]), whole(params[1]), per_micro(a_three), per_micro(d_resid),
            per_micro(a_two), own_mask, whole(w_out),
        ],
        [out_micro(chan, BF16), out_micro(inner, F32), out_micro(inner, BF16), out_micro(inner, F32, 2)],
        flops=2 * big * inner, nbytes=10 * big, vmem=20,
    )
    dz_two_up, dz_two_down = neighbours(dz_two_low)
    grads_two = all_sum(part)
    d_two_cat, d_two = call(
        lower_second_kernel, (micros,),
        [
            smem(inverse), per_micro(stats_two), per_micro(grads_two), whole(params[1]),
            per_micro(a_two), per_micro(a_two_up), per_micro(a_two_down),
            per_micro(dz_two), per_micro(dz_two_up), per_micro(dz_two_down), all_masks,
        ],
        [out_micro(3 * inner, BF16), out_micro(3 * inner, BF16)],
        [pltpu.VMEM(padded[1:], F32)],
        flops=60 * small, nbytes=28 * small, vmem=16,
    )
    spread = Spread(inner, 9 * inner, chan)
    grads = call(
        functools.partial(grads_kernel, spread), (3 + chan // tile,),
        [
            (
                h_one.reshape(3, total_pixels, inner),
                block((1, total_pixels, inner), lambda t: (jnp.minimum(t, 2), 0, 0)),
            ),
            whole(d_two.reshape(total_pixels, 3 * inner)),
            (
                d_three.reshape(total_pixels, chan),
                block((total_pixels, tile), lambda t: (0, jnp.maximum(t - 3, 0))),
            ),
            whole(h_two.reshape(total_pixels, inner)), *spread.ins,
        ],
        spread.outs, [pltpu.VMEM((9 * inner, inner), BF16)],
        flops=18 * small * inner + 2 * big * inner, nbytes=12 * small + 18 * inner * inner, vmem=21,
    )
    sums = Sums(spread, grads)
    dz_one, part = call(
        functools.partial(back_second_kernel, ins_mid), (micros,),
        [
            smem(inverse), per_micro(stats_one), whole(params[0]), per_micro(d_two_cat),
            per_micro(a_one), own_mask, *ins_mid.ins, anywhere(grads[0]),
        ],
        [out_micro(inner, F32), out_micro(inner, F32, 2)],
        [pltpu.VMEM(padded, F32), held],
        flops=18 * small * inner, nbytes=30 * small + 18 * inner * inner, vmem=21,
    )
    chip_one = chip_sums(part)
    if sums.direct:
        chip_one, *sends = in_order(chip_one, *sums.send_far())
        sums.take_far(sends)
    grads_one = line_sums(chip_one)
    spread_in = Spread(inner, chan)
    d_one, *grad_in = call(
        functools.partial(first_back_kernel, spread_in), (chan // tile,),
        [
            smem(inverse), whole(stats_one), whole(grads_one), whole(params[0]), whole(dz_one), whole(a_one),
            (masks, block((1, micros, pixels, 128), lambda c: (1, 0, 0, 0))),
            (x.reshape(total_pixels, chan), block((total_pixels, tile), lambda c: (0, c))),
            *spread_in.ins,
        ],
        [out((micros, pixels, inner), BF16, (micros, pixels, inner), lambda c: (0, 0, 0)), *spread_in.outs],
        [pltpu.VMEM((tile, inner), F32)],
        flops=2 * big * inner, nbytes=4 * big, vmem=14,
    )
    if sums.direct:
        d_one, *rest = in_order(d_one, *grad_in, *sums.far)
        grad_in, sums.far = rest[:2], rest[2:]
    sums_in = Sums(spread_in, grad_in)
    if sums.direct:
        d_one, *sends = in_order(d_one, *sums.send_near())
        sums.take_near(sends)
    strip = total_pixels // 4
    input_grad = call(
        input_grad_kernel, (4,),
        [
            (d_one.reshape(total_pixels, inner), block((strip, inner), lambda s: (s, 0))),
            whole(w_in),
            (d_resid.reshape(total_pixels, chan), block((strip, chan), lambda s: (s, 0))),
        ],
        [out((total_pixels, chan), BF16, (strip, chan), lambda s: (s, 0))],
        flops=2 * big * inner, nbytes=8 * big, vmem=11,
    )
    if sums.direct:
        input_grad, *sums.near = in_order(input_grad, *sums.near)
        line, *sends = in_order(sums.send_line(), *sums_in.send_far())
        sums.take_line(line)
        sums_in.take_far(sends)
        sums.parts[1], sums.parts[2], *sums_in.far = in_order(*sums.parts[1:3], *sums_in.far)
        sums_in.take_near(sums_in.send_near())
        sums_in.take_line(sums_in.send_line())
    grad_in, grad_both = sums_in.finish(), sums.finish()
    grad_mid, grad_out = grad_both[: weight_mid.shape[0]], grad_both[weight_mid.shape[0] :]

    norm_total = jnp.concatenate([grads_one[:, :2], grads_two, grads_three], axis=2)
    norm_total = jnp.sum(norm_total, axis=0)[::-1]
    squares = jnp.sum(grad_in * grad_in, axis=0) + jnp.sum(grad_both * grad_both, axis=0)
    squares = all_sum(squares.reshape(-1, 128))
    total = jnp.sum(squares).reshape(1, 1) + jnp.sum(norm_total * norm_total)
    grad_norm = jnp.sqrt(total)
    scale = CLIP / jnp.maximum(grad_norm, CLIP)
    new_in = adamw(weight_in, first_in, second_in, grad_in * scale, RATE, DECAY)
    new_mid = adamw(weight_mid, first_mid, second_mid, grad_mid * scale, RATE, DECAY)
    new_out = adamw(weight_out, first_out, second_out, (grad_out * scale).T, RATE, DECAY)
    new_norm = adamw(norm_params, norm_first, norm_second, norm_total * scale, RATE_NORM, 0.0)
    shape = (micros, 1, row_span, columns, chan)
    return (
        block_out.reshape(shape),
        input_grad.reshape(shape),
        *[group[k] for k in range(3) for group in (new_in, new_mid, new_out)],
        *new_norm,
        grad_norm.reshape(1),
    )


def solution(mesh):
    acts = P(None, "batch", "rows", None, None)
    by_row, by_col = P(("batch", "rows"), None), P(None, ("batch", "rows"))
    weights = (by_row, by_row, by_col)
    return jax.shard_map(
        per_device,
        mesh=mesh,
        in_specs=(
            acts, P(None, None, "batch", "rows", None, None), P(), P(), *(weights * 3), P(), P(), P()
        ),
        out_specs=(acts, acts, *(weights * 3), P(), P(), P(), P()),
        check_vma=False,
    )
```

```python
import functools

import jax
import jax.numpy as jnp
import numpy as np
from jax import lax
from jax.experimental import pallas as pl
from jax.experimental.pallas import tpu as pltpu
from jax.sharding import PartitionSpec as P

DILATION_SIZE = 4
NEWTON = 6
STEP = 10

EPS_NORM = 1e-05
CLIP = 1.0
RATE = 0.02
RATE_NORM = 0.3
BETA_ONE = 0.9
BETA_TWO = 0.999
ADAM_EPS = 1e-08
DECAY = 0.01

F32 = jnp.float32
BF16 = jnp.bfloat16


def swap(x, axis, mask):
    return lax.ppermute(x, axis, [(i, i ^ mask) for i in range(lax.axis_size(axis))])


def row_groups():
    groups = []
    bit, rest = 1, lax.axis_size("rows") // 2
    while rest > 1:
        size = min(4, rest)
        groups.append((bit, size))
        bit += size.bit_length() - 1
        rest //= size
    return groups


def group_sum(x, axis, shift, size):
    got = [x] + [swap(x, axis, m << shift) for m in range(1, size)]
    if size == 2:
        return got[0] + got[1]
    return (got[0] + got[1]) + (got[2] + got[3])


def chip_sums(x):
    return group_sum(group_sum(x, "rows", 0, 2), "batch", 0, lax.axis_size("batch"))


def all_sum(x):
    return line_sums(chip_sums(x))


def line_sums(x):
    for bit, size in row_groups():
        x = group_sum(x, "rows", bit, size)
    return x


def put(buf, piece, index, axis):
    return lax.dynamic_update_slice_in_dim(buf, jnp.expand_dims(piece, axis), index, axis)


def take(buf, index, axis):
    return lax.dynamic_index_in_dim(buf, index, axis, keepdims=False)


def gather_shards(shard):
    mine = lax.axis_index("rows")
    core = mine & 1
    batch = lax.axis_index("batch")
    block = shard[None]
    for bit, size in row_groups():
        place = (mine >> bit) & (size - 1)
        got = [block] + [swap(block, "rows", m << bit) for m in range(1, size)]
        buf = jnp.zeros((size,) + block.shape, block.dtype)
        for m, piece in enumerate(got):
            buf = put(buf, piece, place ^ m, 0)
        block = buf.reshape((-1,) + block.shape[1:])
    half = block.shape[0] // 2
    from_x = swap(block, "batch", 1)
    from_y = swap(block, "batch", 2)
    far_low = swap(from_x[:half], "batch", 2)
    far_high = swap(from_y[half:], "batch", 1)
    far = jnp.concatenate([far_low, far_high], axis=0)
    full = jnp.zeros((4, block.shape[0], 2) + block.shape[1:], block.dtype)
    for m, piece in enumerate((block, from_x, from_y, far)):
        other = swap(piece, "rows", 1)
        for value, where in ((piece, core), (other, 1 - core)):
            full = lax.dynamic_update_slice(
                full, value[None, :, None], (batch ^ m, 0, where, 0, 0)
            )
    return full


def scatter_sums(grad):
    mine = lax.axis_index("rows")
    core = mine & 1
    batch = lax.axis_index("batch")
    count = lax.axis_size("rows")
    grad = grad.reshape(4, count // 2, 2, -1, grad.shape[-1])
    got = swap(take(grad, 1 - core, 2).astype(BF16), "rows", 1)
    part = take(grad, core, 2).astype(F32) + got.astype(F32)
    half = part.shape[1] // 2
    own, to_x, to_y, far = [take(part, batch ^ m, 0) for m in range(4)]
    low = swap(far[:half].astype(BF16), "batch", 1).astype(F32)
    high = swap(far[half:].astype(BF16), "batch", 2).astype(F32)
    to_x = jnp.concatenate([to_x[:half], to_x[half:] + high], axis=0)
    to_y = jnp.concatenate([to_y[:half] + low, to_y[half:]], axis=0)
    from_x = swap(to_x.astype(BF16), "batch", 1)
    from_y = swap(to_y.astype(BF16), "batch", 2)
    own = own + from_x.astype(F32) + from_y.astype(F32)
    for bit, size in reversed(row_groups()):
        place = (mine >> bit) & (size - 1)
        own = own.reshape((size, -1) + own.shape[1:])
        total = take(own, place, 0)
        for m in range(1, size):
            total = total + swap(take(own, place ^ m, 0).astype(BF16), "rows", m << bit).astype(F32)
        own = total
    return own.reshape(own.shape[-2:])


def joined(pieces, *after):
    sizes = [piece.shape[0] for piece in pieces]

    def kernel(*refs):
        first = 0
        for ref, size in zip(refs, sizes):
            refs[-1][first : first + size] = ref[...].astype(BF16)
            first += size

    return pl.pallas_call(
        kernel,
        in_specs=[pl.BlockSpec(memory_space=pltpu.VMEM)] * len(pieces) + [pl.BlockSpec(memory_space=pl.ANY)] * len(after),
        out_specs=pl.BlockSpec(memory_space=pltpu.VMEM),
        out_shape=jax.ShapeDtypeStruct((sum(sizes),) + pieces[0].shape[1:], BF16),
    )(*pieces, *after)


def owners(table):
    mine, batch = lax.axis_index("rows"), lax.axis_index("batch")
    far, near, core = np.array(table, np.int32).T
    return ((batch ^ far) * (lax.axis_size("rows") // 2) + ((mine >> 1) ^ near)) * 2 + ((mine & 1) ^ core)


class Gather:
    def along_line(self, shard):
        blocks = [shard[None]]
        for bit, size in row_groups():
            block = jnp.concatenate(blocks, axis=0)
            blocks = [block] + [swap(block, "rows", m << bit) for m in range(1, size)]
        return blocks

    def near(self, block):
        self.block = block
        return swap(block, "batch", 1), swap(block, "batch", 2)

    def far(self, from_x, from_y):
        self.from_x, self.from_y = from_x, from_y
        half = from_x.shape[0] // 2
        return swap(from_x[:half], "batch", 2), swap(from_y[half:], "batch", 1)

    def pieces(self, far_low, far_high):
        got, table = [], []
        half = far_low.shape[0]
        parts = ((self.block, 0, 0), (self.from_x, 1, 0), (self.from_y, 2, 0), (far_low, 3, 0), (far_high, 3, half))
        for piece, mask, first in parts:
            for array, core in ((piece, 0), (swap(piece, "rows", 1), 1)):
                got.append(array)
                table += [(mask, first + j, core) for j in range(piece.shape[0])]
        return got, table


def in_order(*values):
    return lax.optimization_barrier(values)


class Assembly:
    def __init__(self, arrays, table, first, size):
        self.first, self.size = first, size
        starts = owners(table) * size if table else jnp.zeros(1, jnp.int32)
        self.ins = [smem(starts)] + [whole(array) for array in arrays]
        self.count = len(self.ins)

    def run(self, refs, held):
        starts, k = refs[0], 0
        for ref in refs[1:]:
            for j in range(ref.shape[0]):
                rows = pl.ds(pl.multiple_of(starts[k], self.size), self.size)
                held[rows, :] = ref[j, self.first : self.first + self.size, :]
                k += 1


def assemble_kernel(assembly, *refs):
    assembly.run(refs[:-1], refs[-1])


class Spread:
    def __init__(self, width, *rows):
        mine, batch = lax.axis_index("rows"), lax.axis_index("batch")
        line = lax.axis_size("rows") // 2
        self.chips = 4 * line
        self.sizes = [r // (2 * self.chips) for r in rows]
        self.direct = not any(size % 16 for size in self.sizes)
        chip = jnp.arange(self.chips, dtype=jnp.int32)
        far = (chip // line) ^ batch
        near = (chip % line) ^ (mine >> 1)
        half = line // 2
        place = ((near // half) * 4 + (far ^ (far >> 1))) * half + near % half
        self.ins = [smem(place.astype(jnp.int32)), smem((mine & 1).astype(jnp.int32).reshape(1))]
        shapes = [(r, width) for r in rows]
        if self.direct:
            shapes = [(self.chips, sum(self.sizes), width)] * 2
        self.outs = [constant(shape, BF16) for shape in shapes]

    def emit(self, weight, product, base, rows, place_ref, core_ref, outs):
        if not self.direct:
            outs[weight][pl.ds(base, rows), :] = product[0:rows, :].astype(BF16)
            return
        core = core_ref[0]
        size, low = self.sizes[weight], sum(self.sizes[:weight])
        pair = 2 * size
        first = base // pair
        for k in range(rows // pair):
            to = place_ref[first + k]
            for ref, c in ((outs[0], 1 - core), (outs[1], core)):
                start = pl.multiple_of(k * pair + c * size, 16)
                ref[to, low : low + size, :] = product[pl.ds(start, size), :].astype(BF16)


class Sums:
    def __init__(self, spread, outs):
        self.direct = spread.direct
        if not self.direct:
            parts = [part.reshape(2 * spread.chips, size, -1) for part, size in zip(outs, spread.sizes)]
            self.total = scatter_sums(jnp.concatenate(parts, axis=1).reshape(-1, outs[0].shape[-1]))
            return
        shape = (2, 4, lax.axis_size("rows") // 4) + outs[0].shape[1:]
        self.keep = outs[1].reshape(shape)
        self.got = swap(outs[0], "rows", 1).reshape(shape)

    def part(self, half, index):
        return self.keep[half, index].astype(F32) + self.got[half, index].astype(F32)

    def send_far(self):
        return self.part(0, slice(1, 3)).astype(BF16), self.part(1, slice(2, 4)).astype(BF16)

    def take_far(self, sends):
        self.far = swap(sends[0], "batch", 1), swap(sends[1], "batch", 2)

    def send_near(self):
        from_x, from_y = self.far
        return (
            (self.part(1, 1) + from_y[0].astype(F32)).astype(BF16),
            (self.part(0, 3) + from_x[1].astype(F32)).astype(BF16),
        )

    def take_near(self, sends):
        self.near = swap(sends[0], "batch", 1), swap(sends[1], "batch", 2)

    def send_line(self):
        low = self.part(0, 0) + self.far[0][0].astype(F32) + self.near[1].astype(F32)
        high = self.part(1, 0) + self.far[1][1].astype(F32) + self.near[0].astype(F32)
        return jnp.concatenate([low, high], axis=0)

    def take_line(self, own):
        self.parts = []
        for bit, size in reversed(row_groups()):
            if self.parts:
                own = sum(part.astype(F32) for part in self.parts)
            own = own.reshape((size, -1) + own.shape[1:])
            self.parts = [own[0]] + [swap(own[m].astype(BF16), "rows", m << bit) for m in range(1, size)]

    def finish(self):
        if self.direct:
            own = sum(part.astype(F32) for part in self.parts)
            self.total = own.reshape(own.shape[-2:])
        return self.total


CHUNK = 16
PAD = 8
NN, NT, TN = (1, 0), (1, 1), (0, 0)


def dot(left, right, dims):
    return lax.dot_general(left, right, ((dims[:1], dims[1:]), ((), ())), preferred_element_type=F32)


def softplus(z):
    e = jnp.exp(-jnp.abs(z))
    return jnp.maximum(z, 0.0) + jnp.where(e < 1e-3, e * (1.0 - 0.5 * e), jnp.log(1.0 + e))


def sigmoid(z):
    return 0.5 * jnp.tanh(0.5 * z) + 0.5


def wide(mask, width):
    return jnp.concatenate([mask] * (width // mask.shape[-1]), axis=-1)


def fold(v):
    return v[:8] + v[8:]


def down(v):
    return jnp.sum(v, axis=0, keepdims=True)


def loop(rows, body, init, unroll=2):
    def step(i, carry):
        return body(pl.ds(pl.multiple_of(i * CHUNK, CHUNK), CHUNK), carry)

    return lax.fori_loop(0, rows // CHUNK, step, init, unroll=unroll)


def zeros8(width, count=2):
    return tuple(jnp.zeros((8, width), F32) for _ in range(count))


def norm_stats(sums_ref, inv, gain):
    mean = sums_ref[0, 0:1, :] * inv
    rstd = lax.rsqrt(sums_ref[0, 1:2, :] * inv - mean * mean + EPS_NORM)
    return mean, rstd, gain * rstd


def call(kernel, grid, ins, outs, scratch=(), flops=0, nbytes=0, vmem=48):
    got = pl.pallas_call(
        kernel,
        grid=grid,
        in_specs=[spec for _, spec in ins],
        out_specs=[spec for _, spec in outs],
        out_shape=[shape for shape, _ in outs],
        scratch_shapes=list(scratch),
        compiler_params=pltpu.CompilerParams(
            dimension_semantics=("arbitrary",) * len(grid), vmem_limit_bytes=vmem * 1024 * 1024
        ),
        cost_estimate=pl.CostEstimate(flops=flops, bytes_accessed=nbytes, transcendentals=0),
    )(*[array for array, _ in ins])
    return got[0] if len(outs) == 1 else got


def block(shape, index, **kw):
    return pl.BlockSpec(shape, index, **kw)


def listed(got):
    return list(got) if isinstance(got, (list, tuple)) else [got]


def whole(array):
    zeros = (0,) * len(array.shape)
    return (array, pl.BlockSpec(array.shape, lambda *_: zeros, pipeline_mode=pl.Buffered(1)))


def smem(array):
    return (array, pl.BlockSpec(memory_space=pltpu.SMEM))


def anywhere(array):
    return (array, pl.BlockSpec(memory_space=pl.ANY))


def constant(shape, dtype):
    spec = pl.BlockSpec(shape, lambda *_: (0,) * len(shape), pipeline_mode=pl.Buffered(1))
    return (jax.ShapeDtypeStruct(shape, dtype), spec)


def out(shape, dtype, spec_shape, index):
    return (jax.ShapeDtypeStruct(shape, dtype), pl.BlockSpec(spec_shape, index))


def gram_kernel(task_ref, mask_ref, out_ref):
    lanes = mask_ref.shape[-1]
    chan = task_ref.shape[-1]

    @pl.when(pl.program_id(0) == 0)
    def _():
        out_ref[...] = jnp.zeros_like(out_ref)

    def step(rows, carry):
        sums = [jnp.zeros((CHUNK, lanes), F32)] * 6
        for col in range(chan // lanes):
            cols = pl.ds(col * lanes, lanes)
            t = [task_ref[k, 0, 0, 0, rows, cols].astype(F32) for k in range(3)]
            pairs = [t[i] * t[j] for i in range(3) for j in range(i, 3)]
            sums = [s + p for s, p in zip(sums, pairs)]
        mask = mask_ref[0, 0, rows, :]
        return tuple(c + fold(s * mask) for c, s in zip(carry, sums))

    got = loop(task_ref.shape[4], step, zeros8(lanes, 6), unroll=1)
    for k in range(6):
        out_ref[k : k + 1, :] += down(got[k])


def first_kernel(assembly, x_ref, mask_ref, gram_ref, *refs):
    pieces, (wide_ref, low_ref, sums_ref, w_ref) = refs[: assembly.count], refs[assembly.count :]
    width = w_ref.shape[1]

    @pl.when(pl.program_id(0) == 0)
    def _():
        assembly.run(pieces, w_ref)

    wide_ref[0] = dot(x_ref[0], w_ref[...], NN)

    def step(rows, carry):
        v = wide_ref[0, rows, :]
        low_ref[0, rows, :] = v.astype(BF16)
        kept = v * wide(mask_ref[0, 0, rows, :], width)
        return carry[0] + fold(kept), carry[1] + fold(kept * v)

    got = loop(x_ref.shape[1], step, zeros8(width))
    sums_ref[0] = jnp.zeros_like(sums_ref[0])
    sums_ref[0, 0:1, :] = down(got[0])
    sums_ref[0, 1:2, :] = down(got[1])
    for k in range(6):
        lane = (k % 4) * 128
        sums_ref[0, 2 + k // 4 : 3 + k // 4, lane : lane + 128] = gram_ref[0, k : k + 1, :]


def upstream_kernel(sums_ref, task_ref, mask_ref, *refs):
    out_ref, coeff_ref = refs[-2:]
    lanes = mask_ref.shape[-1]

    @pl.when((pl.program_id(0) == 0) & (pl.program_id(1) == 0))
    def _():
        def entry(k):
            lane, row = (k % 4) * 128, 2 + k // 4
            both = sums_ref[0, row : row + 1, lane : lane + 128] + sums_ref[1, row : row + 1, lane : lane + 128]
            return jnp.sum(both, axis=1, keepdims=True)

        place = {}
        k = 0
        for i in range(3):
            for j in range(i, 3):
                place[i, j] = place[j, i] = entry(k)
                k += 1
        trace = place[0, 0] + place[1, 1] + place[2, 2]
        ymat = [[place[i, j] / trace for j in range(3)] for i in range(3)]
        zmat = [[jnp.full((1, 1), 1.0 if i == j else 0.0, F32) for j in range(3)] for i in range(3)]

        def mul(a, b):
            return [
                [a[i][0] * b[0][j] + a[i][1] * b[1][j] + a[i][2] * b[2][j] for j in range(3)]
                for i in range(3)
            ]

        for _ in range(NEWTON):
            zy = mul(zmat, ymat)
            pmat = [[(1.5 if i == j else 0.0) - 0.5 * zy[i][j] for j in range(3)] for i in range(3)]
            ymat = mul(ymat, pmat)
            zmat = mul(pmat, zmat)
        for i in range(3):
            value = (zmat[i][0] + zmat[i][1] + zmat[i][2]) / jnp.sqrt(F32(3.0))
            coeff_ref[i] = jnp.broadcast_to(value, (8, lanes))

    def step(rows, carry):
        mask = mask_ref[0, 0, rows, :]
        c = [jnp.concatenate([coeff_ref[i]] * (CHUNK // 8), axis=0) * mask for i in range(3)]
        for col in range(task_ref.shape[-1] // lanes):
            cols = pl.ds(col * lanes, lanes)
            t = [task_ref[k, 0, 0, 0, rows, cols].astype(F32) for k in range(3)]
            out_ref[0, rows, cols] = (c[0] * t[0] + c[1] * t[1] + c[2] * t[2]).astype(BF16)
        return carry

    loop(task_ref.shape[4], step, 0, unroll=1)


def shifted_sum(parts, row, start, rows, sign):
    at = PAD + start
    low, high = at + sign * DILATION_SIZE, at - sign * DILATION_SIZE
    return (
        parts[1, row, at : at + rows, :]
        + parts[0, row, low : low + rows, :]
        + parts[2, row, high : high + rows, :]
    )


def clear_pads(ref):
    edge = ref.shape[-2]
    zero = jnp.zeros(ref.shape[:-2] + (PAD, ref.shape[-1]), ref.dtype)
    ref[..., 0:PAD, :] = zero
    ref[..., edge - PAD : edge, :] = zero


def second_kernel(
    assembly, inv_ref, sums_ref, param_ref, own_ref, up_ref, down_ref, mask_ref, *refs
):
    h_ref, wide_ref, low_ref, out_ref, cat_ref, part_ref, w_ref = refs[-7:]
    micro = pl.program_id(0)
    width = own_ref.shape[-1]
    pixels = own_ref.shape[1]
    columns = part_ref.shape[2] - 2 * PAD

    @pl.when(micro == 0)
    def _():
        assembly.run(refs[: assembly.count], w_ref)
        clear_pads(part_ref)

    mean, rstd, scale = norm_stats(sums_ref, inv_ref[micro], param_ref[0:1, :])
    offset = param_ref[1:2, :] - mean * scale
    for k, ref in enumerate((up_ref, own_ref, down_ref)):
        def step(rows, carry):
            z = ref[0, rows, :].astype(F32) * scale + offset
            h = (softplus(z) * wide(mask_ref[k, 0, rows, :], width)).astype(BF16)
            h_ref[k, 0, rows, :] = h
            cat_ref[rows, k * width : (k + 1) * width] = h
            return carry

        loop(pixels, step, 0)

    for tx in range(3):
        taps = [w_ref[(3 * ty + tx) * width : (3 * ty + tx + 1) * width, :] for ty in range(3)]
        product = dot(cat_ref[...], jnp.concatenate(taps, axis=0), NN)
        part_ref[tx, :, PAD : PAD + columns, :] = product.reshape(-1, columns, width)

    def row_step(row, carry):
        for start in range(0, columns, CHUNK):
            rows = pl.ds(pl.multiple_of(row * columns + start, CHUNK), CHUNK)
            v = shifted_sum(part_ref, row, start, CHUNK, -1)
            wide_ref[0, rows, :] = v
            low_ref[0, rows, :] = v.astype(BF16)
            kept = v * wide(mask_ref[1, 0, rows, :], width)
            carry = carry[0] + fold(kept), carry[1] + fold(kept * v)
        return carry

    got = lax.fori_loop(0, pixels // columns, row_step, zeros8(width))
    out_ref[0, 0:1, :] = down(got[0])
    out_ref[0, 1:2, :] = down(got[1])


def third_kernel(inv_ref, sums_ref, param_ref, a_ref, mask_ref, w_ref, h_ref, wide_ref, out_ref):
    micro = pl.program_id(0)
    width = a_ref.shape[-1]
    tile = 512
    mean, rstd, scale = norm_stats(sums_ref, inv_ref[micro], param_ref[0:1, :])
    offset = param_ref[1:2, :] - mean * scale

    def step(rows, carry):
        z = a_ref[0, rows, :] * scale + offset
        h_ref[0, rows, :] = (softplus(z) * wide(mask_ref[0, 0, rows, :], width)).astype(BF16)
        return carry

    loop(a_ref.shape[1], step, 0)
    for col in range(0, w_ref.shape[0], tile):
        cols = pl.ds(col, tile)
        wide_ref[0, :, cols] = dot(h_ref[0], w_ref[cols, :], NT)

        def sum_step(rows, carry):
            v = wide_ref[0, rows, cols]
            kept = v * wide(mask_ref[0, 0, rows, :], tile)
            return carry[0] + fold(kept), carry[1] + fold(kept * v)

        got = loop(a_ref.shape[1], sum_step, zeros8(tile))
        out_ref[0, 0:1, cols] = down(got[0])
        out_ref[0, 1:2, cols] = down(got[1])


def peak_kernel(
    inv_ref, sums_ref, param_ref, a_ref, x_ref, up_ref, mask_ref, block_ref, du_ref, out_ref
):
    width = a_ref.shape[-1]
    mean, rstd, scale = norm_stats(sums_ref, inv_ref[pl.program_id(0)], param_ref[0:1, :])
    shift = param_ref[1:2, :]

    def step(rows, carry):
        centred = a_ref[0, rows, :] - mean
        u = centred * scale + (shift + x_ref[0, rows, :].astype(F32))
        mask = wide(mask_ref[0, 0, rows, :], width)
        upper = 0.5 * jnp.tanh(0.5 * jnp.abs(u)) + 0.5
        block_ref[0, rows, :] = ((jnp.maximum(u, 0.0) - jnp.log(upper)) * mask).astype(BF16)
        du = up_ref[0, rows, :].astype(F32) * jnp.where(u >= 0.0, upper, 1.0 - upper)
        du_ref[0, rows, :] = du.astype(BF16)
        return carry[0] + fold(du), carry[1] + fold(du * centred)

    got = loop(a_ref.shape[1], step, zeros8(width))
    out_ref[0, 0:1, :] = down(got[0])
    out_ref[0, 1:2, :] = down(got[1]) * rstd


def lower_consts(stats_ref, grads_ref, inv, gain):
    mean, rstd, scale = norm_stats(stats_ref, inv, gain)
    return mean, scale, grads_ref[0, 0:1, :] * inv, grads_ref[0, 1:2, :] * inv * rstd


def back_third_kernel(
    inv_ref, stats3_ref, grads3_ref, stats2_ref, param3_ref, param2_ref,
    a3_ref, du_ref, a2_ref, mask_ref, w_ref,
    d_ref, wide_ref, low_ref, out_ref,
):
    inv = inv_ref[pl.program_id(0)]
    tile = 512
    for col in range(0, a3_ref.shape[2], tile):
        cols = pl.ds(col, tile)
        mean = stats3_ref[0, 0:1, cols] * inv
        rstd = lax.rsqrt(stats3_ref[0, 1:2, cols] * inv - mean * mean + EPS_NORM)
        scale = param3_ref[0:1, cols] * rstd
        base = grads3_ref[0, 0:1, cols] * inv
        slope = grads3_ref[0, 1:2, cols] * inv * rstd

        def step(rows, carry):
            d = du_ref[0, rows, cols].astype(F32) - (base + (a3_ref[0, rows, cols] - mean) * slope)
            d_ref[0, rows, cols] = (d * scale * wide(mask_ref[0, 0, rows, :], tile)).astype(BF16)
            return carry

        loop(a3_ref.shape[1], step, 0)
    wide_ref[0] = dot(d_ref[0], w_ref[...], NN)
    width = w_ref.shape[1]
    mean, rstd, scale = norm_stats(stats2_ref, inv, param2_ref[0:1, :])
    shift = param2_ref[1:2, :]

    def last(rows, carry):
        centred = a2_ref[0, rows, :] - mean
        gate = sigmoid(centred * scale + shift) * wide(mask_ref[0, 0, rows, :], width)
        dz = wide_ref[0, rows, :] * gate
        wide_ref[0, rows, :] = dz
        low_ref[0, rows, :] = dz.astype(BF16)
        return carry[0] + fold(dz), carry[1] + fold(dz * centred)

    got = loop(a2_ref.shape[1], last, zeros8(width))
    out_ref[0, 0:1, :] = down(got[0])
    out_ref[0, 1:2, :] = down(got[1]) * rstd


def lower_second_kernel(
    inv_ref, stats2_ref, grads2_ref, param2_ref,
    a2_ref, a2_up_ref, a2_down_ref, dz_ref, dz_up_ref, dz_down_ref, mask_ref, cat_ref, shift_ref, pad_ref,
):
    inv = inv_ref[pl.program_id(0)]
    pixels, width = a2_ref.shape[1:]
    columns = pad_ref.shape[1] - 2 * PAD

    @pl.when(pl.program_id(0) == 0)
    def _():
        clear_pads(pad_ref)

    mean, scale, base, slope = lower_consts(stats2_ref, grads2_ref, inv, param2_ref[0:1, :])

    def lowered(k, a, dz, rows):
        d = dz.astype(F32) - (base + (a.astype(F32) - mean) * slope)
        return d * scale * wide(mask_ref[k, 0, rows, :], width)

    for k, a_ref, d_ref, place in ((0, a2_up_ref, dz_up_ref, 2), (2, a2_down_ref, dz_down_ref, 0)):
        def step(rows, carry):
            d = lowered(k, a_ref[0, rows, :], d_ref[0, rows, :], rows)
            cat_ref[0, rows, place * width : (place + 1) * width] = d.astype(BF16)
            return carry

        loop(pixels, step, 0)

    def own_step(row, carry):
        for start in range(0, columns, CHUNK):
            rows = pl.ds(pl.multiple_of(row * columns + start, CHUNK), CHUNK)
            d = lowered(1, a2_ref[0, rows, :], dz_ref[0, rows, :], rows)
            low = d.astype(BF16)
            cat_ref[0, rows, width : 2 * width] = low
            shift_ref[0, rows, width : 2 * width] = low
            pad_ref[row, PAD + start : PAD + start + CHUNK, :] = d
        for start in range(0, columns, CHUNK):
            rows = pl.ds(pl.multiple_of(row * columns + start, CHUNK), CHUNK)
            for tx in (-1, 1):
                at = PAD + start - tx * DILATION_SIZE
                moved = pad_ref[row, at : at + CHUNK, :].astype(BF16)
                shift_ref[0, rows, (tx + 1) * width : (tx + 2) * width] = moved
        return carry

    lax.fori_loop(0, pixels // columns, own_step, 0)


def back_second_kernel(
    assembly, inv_ref, stats1_ref, param1_ref, cat_ref, a1_ref, mask_ref, *refs
):
    wide_ref, out_ref, part_ref, w_ref = refs[-4:]
    inv = inv_ref[pl.program_id(0)]
    pixels, width = a1_ref.shape[1:]
    columns = part_ref.shape[2] - 2 * PAD

    @pl.when(pl.program_id(0) == 0)
    def _():
        assembly.run(refs[: assembly.count], w_ref)
        clear_pads(part_ref)

    for tx in range(3):
        taps = [w_ref[(3 * ty + tx) * width : (3 * ty + tx + 1) * width, :] for ty in range(3)]
        product = dot(cat_ref[0], jnp.concatenate(taps, axis=1), NT)
        part_ref[tx, :, PAD : PAD + columns, :] = product.reshape(-1, columns, width)

    mean1, rstd1, scale1 = norm_stats(stats1_ref, inv, param1_ref[0:1, :])
    shift1 = param1_ref[1:2, :]

    def row_step(row, carry):
        for start in range(0, columns, CHUNK):
            rows = pl.ds(pl.multiple_of(row * columns + start, CHUNK), CHUNK)
            centred = a1_ref[0, rows, :] - mean1
            gate = sigmoid(centred * scale1 + shift1) * wide(mask_ref[0, 0, rows, :], width)
            dz = shifted_sum(part_ref, row, start, CHUNK, 1) * gate
            wide_ref[0, rows, :] = dz
            carry = carry[0] + fold(dz), carry[1] + fold(dz * centred)
        return carry

    got = lax.fori_loop(0, pixels // columns, row_step, zeros8(width))
    out_ref[0, 0:1, :] = down(got[0])
    out_ref[0, 1:2, :] = down(got[1]) * rstd1


def grads_kernel(spread, h_ref, d_ref, d3_ref, h2_ref, place_ref, core_ref, *refs):
    outs, product = refs[:-1], refs[-1]
    width = h_ref.shape[-1]
    step = pl.program_id(0)

    @pl.when(step < 3)
    def _():
        for tx in range(3):
            rows = pl.ds(pl.multiple_of((3 * step + tx) * width, width), width)
            product[rows, :] = dot(h_ref[0], d_ref[:, tx * width : (tx + 1) * width], TN).astype(BF16)

    @pl.when(step == 2)
    def _():
        spread.emit(0, product, 0, product.shape[0], place_ref, core_ref, outs)

    @pl.when(step >= 3)
    def _():
        rows = d3_ref.shape[1]
        product[0:rows, :] = dot(d3_ref[...], h2_ref[...], TN).astype(BF16)
        spread.emit(1, product, pl.multiple_of((step - 3) * rows, rows), rows, place_ref, core_ref, outs)


def first_back_kernel(
    spread, inv_ref, stats_ref, grads_ref, param_ref, dz_ref, a_ref, mask_ref, x_ref, place_ref, core_ref, *refs
):
    d_ref, outs, product = refs[0], refs[1:-1], refs[-1]
    pixels, width = dz_ref.shape[1:]

    @pl.when(pl.program_id(0) == 0)
    def _():
        for micro in range(dz_ref.shape[0]):
            inv = inv_ref[micro]
            mean, scale, base, slope = lower_consts(
                stats_ref.at[micro : micro + 1], grads_ref.at[micro : micro + 1], inv, param_ref[0:1, :]
            )

            def step(rows, carry):
                d = dz_ref[micro, rows, :] - (base + (a_ref[micro, rows, :] - mean) * slope)
                d = d * scale * wide(mask_ref[0, micro, rows, :], width)
                d_ref[micro, rows, :] = d.astype(BF16)
                return carry

            loop(pixels, step, 0)

    product[...] = dot(x_ref[...], d_ref[...].reshape(-1, width), TN)
    rows = product.shape[0]
    spread.emit(0, product, pl.multiple_of(pl.program_id(0) * rows, rows), rows, place_ref, core_ref, outs)


def input_grad_kernel(d_ref, w_ref, du_ref, out_ref):
    out_ref[...] = (dot(d_ref[...], w_ref[...], NT) + du_ref[...].astype(F32)).astype(BF16)


def adamw(weight, first, second, grad, rate, decay):
    new_first = BETA_ONE * first + (1.0 - BETA_ONE) * grad
    new_second = BETA_TWO * second + (1.0 - BETA_TWO) * grad * grad
    first_hat = new_first / (1.0 - BETA_ONE**STEP)
    second_hat = new_second / (1.0 - BETA_TWO**STEP)
    new_weight = weight - rate * (first_hat / (jnp.sqrt(second_hat) + ADAM_EPS) + decay * weight)
    return (new_weight, new_first, new_second)


def neighbours(x):
    count = lax.axis_size("rows")
    above = lax.ppermute(x, "rows", [(i, i + 1) for i in range(count - 1)])
    below = lax.ppermute(x, "rows", [(i + 1, i) for i in range(count - 1)])
    return above, below


def per_device(
    features, task_grads, row_counts, col_counts,
    weight_in, weight_mid, weight_out,
    first_in, first_mid, first_out,
    second_in, second_mid, second_out,
    norm_params, norm_first, norm_second,
):
    micros, _, row_span, columns, chan = features.shape
    inner = weight_in.shape[1]
    pixels = row_span * columns
    total_pixels = micros * pixels
    batch = lax.axis_index("batch")
    own_rows = lax.dynamic_index_in_dim(row_counts, batch, 1, keepdims=False)
    own_cols = lax.dynamic_index_in_dim(col_counts, batch, 1, keepdims=False)
    base = lax.axis_index("rows") * row_span + jnp.arange(-1, 2, dtype=jnp.int32) * row_span
    row_ids = base[:, None] + jnp.arange(row_span, dtype=jnp.int32)
    col_ids = jnp.arange(columns, dtype=jnp.int32)
    in_rows = (row_ids[:, None] >= 0) & (row_ids[:, None] < own_rows[None, :, None])
    in_cols = col_ids < own_cols[:, None]
    masks = (in_rows[:, :, :, None] & in_cols[None, :, None, :]).astype(F32)
    masks = jnp.broadcast_to(masks.reshape(3, micros, pixels, 1), (3, micros, pixels, 128))
    inverse = 1.0 / jnp.sum(row_counts * col_counts, axis=1).astype(F32)

    grams = []
    for micro in range(micros):
        grams.append(call(
            gram_kernel, (row_span,),
            [
                (task_grads, block((3, 1, 1, 1, columns, chan), functools.partial(lambda m, r: (0, m, 0, r, 0, 0), micro))),
                (masks, block((1, 1, columns, 128), functools.partial(lambda m, r: (1, m, r, 0), micro))),
            ],
            [out((8, 128), F32, (8, 128), lambda r: (0, 0))],
            flops=6 * total_pixels * chan, nbytes=3 * total_pixels * chan, vmem=4,
        ))
    x = features.reshape(micros, pixels, chan)
    params = [norm_params[:, :inner], norm_params[:, inner : 2 * inner], norm_params[:, 2 * inner :]]

    def per_micro(array):
        return (array, block((1,) + array.shape[1:], lambda m, *_: (m,) + (0,) * (len(array.shape) - 1)))

    def out_micro(width, dtype, rows=pixels):
        return out((micros, rows, width), dtype, (1, rows, width), lambda m: (m, 0, 0))

    own_mask = (masks, block((1, 1, pixels, 128), lambda m, *_: (1, m, 0, 0)))
    all_masks = (masks, block((3, 1, pixels, 128), lambda m: (0, m, 0, 0)))
    row_mask = (masks, block((1, 1, columns, 128), lambda m, r: (1, m, r, 0)))
    task_rows = (
        task_grads, block((3, 1, 1, 1, columns, chan), lambda m, r: (0, m, 0, r, 0, 0))
    )
    big = total_pixels * chan
    small = total_pixels * inner
    part_rows = weight_in.shape[0]
    mid_rows = weight_mid.shape[0]
    low_mid = weight_mid.astype(BF16)
    both = jnp.concatenate([weight_in.astype(BF16), weight_out.T.astype(BF16)], axis=0)
    direct = part_rows % 16 == 0 and mid_rows % 16 == 0
    if direct:
        gather_both, gather_mid = Gather(), Gather()
        line_both = gather_both.along_line(both)
        near_both, low_mid = in_order(joined(line_both, *grams), low_mid)
        from_both = gather_both.near(near_both)
        line_mid = gather_mid.along_line(low_mid)
        far_both = gather_both.far(*from_both)
        arrays, table = gather_both.pieces(*far_both)
        line_mid = in_order(*line_mid, *far_both)[: len(line_mid)]
        near_mid, *arrays = in_order(joined(line_mid), *arrays)
        from_mid = gather_mid.near(near_mid)
        ins_in, ins_out = [Assembly(arrays, table, k * part_rows, part_rows) for k in range(2)]
    else:
        full = gather_shards(both).reshape(-1, 2, part_rows, inner)
        ins_in, ins_out = [Assembly([full[:, k].reshape(1, -1, inner)], (), 0, chan) for k in range(2)]
        ins_mid = Assembly([gather_shards(low_mid).reshape(1, -1, inner)], (), 0, 9 * inner)
    whole_weight = constant((chan, inner), BF16)
    a_one, a_one_low, part, w_in = call(
        functools.partial(first_kernel, ins_in), (micros,),
        [per_micro(x), own_mask, per_micro(jnp.stack(grams)), *ins_in.ins],
        [out_micro(inner, F32), out_micro(inner, BF16), out_micro(inner, F32, 4), whole_weight],
        flops=2 * big * inner, nbytes=2 * big + 8 * small, vmem=12,
    )
    a_one_up, a_one_down = neighbours(a_one_low)
    core_one = group_sum(part, "rows", 0, 2)
    if direct:
        core_one, *from_mid = in_order(core_one, *from_mid)
    chip_one = group_sum(core_one, "batch", 0, lax.axis_size("batch"))
    chip_one, a_one_up, a_one_down = in_order(chip_one, a_one_up, a_one_down)
    if direct:
        far_mid = gather_mid.far(*from_mid)
    stats_one = line_sums(chip_one)
    upstream = call(
        upstream_kernel, (micros, row_span),
        [whole(stats_one), task_rows, row_mask],
        [out((micros, pixels, chan), BF16, (1, columns, chan), lambda m, r: (m, r, 0))],
        [pltpu.VMEM((3, 8, 128), F32)],
        flops=8 * big, nbytes=10 * big, vmem=6,
    )
    if direct:
        upstream, *far_mid = in_order(upstream, *far_mid)
        ins_mid = Assembly(*gather_mid.pieces(*far_mid), 0, mid_rows)
    padded = (3, row_span, columns + 2 * PAD, inner)
    held = pltpu.VMEM((9 * inner, inner), BF16)
    taps = [pltpu.VMEM((pixels, 3 * inner), BF16), pltpu.VMEM(padded, F32), held]
    h_one, a_two, a_two_low, part = call(
        functools.partial(second_kernel, ins_mid), (micros,),
        [
            smem(inverse), per_micro(stats_one), whole(params[0]), per_micro(a_one),
            per_micro(a_one_up), per_micro(a_one_down), all_masks,
            *ins_mid.ins, anywhere(upstream),
        ],
        [
            out((3, micros, pixels, inner), BF16, (3, 1, pixels, inner), lambda m: (0, m, 0, 0)),
            out_micro(inner, F32), out_micro(inner, BF16), out_micro(inner, F32, 2),
        ],
        taps,
        flops=18 * small * inner, nbytes=20 * small + 18 * inner * inner, vmem=27,
    )
    w_out = call(
        functools.partial(assemble_kernel, ins_out), (1,), ins_out.ins, [whole_weight], nbytes=8 * chan * inner, vmem=9
    )
    stats_two = all_sum(part)
    h_two, a_three, part = call(
        third_kernel, (micros,),
        [
            smem(inverse), per_micro(stats_two), whole(params[1]), per_micro(a_two), own_mask,
            whole(w_out),
        ],
        [out_micro(inner, BF16), out_micro(chan, F32), out_micro(chan, F32, 2)],
        flops=2 * big * inner, nbytes=4 * big + 8 * small, vmem=13,
    )
    stats_three = all_sum(part)
    stats_three, a_two_low = in_order(stats_three, a_two_low)
    a_two_up, a_two_down = neighbours(a_two_low)
    tile = 512

    def tiled(array):
        return (array, block((1, array.shape[1], tile), lambda m, c: (m, 0, c)))

    def out_tiled(dtype, rows=pixels):
        return out((micros, rows, chan), dtype, (1, rows, tile), lambda m, c: (m, 0, c))

    block_out, d_resid, part = call(
        peak_kernel, (micros, chan // tile),
        [
            smem(inverse), tiled(stats_three), (params[2], block((2, tile), lambda m, c: (0, c))),
            tiled(a_three), tiled(x), tiled(upstream), own_mask,
        ],
        [out_tiled(BF16), out_tiled(BF16), out_tiled(F32, 2)],
        flops=40 * big, nbytes=16 * big, vmem=9,
    )
    part, a_two_up, a_two_down = in_order(part, a_two_up, a_two_down)
    grads_three = all_sum(part)
    d_three, dz_two, dz_two_low, part = call(
        back_third_kernel, (micros,),
        [
            smem(inverse), per_micro(stats_three), per_micro(grads_three), per_micro(stats_two),
            whole(params[2]), whole(params[1]), per_micro(a_three), per_micro(d_resid),
            per_micro(a_two), own_mask, whole(w_out),
        ],
        [out_micro(chan, BF16), out_micro(inner, F32), out_micro(inner, BF16), out_micro(inner, F32, 2)],
        flops=2 * big * inner, nbytes=10 * big, vmem=20,
    )
    dz_two_up, dz_two_down = neighbours(dz_two_low)
    grads_two = all_sum(part)
    d_two_cat, d_two = call(
        lower_second_kernel, (micros,),
        [
            smem(inverse), per_micro(stats_two), per_micro(grads_two), whole(params[1]),
            per_micro(a_two), per_micro(a_two_up), per_micro(a_two_down),
            per_micro(dz_two), per_micro(dz_two_up), per_micro(dz_two_down), all_masks,
        ],
        [out_micro(3 * inner, BF16), out_micro(3 * inner, BF16)],
        [pltpu.VMEM(padded[1:], F32)],
        flops=60 * small, nbytes=28 * small, vmem=16,
    )
    spread = Spread(inner, 9 * inner, chan)
    grads = call(
        functools.partial(grads_kernel, spread), (3 + chan // tile,),
        [
            (
                h_one.reshape(3, total_pixels, inner),
                block((1, total_pixels, inner), lambda t: (jnp.minimum(t, 2), 0, 0)),
            ),
            whole(d_two.reshape(total_pixels, 3 * inner)),
            (
                d_three.reshape(total_pixels, chan),
                block((total_pixels, tile), lambda t: (0, jnp.maximum(t - 3, 0))),
            ),
            whole(h_two.reshape(total_pixels, inner)), *spread.ins,
        ],
        spread.outs, [pltpu.VMEM((9 * inner, inner), BF16)],
        flops=18 * small * inner + 2 * big * inner, nbytes=12 * small + 18 * inner * inner, vmem=21,
    )
    sums = Sums(spread, grads)
    dz_one, part = call(
        functools.partial(back_second_kernel, ins_mid), (micros,),
        [
            smem(inverse), per_micro(stats_one), whole(params[0]), per_micro(d_two_cat),
            per_micro(a_one), own_mask, *ins_mid.ins, anywhere(grads[0]),
        ],
        [out_micro(inner, F32), out_micro(inner, F32, 2)],
        [pltpu.VMEM(padded, F32), held],
        flops=18 * small * inner, nbytes=30 * small + 18 * inner * inner, vmem=21,
    )
    chip_one = chip_sums(part)
    if sums.direct:
        chip_one, *sends = in_order(chip_one, *sums.send_far())
        sums.take_far(sends)
    grads_one = line_sums(chip_one)
    spread_in = Spread(inner, chan)
    d_one, *grad_in = call(
        functools.partial(first_back_kernel, spread_in), (chan // tile,),
        [
            smem(inverse), whole(stats_one), whole(grads_one), whole(params[0]), whole(dz_one), whole(a_one),
            (masks, block((1, micros, pixels, 128), lambda c: (1, 0, 0, 0))),
            (x.reshape(total_pixels, chan), block((total_pixels, tile), lambda c: (0, c))),
            *spread_in.ins,
        ],
        [out((micros, pixels, inner), BF16, (micros, pixels, inner), lambda c: (0, 0, 0)), *spread_in.outs],
        [pltpu.VMEM((tile, inner), F32)],
        flops=2 * big * inner, nbytes=4 * big, vmem=14,
    )
    if sums.direct:
        d_one, *rest = in_order(d_one, *grad_in, *sums.far)
        grad_in, sums.far = rest[:2], rest[2:]
    sums_in = Sums(spread_in, grad_in)
    if sums.direct:
        d_one, *sends = in_order(d_one, *sums.send_near())
        sums.take_near(sends)
    strip = total_pixels // 4
    input_grad = call(
        input_grad_kernel, (4,),
        [
            (d_one.reshape(total_pixels, inner), block((strip, inner), lambda s: (s, 0))),
            whole(w_in),
            (d_resid.reshape(total_pixels, chan), block((strip, chan), lambda s: (s, 0))),
        ],
        [out((total_pixels, chan), BF16, (strip, chan), lambda s: (s, 0))],
        flops=2 * big * inner, nbytes=8 * big, vmem=11,
    )
    if sums.direct:
        input_grad, *sums.near = in_order(input_grad, *sums.near)
        line, *sends = in_order(sums.send_line(), *sums_in.send_far())
        sums.take_line(line)
        sums_in.take_far(sends)
        sums.parts[1], sums.parts[2], *sums_in.far = in_order(*sums.parts[1:3], *sums_in.far)
        sums_in.take_near(sums_in.send_near())
        sums_in.take_line(sums_in.send_line())
    grad_in, grad_both = sums_in.finish(), sums.finish()
    grad_mid, grad_out = grad_both[: weight_mid.shape[0]], grad_both[weight_mid.shape[0] :]

    norm_total = jnp.concatenate([grads_one[:, :2], grads_two, grads_three], axis=2)
    norm_total = jnp.sum(norm_total, axis=0)[::-1]
    squares = jnp.sum(grad_in * grad_in, axis=0) + jnp.sum(grad_both * grad_both, axis=0)
    squares = all_sum(squares.reshape(-1, 128))
    total = jnp.sum(squares).reshape(1, 1) + jnp.sum(norm_total * norm_total)
    grad_norm = jnp.sqrt(total)
    scale = CLIP / jnp.maximum(grad_norm, CLIP)
    new_in = adamw(weight_in, first_in, second_in, grad_in * scale, RATE, DECAY)
    new_mid = adamw(weight_mid, first_mid, second_mid, grad_mid * scale, RATE, DECAY)
    new_out = adamw(weight_out, first_out, second_out, (grad_out * scale).T, RATE, DECAY)
    new_norm = adamw(norm_params, norm_first, norm_second, norm_total * scale, RATE_NORM, 0.0)
    shape = (micros, 1, row_span, columns, chan)
    return (
        block_out.reshape(shape),
        input_grad.reshape(shape),
        *[group[k] for k in range(3) for group in (new_in, new_mid, new_out)],
        *new_norm,
        grad_norm.reshape(1),
    )


def solution(mesh):
    acts = P(None, "batch", "rows", None, None)
    by_row, by_col = P(("batch", "rows"), None), P(None, ("batch", "rows"))
    weights = (by_row, by_row, by_col)
    return jax.shard_map(
        per_device,
        mesh=mesh,
        in_specs=(
            acts, P(None, None, "batch", "rows", None, None), P(), P(), *(weights * 3), P(), P(), P()
        ),
        out_specs=(acts, acts, *(weights * 3), P(), P(), P(), P()),
        check_vma=False,
    )
```
